32 devices in a mesh: prow: 8 (over z, x), pcol: 4 (over y, core).
Axes of the slice: x: 2, y: 2, z: 4, core: 2. Of those that a mesh axis runs over, the one named last changes fastest.
Arguments:
- kernel_tiles: float32 [4, 8, 256, 8, 4, 256], P(None, 'prow', None, None, 'pcol'), may hold values from 0 to 11, as said below
Outputs:
- factored: float32 [4, 8, 256, 8, 4, 256], P(None, 'prow', None, None, 'pcol')
The draws below stay inside these ranges and needn't reach their ends.
Inputs may be any that keep to these rules, and one draw needn't show every extreme that they name: kernel_tiles is a symmetric positive definite matrix in the stated layout: a product of two exponential covariances of locations and times, scaled per point, plus a diagonal term of at least 0.5.
All inputs are finite; a program needn't handle non-finite values.
Results may differ from the reference program's by a relative error of at most 0.000061.
Values sent between devices are 32-bit elements; how exact they have to be, the bound alone decides.
No kernel may reach another device: no remote copies, remote signals or barrier semaphores. Data moves between devices by JAX's collectives and lax.ppermute only.
A program may use at most 128 MiB of HBM per device.

```python
import math
import jax
import jax.numpy as jnp
from jax import lax

NB = 256
RT = 4
TILES = 32
CT = 8
ORDER = 8192


def draw_kernel_tiles(key, part):
    streams = jax.random.split(key, 4)
    total = TILES * NB
    place = jax.random.uniform(streams[0], (total,), jnp.float32, 0.0, 16.0)
    moment = jax.random.uniform(streams[1], (total,), jnp.float32, 0.0, 4.0)
    amplitude = jnp.exp(jax.random.uniform(streams[2], (total,), jnp.float32, math.log(0.5), math.log(2.0)))
    nugget = jax.random.uniform(streams[3], (total,), jnp.float32, 0.5, 1.5)
    distance = jnp.abs(place[:, None] - place[None, :]) + jnp.abs(moment[:, None] - moment[None, :])
    matrix = amplitude[:, None] * amplitude[None, :] * jnp.exp(-distance) + jnp.diag(nugget)
    return matrix.reshape(RT, TILES // RT, NB, CT, TILES // CT, NB)


def setup_inputs(seed: int = 0) -> dict:
    keys = jax.random.split(jax.random.key(seed), 2)
    kernel_tiles = draw_kernel_tiles(jax.random.fold_in(keys[1], 71), 0)
    return {"kernel_tiles": kernel_tiles}


def reference(kernel_tiles):
    matrix = kernel_tiles.reshape(ORDER, ORDER)
    first = jnp.linalg.cholesky(matrix[:NB, :NB])
    left = jax.scipy.linalg.solve_triangular(first, matrix[NB:, :NB].T, lower=True).T
    schur = matrix[NB:, NB:] - jnp.dot(left, left.T, precision=lax.Precision.HIGHEST)
    second = jnp.linalg.cholesky(schur[:NB, :NB])
    lower_part = jax.scipy.linalg.solve_triangular(second, schur[NB:, :NB].T, lower=True).T
    remainder = schur[NB:, NB:] - jnp.dot(lower_part, lower_part.T, precision=lax.Precision.HIGHEST)
    result = jnp.zeros((ORDER, ORDER), jnp.float32)
    result = result.at[:, :NB].set(jnp.concatenate([first, left], axis=0))
    result = result.at[NB:, NB:2 * NB].set(jnp.concatenate([second, lower_part], axis=0))
    result = result.at[2 * NB:, 2 * NB:].set(remainder)
    return result.reshape(kernel_tiles.shape)
```

```python
import functools

import jax
import jax.numpy as jnp
from jax import lax
from jax.experimental import pallas as pl
from jax.experimental.pallas import tpu as pltpu
from jax.sharding import PartitionSpec as P

HI = lax.Precision.HIGHEST
F32 = jnp.float32
BF16 = jnp.bfloat16
LANES = 128
VMEM_BYTES = 56 * 1024 * 1024


def splat(x, shape):
    return jnp.broadcast_to(x, shape)


def inverse_factor_128(block):
    size = 128
    step = 8
    count = size // step
    lane = lax.broadcasted_iota(jnp.int32, (step, size), 1)
    sub = lax.broadcasted_iota(jnp.int32, (step, size), 0)
    rows = [block[step * i : step * (i + 1), :] for i in range(count)]
    shape = (step, size)
    for j in range(count):
        base = step * j
        cols = [splat(rows[j][:, base + t : base + t + 1], shape) for t in range(step)]
        a = {}
        for t in range(step):
            for s in range(t, step):
                a[s, t] = splat(cols[t][s : s + 1, :], shape)
        m = {}
        inv = []
        for t in range(step):
            inv.append(1.0 / a[t, t])
            for s in range(t + 1, step):
                m[s, t] = a[s, t] * inv[t]
            for u in range(t + 1, step):
                for s in range(u, step):
                    a[s, u] = a[s, u] - m[s, t] * a[u, t]
        in_block = (lane >= base) & (lane < base + step)
        unit = jnp.where(lane - base == sub, F32(1.0), F32(0.0))
        own = jnp.where(in_block, unit, rows[j])
        u = []
        for t in range(step):
            row = splat(own[t : t + 1, :], shape)
            for s in range(t):
                row = row - m[t, s] * u[s]
            u.append(row)
        done = u[step - 1] * lax.rsqrt(a[step - 1, step - 1])
        for t in range(step - 1):
            done = jnp.where(sub == t, u[t] * lax.rsqrt(a[t, t]), done)
        g = [None] * step
        for t in reversed(range(step)):
            row = u[t] * inv[t]
            for s in range(t + 1, step):
                row = row - m[s, t] * g[s]
            g[t] = row
        for i in range(j + 1, count):
            acc = jnp.where(in_block, F32(0.0), rows[i])
            for t in range(step):
                acc = acc - splat(rows[i][:, base + t : base + t + 1], shape) * g[t]
            rows[i] = acc
        rows[j] = jnp.where(lane < base + step, done, F32(0.0))
    return jnp.concatenate(rows, axis=0)


def corner_kernel(place_ref, mine_ref, other_ref, inverse_ref, gram_ref, state):
    core, side, across = place_ref[0], place_ref[1], place_ref[2]
    rows = state.shape[0]
    tile = rows // 2
    half = tile // 2
    per = tile // LANES
    for which, ref in ((core, mine_ref), (1 - core, other_ref)):
        for target in range(2):

            @pl.when(which == target)
            def _(ref=ref, target=target):
                for part in range(4):
                    at_side = side if part % 2 == 0 else 1 - side
                    at_half = across if part < 2 else 1 - across
                    at = pl.multiple_of(at_side * tile + at_half * half, half)
                    for h in range(per):
                        start = target * tile + h * LANES
                        state[pl.ds(at, half), start : start + LANES] = ref[
                            pl.ds(part * half * per + h, half, stride=per), :
                        ]

    for o in range(rows // LANES):
        lo, hi = o * LANES, (o + 1) * LANES
        diag = inverse_factor_128(state[lo:hi, lo:hi])
        upper = jnp.dot(diag, state[lo:hi, :], precision=HI, preferred_element_type=F32)
        parts = ([upper[:, :lo]] if lo else []) + [diag] + ([upper[:, hi:]] if hi < rows else [])
        wide = jnp.concatenate(parts, axis=1)
        if hi < rows:
            state[hi:, lo:hi] = jnp.zeros((rows - hi, LANES), F32)
            state[hi:, :] -= lax.dot_general(
                upper[:, hi:], wide, (((0,), (0,)), ((), ())), precision=HI, preferred_element_type=F32
            )
            inverse_ref[lo:hi, hi:] = jnp.zeros((LANES, rows - hi), F32)
        inverse_ref[lo:hi, :hi] = wide[:, :hi]
    whole = inverse_ref[...]
    gram_ref[...] = lax.dot_general(
        whole, whole, (((0,), (0,)), ((), ())), precision=HI, preferred_element_type=F32
    )


def corner_inverse(place, mine, other):
    width = mine.shape[0] // 2
    vmem = pl.BlockSpec(memory_space=pltpu.VMEM)
    return pl.pallas_call(
        corner_kernel,
        out_shape=(jax.ShapeDtypeStruct((width, width), F32),) * 2,
        in_specs=[pl.BlockSpec(memory_space=pltpu.SMEM), vmem, vmem],
        out_specs=(vmem, vmem),
        scratch_shapes=[pltpu.VMEM((width, width), F32)],
        compiler_params=pltpu.CompilerParams(vmem_limit_bytes=16 * 1024 * 1024),
        cost_estimate=pl.CostEstimate(flops=30_000_000_000, bytes_accessed=4 * 1024 * 1024, transcendentals=0),
        name="corner_inverse",
    )(place, mine, other)


def gather_kernel(row_tiles, col_tiles, tile, block_ref, across_ref, even_ref, odd_ref):
    step = pl.program_id(0)
    per = tile // LANES
    stride = col_tiles * per
    keep = row_tiles * per
    first = jnp.concatenate([block_ref[pl.ds(h, tile, stride=stride), :] for h in range(per)], axis=1).T
    for h in range(per):
        across_ref[pl.ds(step * per + h, tile, stride=keep), :] = first[:, h * LANES : (h + 1) * LANES]

    @pl.when(step == 0)
    def _():
        keep = col_tiles // 2 * per
        for parity, ref in enumerate((even_ref, odd_ref)):
            for i in range(col_tiles // 2):
                for h in range(per):
                    ref[pl.ds(i * per + h, tile, stride=keep), :] = block_ref[
                        pl.ds((2 * i + parity) * per + h, tile, stride=stride), :
                    ]


def gather_pieces(block, row_tiles, col_tiles, tile):
    per = tile // LANES
    shapes = [tile * row_tiles * per] + [tile * (col_tiles // 2) * per] * 2
    return pl.pallas_call(
        functools.partial(gather_kernel, row_tiles, col_tiles, tile),
        grid=(row_tiles,),
        out_shape=[jax.ShapeDtypeStruct((s, LANES), F32) for s in shapes],
        in_specs=[pl.BlockSpec((tile * col_tiles * per, LANES), lambda a: (a, 0))],
        out_specs=[pl.BlockSpec((s, LANES), lambda a: (0, 0)) for s in shapes],
        compiler_params=pltpu.CompilerParams(vmem_limit_bytes=24 * 1024 * 1024),
        cost_estimate=pl.CostEstimate(flops=0, bytes_accessed=12 * 1024 * 1024, transcendentals=0),
        name="gather_pieces",
    )(block)


def halves(x):
    high = x.astype(BF16)
    return high, (x - high.astype(F32)).astype(BF16)


def product(a, b, dims):
    (a_high, a_low), (b_high, b_low) = a, b
    dot = functools.partial(lax.dot_general, dimension_numbers=(dims, ((), ())), preferred_element_type=F32)
    return dot(a_high, b_high) + (dot(a_low, b_high) + dot(a_high, b_low))


def load_columns(place_ref, pieces, raw, col_high, col_low, sems, tile, count):
    per = tile // LANES
    for panel in range(2):
        for which, ref in enumerate(pieces):

            @pl.when(place_ref[3 + panel] == which)
            def _(panel=panel, ref=ref):
                pltpu.make_async_copy(ref, raw.at[panel], sems.at[panel]).start()

    for panel in range(2):
        pltpu.make_async_copy(pieces[0], raw.at[panel], sems.at[panel]).wait()
        for i in range(count):
            for h in range(per):
                high, low = halves(raw[panel, pl.ds(i * per + h, tile, stride=count * per), :])
                at = (i * per + h) * LANES
                col_high[panel * tile : (panel + 1) * tile, at : at + LANES] = high
                col_low[panel * tile : (panel + 1) * tile, at : at + LANES] = low


def subtract(place_ref, block_ref, out_ref, weights, col_high, col_low, tile, count):
    per = tile // LANES
    parity = place_ref[2]
    for i in range(count):
        at = i * tile
        update = product(weights, (col_high[:, at : at + tile], col_low[:, at : at + tile]), ((1,), (0,)))
        for h in range(per):
            where = pl.ds((2 * i + parity) * per + h, tile, stride=2 * count * per)
            out_ref[where, :] = block_ref[where, :] - update[:, h * LANES : (h + 1) * LANES]


def first_kernel(tile, row_tiles, count, place_ref, block_ref, rows_mine, rows_other, inverse_ref, gram_ref,
                 piece_a, piece_b, piece_c, out_ref, high_ref, low_ref, solved_ref, raw, col_high, col_low, sems):
    step = pl.program_id(0)
    row, col, core = place_ref[0], place_ref[1], place_ref[5]
    per = tile // LANES

    @pl.when(step == 0)
    def _():
        load_columns(place_ref, (piece_a, piece_b, piece_c), raw, col_high, col_low, sems, tile, count)

    out_ref[...] = block_ref[...]
    mine, other = [
        jnp.concatenate([r[pl.ds(step * per + h, tile, stride=row_tiles * per), :] for h in range(per)], axis=1)
        for r in (rows_mine, rows_other)
    ]
    lead = jnp.concatenate([jnp.where(core == 0, mine, other), jnp.where(core == 0, other, mine)], axis=0)
    weights = halves(
        lax.dot_general(lead, gram_ref[...], (((0,), (0,)), ((), ())), precision=HI, preferred_element_type=F32)
    )
    high_ref[...], low_ref[...] = weights
    subtract(place_ref, block_ref, out_ref, weights, col_high, col_low, tile, count)

    @pl.when(col < 2)
    def _():
        where = pl.ds(pl.multiple_of(jnp.minimum(col, 1) * tile, tile), tile)
        solved = product(halves(lead.T), halves(inverse_ref[where, :]), ((1,), (1,)))
        r = lax.broadcasted_iota(jnp.int32, (tile, tile), 0)
        s = lax.broadcasted_iota(jnp.int32, (tile, tile), 1)
        top = (step == 0) & (row < 2)
        on_diag = top & (row == col)
        above = top & (row < col)
        keep = jnp.where(on_diag, s - r, jnp.where(above, 1, 0)) <= 0
        solved_ref[...] = jnp.where(keep, solved, F32(0.0))


def second_kernel(tile, row_tiles, count, place_ref, block_ref, high_ref, low_ref, solved_ref, piece_a, piece_b,
                  piece_c, out_ref, raw, col_high, col_low, sems):
    step = pl.program_id(0)
    row, col = place_ref[0], place_ref[1]
    per = tile // LANES
    top = (step == 0) & (row < 2)

    @pl.when(step == 0)
    def _():
        load_columns(place_ref, (piece_a, piece_b, piece_c), raw, col_high, col_low, sems, tile, count)

    @pl.when(top)
    def _():
        out_ref[...] = jnp.zeros_like(out_ref)

    @pl.when(jnp.logical_not(top))
    def _():
        out_ref[...] = block_ref[...]
        subtract(place_ref, block_ref, out_ref, (high_ref[...], low_ref[...]), col_high, col_low, tile, count)

    @pl.when(col < 2)
    def _():
        for h in range(per):
            out_ref[pl.ds(h, tile, stride=2 * count * per), :] = solved_ref[:, h * LANES : (h + 1) * LANES]


def trailing(places, block, rows_mine, rows_other, inverse, gram, pieces, row_tiles, col_tiles, tile):
    per = tile // LANES
    depth = inverse.shape[0]
    count = col_tiles // 2
    smem = pl.BlockSpec(memory_space=pltpu.SMEM)
    whole = pl.BlockSpec((depth, depth), lambda a: (0, 0))
    rows_spec = pl.BlockSpec(rows_mine.shape, lambda a: (0, 0))
    block_spec = pl.BlockSpec((tile * col_tiles * per, LANES), lambda a: (a, 0))
    weight_spec = pl.BlockSpec((tile, depth), lambda a: (a, 0))
    solved_spec = pl.BlockSpec((tile, tile), lambda a: (a, 0))
    anywhere = [pl.BlockSpec(memory_space=pl.ANY)] * 3
    scratch = [
        pltpu.VMEM((2, tile * count * per, LANES), F32),
        pltpu.VMEM((depth, count * tile), BF16),
        pltpu.VMEM((depth, count * tile), BF16),
        pltpu.SemaphoreType.DMA((2,)),
    ]
    total = row_tiles * tile
    params = pltpu.CompilerParams(vmem_limit_bytes=40 * 1024 * 1024)
    cost = pl.CostEstimate(flops=9_000_000_000, bytes_accessed=20 * 1024 * 1024, transcendentals=0)
    block, high, low, solved = pl.pallas_call(
        functools.partial(first_kernel, tile, row_tiles, count),
        grid=(row_tiles,),
        out_shape=[
            jax.ShapeDtypeStruct(block.shape, F32),
            jax.ShapeDtypeStruct((total, depth), BF16),
            jax.ShapeDtypeStruct((total, depth), BF16),
            jax.ShapeDtypeStruct((total, tile), F32),
        ],
        in_specs=[smem, block_spec, rows_spec, rows_spec, whole, whole] + anywhere,
        out_specs=[block_spec, weight_spec, weight_spec, solved_spec],
        scratch_shapes=scratch,
        compiler_params=params,
        cost_estimate=cost,
        name="trailing_first",
    )(places[0], block, rows_mine, rows_other, inverse, gram, *pieces[0])
    return pl.pallas_call(
        functools.partial(second_kernel, tile, row_tiles, count),
        grid=(row_tiles,),
        out_shape=jax.ShapeDtypeStruct(block.shape, F32),
        in_specs=[smem, block_spec, weight_spec, weight_spec, solved_spec] + anywhere,
        out_specs=block_spec,
        scratch_shapes=scratch,
        compiler_params=params,
        cost_estimate=cost,
        input_output_aliases={1: 0},
        name="trailing_second",
    )(places[1], block, high, low, solved, *pieces[1])


AXES = ("prow", "pcol")


def send(value, route):
    pairs = []
    for device in range(32):
        to = route(device // 8, device // 4 % 2, device // 2 % 2, device % 2)
        if to is not None:
            pairs.append((device, ((to[0] * 2 + to[1]) * 2 + to[2]) * 2 + to[3]))
    return lax.ppermute(value, AXES, pairs)


def far_stage(z, x, y, k):
    to = {(0, 0): 3, (2, 0): 1, (0, 1): 2}.get((z, y))
    return None if to is None else (to, x, y, k)


def near_stage(z, x, y, k):
    to = {(0, 0): 1, (2, 0): 3, (3, 0): 2, (0, 1): 1, (1, 1): 3, (3, 1): 2}.get((z, y))
    return None if to is None else (to, x, y, k)


def by_rows(stage, z, y):
    return z == 0 or (y == 1 and z == (2 if stage == 0 else 1))


def same_core(stage):
    def route(z, x, y, k):
        if by_rows(stage, z, y) or k == x:
            return (z, 1 - x, y, k)
        return (z, x, y, x)

    return route


def cross_core(stage):
    def route(z, x, y, k):
        if by_rows(stage, z, y) or k == x:
            return None
        return (z, 1 - x, y, x)

    return route


def shards(kernel_tiles):
    row_tiles, _, tile, col_tiles, _, _ = kernel_tiles.shape
    row = lax.axis_index("prow")
    col = lax.axis_index("pcol")
    z, x, y, core = row // 2, row % 2, col // 2, col % 2
    per = tile // LANES
    block = kernel_tiles.reshape(row_tiles * tile * col_tiles * per, LANES)

    lead = kernel_tiles[0, 0, :, 0, 0, :].reshape(tile * per, LANES)
    middle = tile * per // 2
    half = send(lead[middle:], lambda z, x, y, k: (z, x, 1, k) if z == 0 and y == 0 else None)
    half = jnp.where(y == 0, lead[:middle], half)
    half = jnp.where(z == 2, send(half, lambda z, x, y, k: (2, x, y, k) if z == 0 else None), half)
    half = jnp.where(z % 2 == 1, send(half, lambda z, x, y, k: (z + 1, x, y, k) if z % 2 == 0 else None), half)
    beside = send(half, lambda z, x, y, k: (z, 1 - x, y, k))
    above = send(half, lambda z, x, y, k: (z, x, 1 - y, k))
    corner = send(half, lambda z, x, y, k: (z, 1 - x, 1 - y, k))
    mine = jnp.concatenate([half, beside, above, corner], axis=0)
    other = send(mine, lambda z, x, y, k: (z, x, y, 1 - k))
    inverse, gram = corner_inverse(jnp.stack([core, x, y]).astype(jnp.int32), mine, other)

    across, even, odd = gather_pieces(block, row_tiles, col_tiles, tile)
    over = send(across, lambda z, x, y, k: (z, x, 1, k) if y == 0 else None)
    far = send(jnp.where(y == 0, across, even), far_stage)
    rows_mine = jnp.where(y == 0, across, over)
    rows_other = send(rows_mine, lambda z, x, y, k: (z, x, y, 1 - k))
    near = send(
        jnp.where(y == 0, jnp.where(z == 3, far, across), jnp.where(z == 0, odd, over)), near_stage
    )
    held = [
        jnp.where(z == 0, even, jnp.where(y == 0, jnp.where(z == 2, across, far), jnp.where(z == 2, far, over))),
        jnp.where(z == 0, odd, near),
    ]
    pieces = [[held[s], send(held[s], same_core(s)), send(held[s], cross_core(s))] for s in range(2)]

    places = []
    for stage in range(2):
        first_odd = jnp.where(y == 0, (z == 1) | (z == 2), z == 3).astype(jnp.int32)
        parity = jnp.where(z == 0, stage, first_odd if stage == 0 else 1 - first_odd)
        rowwise = (z == 0) | ((y == 1) & (z == 2 - stage))
        own = core == x
        zero = jnp.where(rowwise, jnp.where(x == 0, 0, 1), jnp.where(own, jnp.where(core == 0, 0, 1), jnp.where(core == 0, 1, 2)))
        one = jnp.where(rowwise, jnp.where(x == 0, 1, 0), jnp.where(own, jnp.where(core == 0, 1, 0), jnp.where(core == 0, 2, 1)))
        places.append(jnp.stack([row, col, parity, zero, one, core]).astype(jnp.int32))
    result = trailing(places, block, rows_mine, rows_other, inverse, gram, pieces, row_tiles, col_tiles, tile)
    return result.reshape(kernel_tiles.shape)


def from_root(value, axis, root):
    mine = lax.axis_index(axis) == root
    return lax.psum(jnp.where(mine, value, jnp.zeros_like(value)), axis)


def shards_any(kernel_tiles):
    row_tiles, _, tile, col_tiles, _, _ = kernel_tiles.shape
    row = lax.axis_index("prow")
    col = lax.axis_index("pcol")
    per = tile // LANES
    block = kernel_tiles.reshape(row_tiles * tile * col_tiles * per, LANES)
    across, even, odd = gather_pieces(block, row_tiles, col_tiles, tile)
    rows = [from_root(across, "pcol", panel) for panel in range(2)]
    lead = kernel_tiles[0, 0, :, 0, 0, :].reshape(tile * per, LANES)
    middle = tile * per // 2
    columns = []
    for panel in range(2):
        tops = [from_root(from_root(lead, "pcol", panel), "prow", p) for p in range(2)]
        columns.append(jnp.concatenate([t[s : s + middle] for s in (0, middle) for t in tops], axis=0))
    inverse, gram = corner_inverse(jnp.zeros((3,), jnp.int32), columns[0], columns[1])
    pieces = []
    places = []
    zero = jnp.zeros((), jnp.int32)
    for stage, part in enumerate((even, odd)):
        panels = [from_root(part, "prow", p) for p in range(2)]
        pieces.append(panels + [panels[0]])
        places.append(jnp.stack([row, col, zero + stage, zero, zero + 1, zero]).astype(jnp.int32))
    result = trailing(places, block, rows[0], rows[1], inverse, gram, pieces, row_tiles, col_tiles, tile)
    return result.reshape(kernel_tiles.shape)


def solution(mesh):
    in_specs = (P(None, "prow", None, None, "pcol", None),)
    out_specs = P(None, "prow", None, None, "pcol", None)
    body = shards if (mesh.shape["prow"], mesh.shape["pcol"]) == (8, 4) else shards_any
    return jax.shard_map(body, mesh=mesh, in_specs=in_specs, out_specs=out_specs, check_vma=False)
```

```python
import functools

import jax
import jax.numpy as jnp
from jax import lax
from jax.experimental import pallas as pl
from jax.experimental.pallas import tpu as pltpu
from jax.sharding import PartitionSpec as P

HI = lax.Precision.HIGHEST
F32 = jnp.float32
BF16 = jnp.bfloat16
LANES = 128
VMEM_BYTES = 56 * 1024 * 1024


def splat(x, shape):
    return jnp.broadcast_to(x, shape)


def inverse_factor_128(block):
    size = 128
    step = 8
    count = size // step
    lane = lax.broadcasted_iota(jnp.int32, (step, size), 1)
    sub = lax.broadcasted_iota(jnp.int32, (step, size), 0)
    rows = [block[step * i : step * (i + 1), :] for i in range(count)]
    shape = (step, size)
    for j in range(count):
        base = step * j
        cols = [splat(rows[j][:, base + t : base + t + 1], shape) for t in range(step)]
        a = {}
        for t in range(step):
            for s in range(t, step):
                a[s, t] = splat(cols[t][s : s + 1, :], shape)
        m = {}
        inv = []
        for t in range(step):
            inv.append(1.0 / a[t, t])
            for s in range(t + 1, step):
                m[s, t] = a[s, t] * inv[t]
            for u in range(t + 1, step):
                for s in range(u, step):
                    a[s, u] = a[s, u] - m[s, t] * a[u, t]
        in_block = (lane >= base) & (lane < base + step)
        unit = jnp.where(lane - base == sub, F32(1.0), F32(0.0))
        own = jnp.where(in_block, unit, rows[j])
        u = []
        for t in range(step):
            row = splat(own[t : t + 1, :], shape)
            for s in range(t):
                row = row - m[t, s] * u[s]
            u.append(row)
        done = u[step - 1] * lax.rsqrt(a[step - 1, step - 1])
        for t in range(step - 1):
            done = jnp.where(sub == t, u[t] * lax.rsqrt(a[t, t]), done)
        g = [None] * step
        for t in reversed(range(step)):
            row = u[t] * inv[t]
            for s in range(t + 1, step):
                row = row - m[s, t] * g[s]
            g[t] = row
        for i in range(j + 1, count):
            acc = jnp.where(in_block, F32(0.0), rows[i])
            for t in range(step):
                acc = acc - splat(rows[i][:, base + t : base + t + 1], shape) * g[t]
            rows[i] = acc
        rows[j] = jnp.where(lane < base + step, done, F32(0.0))
    return jnp.concatenate(rows, axis=0)


def eliminate(state, first, last):
    rows = state.shape[0]
    for o in range(first, last):
        lo, hi = o * LANES, (o + 1) * LANES
        diag = inverse_factor_128(state[lo:hi, lo:hi])
        upper = jnp.dot(diag, state[lo:hi, :], precision=HI, preferred_element_type=F32)
        parts = ([upper[:, :lo]] if lo else []) + [diag] + ([upper[:, hi:]] if hi < rows else [])
        wide = jnp.concatenate(parts, axis=1)
        if hi < rows:
            state[hi:, lo:hi] = jnp.zeros((rows - hi, LANES), F32)
            state[hi:, :] -= lax.dot_general(
                upper[:, hi:], wide, (((0,), (0,)), ((), ())), precision=HI, preferred_element_type=F32
            )
            state[lo:hi, hi:] = jnp.zeros((LANES, rows - hi), F32)
        state[lo:hi, :hi] = wide[:, :hi]


def corner_start_kernel(place_ref, mine_ref, other_ref, state):
    core, side, across = place_ref[0], place_ref[1], place_ref[2]
    rows = state.shape[0]
    tile = rows // 2
    half = tile // 2
    per = tile // LANES
    for which, ref in ((core, mine_ref), (1 - core, other_ref)):
        for target in range(2):

            @pl.when(which == target)
            def _(ref=ref, target=target):
                for part in range(4):
                    at_side = side if part % 2 == 0 else 1 - side
                    at_half = across if part < 2 else 1 - across
                    at = pl.multiple_of(at_side * tile + at_half * half, half)
                    for h in range(per):
                        start = target * tile + h * LANES
                        state[pl.ds(at, half), start : start + LANES] = ref[
                            pl.ds(part * half * per + h, half, stride=per), :
                        ]

    eliminate(state, 0, tile // LANES)


def corner_end_kernel(state_ref, inverse_ref, gram_ref):
    rows = state_ref.shape[0]
    inverse_ref[...] = state_ref[...]
    eliminate(inverse_ref, rows // 2 // LANES, rows // LANES)
    whole = inverse_ref[...]
    gram_ref[...] = lax.dot_general(
        whole, whole, (((0,), (0,)), ((), ())), precision=HI, preferred_element_type=F32
    )


CORNER_COST = pl.CostEstimate(flops=15_000_000_000, bytes_accessed=2 * 1024 * 1024, transcendentals=0)


def corner_start(place, mine, other):
    width = mine.shape[0] // 2
    vmem = pl.BlockSpec(memory_space=pltpu.VMEM)
    return pl.pallas_call(
        corner_start_kernel,
        out_shape=jax.ShapeDtypeStruct((width, width), F32),
        in_specs=[pl.BlockSpec(memory_space=pltpu.SMEM), vmem, vmem],
        out_specs=vmem,
        compiler_params=pltpu.CompilerParams(vmem_limit_bytes=16 * 1024 * 1024),
        cost_estimate=CORNER_COST,
        name="corner_start",
    )(place, mine, other)


def corner_end(state):
    vmem = pl.BlockSpec(memory_space=pltpu.VMEM)
    return pl.pallas_call(
        corner_end_kernel,
        out_shape=(jax.ShapeDtypeStruct(state.shape, F32),) * 2,
        in_specs=[vmem],
        out_specs=(vmem, vmem),
        compiler_params=pltpu.CompilerParams(vmem_limit_bytes=16 * 1024 * 1024),
        cost_estimate=CORNER_COST,
        name="corner_end",
    )(state)


def gather_kernel(row_tiles, col_tiles, tile, block_ref, across_ref, even_ref, odd_ref):
    step = pl.program_id(0)
    per = tile // LANES
    stride = col_tiles * per
    keep = row_tiles * per
    first = jnp.concatenate([block_ref[pl.ds(h, tile, stride=stride), :] for h in range(per)], axis=1).T
    for h in range(per):
        across_ref[pl.ds(step * per + h, tile, stride=keep), :] = first[:, h * LANES : (h + 1) * LANES]

    @pl.when(step == 0)
    def _():
        keep = col_tiles // 2 * per
        for parity, ref in enumerate((even_ref, odd_ref)):
            for i in range(col_tiles // 2):
                for h in range(per):
                    ref[pl.ds(i * per + h, tile, stride=keep), :] = block_ref[
                        pl.ds((2 * i + parity) * per + h, tile, stride=stride), :
                    ]


def gather_pieces(block, row_tiles, col_tiles, tile):
    per = tile // LANES
    shapes = [tile * row_tiles * per] + [tile * (col_tiles // 2) * per] * 2
    return pl.pallas_call(
        functools.partial(gather_kernel, row_tiles, col_tiles, tile),
        grid=(row_tiles,),
        out_shape=[jax.ShapeDtypeStruct((s, LANES), F32) for s in shapes],
        in_specs=[pl.BlockSpec((tile * col_tiles * per, LANES), lambda a: (a, 0))],
        out_specs=[pl.BlockSpec((s, LANES), lambda a: (0, 0)) for s in shapes],
        compiler_params=pltpu.CompilerParams(vmem_limit_bytes=VMEM_BYTES),
        cost_estimate=pl.CostEstimate(flops=0, bytes_accessed=12 * 1024 * 1024, transcendentals=0),
        name="gather_pieces",
    )(block)


def halves(x):
    high = x.astype(BF16)
    return high, (x - high.astype(F32)).astype(BF16)


def product(a, b, dims):
    (a_high, a_low), (b_high, b_low) = a, b
    dot = functools.partial(lax.dot_general, dimension_numbers=(dims, ((), ())), preferred_element_type=F32)
    return dot(a_high, b_high) + (dot(a_low, b_high) + dot(a_high, b_low))


def load_columns(place_ref, pieces, raw, col_high, col_low, sems, tile, count):
    per = tile // LANES
    for panel in range(2):
        for which, ref in enumerate(pieces):

            @pl.when(place_ref[3 + panel] == which)
            def _(panel=panel, ref=ref):
                pltpu.make_async_copy(ref, raw.at[panel], sems.at[panel]).start()

    for panel in range(2):
        pltpu.make_async_copy(pieces[0], raw.at[panel], sems.at[panel]).wait()
        for i in range(count):
            for h in range(per):
                high, low = halves(raw[panel, pl.ds(i * per + h, tile, stride=count * per), :])
                at = (i * per + h) * LANES
                col_high[panel * tile : (panel + 1) * tile, at : at + LANES] = high
                col_low[panel * tile : (panel + 1) * tile, at : at + LANES] = low


def subtract(place_ref, block_ref, out_ref, weights, col_high, col_low, tile, count):
    per = tile // LANES
    parity = place_ref[2]
    for i in range(count):
        at = i * tile
        update = product(weights, (col_high[:, at : at + tile], col_low[:, at : at + tile]), ((1,), (0,)))
        for h in range(per):
            where = pl.ds((2 * i + parity) * per + h, tile, stride=2 * count * per)
            out_ref[where, :] = block_ref[where, :] - update[:, h * LANES : (h + 1) * LANES]


def first_kernel(tile, row_tiles, count, place_ref, block_ref, rows_mine, rows_other, inverse_ref, gram_ref,
                 piece_a, piece_b, piece_c, out_ref, high_ref, low_ref, solved_ref, raw, col_high, col_low, sems):
    step = pl.program_id(0)
    row, col, core = place_ref[0], place_ref[1], place_ref[5]
    per = tile // LANES

    @pl.when(step == 0)
    def _():
        load_columns(place_ref, (piece_a, piece_b, piece_c), raw, col_high, col_low, sems, tile, count)

    out_ref[...] = block_ref[...]
    mine, other = [
        jnp.concatenate([r[pl.ds(step * per + h, tile, stride=row_tiles * per), :] for h in range(per)], axis=1)
        for r in (rows_mine, rows_other)
    ]
    lead = jnp.concatenate([jnp.where(core == 0, mine, other), jnp.where(core == 0, other, mine)], axis=0)
    weights = halves(
        lax.dot_general(lead, gram_ref[...], (((0,), (0,)), ((), ())), precision=HI, preferred_element_type=F32)
    )
    high_ref[...], low_ref[...] = weights
    subtract(place_ref, block_ref, out_ref, weights, col_high, col_low, tile, count)

    @pl.when(col < 2)
    def _():
        where = pl.ds(pl.multiple_of(jnp.minimum(col, 1) * tile, tile), tile)
        solved = product(halves(lead.T), halves(inverse_ref[where, :]), ((1,), (1,)))
        r = lax.broadcasted_iota(jnp.int32, (tile, tile), 0)
        s = lax.broadcasted_iota(jnp.int32, (tile, tile), 1)
        top = (step == 0) & (row < 2)
        on_diag = top & (row == col)
        above = top & (row < col)
        keep = jnp.where(on_diag, s - r, jnp.where(above, 1, 0)) <= 0
        solved_ref[...] = jnp.where(keep, solved, F32(0.0))


def second_kernel(tile, row_tiles, count, place_ref, block_ref, high_ref, low_ref, solved_ref, piece_a, piece_b,
                  piece_c, out_ref, raw, col_high, col_low, sems):
    step = pl.program_id(0)
    row, col = place_ref[0], place_ref[1]
    per = tile // LANES
    top = (step == 0) & (row < 2)

    @pl.when(step == 0)
    def _():
        load_columns(place_ref, (piece_a, piece_b, piece_c), raw, col_high, col_low, sems, tile, count)

    @pl.when(top)
    def _():
        out_ref[...] = jnp.zeros_like(out_ref)

    @pl.when(jnp.logical_not(top))
    def _():
        out_ref[...] = block_ref[...]
        subtract(place_ref, block_ref, out_ref, (high_ref[...], low_ref[...]), col_high, col_low, tile, count)

    @pl.when(col < 2)
    def _():
        for h in range(per):
            out_ref[pl.ds(h, tile, stride=2 * count * per), :] = solved_ref[:, h * LANES : (h + 1) * LANES]


def trailing(places, block, rows_mine, rows_other, inverse, gram, pieces, row_tiles, col_tiles, tile):
    per = tile // LANES
    depth = inverse.shape[0]
    count = col_tiles // 2
    smem = pl.BlockSpec(memory_space=pltpu.SMEM)
    whole = pl.BlockSpec((depth, depth), lambda a: (0, 0))
    rows_spec = pl.BlockSpec(rows_mine.shape, lambda a: (0, 0))
    block_spec = pl.BlockSpec((tile * col_tiles * per, LANES), lambda a: (a, 0))
    weight_spec = pl.BlockSpec((tile, depth), lambda a: (a, 0))
    solved_spec = pl.BlockSpec((tile, tile), lambda a: (a, 0))
    anywhere = [pl.BlockSpec(memory_space=pl.ANY)] * 3
    scratch = [
        pltpu.VMEM((2, tile * count * per, LANES), F32),
        pltpu.VMEM((depth, count * tile), BF16),
        pltpu.VMEM((depth, count * tile), BF16),
        pltpu.SemaphoreType.DMA((2,)),
    ]
    total = row_tiles * tile
    params = pltpu.CompilerParams(vmem_limit_bytes=40 * 1024 * 1024)
    cost = pl.CostEstimate(flops=9_000_000_000, bytes_accessed=20 * 1024 * 1024, transcendentals=0)
    block, high, low, solved = pl.pallas_call(
        functools.partial(first_kernel, tile, row_tiles, count),
        grid=(row_tiles,),
        out_shape=[
            jax.ShapeDtypeStruct(block.shape, F32),
            jax.ShapeDtypeStruct((total, depth), BF16),
            jax.ShapeDtypeStruct((total, depth), BF16),
            jax.ShapeDtypeStruct((total, tile), F32),
        ],
        in_specs=[smem, block_spec, rows_spec, rows_spec, whole, whole] + anywhere,
        out_specs=[block_spec, weight_spec, weight_spec, solved_spec],
        scratch_shapes=scratch,
        compiler_params=params,
        cost_estimate=cost,
        name="trailing_first",
    )(places[0], block, rows_mine, rows_other, inverse, gram, *pieces[0])
    return pl.pallas_call(
        functools.partial(second_kernel, tile, row_tiles, count),
        grid=(row_tiles,),
        out_shape=jax.ShapeDtypeStruct(block.shape, F32),
        in_specs=[smem, block_spec, weight_spec, weight_spec, solved_spec] + anywhere,
        out_specs=block_spec,
        scratch_shapes=scratch,
        compiler_params=params,
        cost_estimate=cost,
        input_output_aliases={1: 0},
        name="trailing_second",
    )(places[1], block, high, low, solved, *pieces[1])


AXES = ("prow", "pcol")


def send(value, route):
    pairs = []
    for device in range(32):
        to = route(device // 8, device // 4 % 2, device // 2 % 2, device % 2)
        if to is not None:
            pairs.append((device, ((to[0] * 2 + to[1]) * 2 + to[2]) * 2 + to[3]))
    return lax.ppermute(value, AXES, pairs)


def far_stage(z, x, y, k):
    to = {(0, 0): 3, (2, 0): 1, (0, 1): 2}.get((z, y))
    return None if to is None else (to, x, y, k)


def near_stage(z, x, y, k):
    to = {(0, 0): 1, (2, 0): 3, (3, 0): 2, (0, 1): 1, (1, 1): 3, (3, 1): 2}.get((z, y))
    return None if to is None else (to, x, y, k)


def by_rows(stage, z, y):
    return z == 0 or (y == 1 and z == (2 if stage == 0 else 1))


def same_core(stage):
    def route(z, x, y, k):
        if by_rows(stage, z, y) or k == x:
            return (z, 1 - x, y, k)
        return (z, x, y, x)

    return route


def cross_core(stage):
    def route(z, x, y, k):
        if by_rows(stage, z, y) or k == x:
            return None
        return (z, 1 - x, y, x)

    return route


def shards(kernel_tiles):
    row_tiles, _, tile, col_tiles, _, _ = kernel_tiles.shape
    row = lax.axis_index("prow")
    col = lax.axis_index("pcol")
    z, x, y, core = row // 2, row % 2, col // 2, col % 2
    per = tile // LANES
    block = kernel_tiles.reshape(row_tiles * tile * col_tiles * per, LANES)

    lead = kernel_tiles[0, 0, :, 0, 0, :].reshape(tile * per, LANES)
    middle = tile * per // 2
    half = send(lead[middle:], lambda z, x, y, k: (z, x, 1, k) if z == 0 and y == 0 else None)
    half = jnp.where(y == 0, lead[:middle], half)
    half = jnp.where(z == 2, send(half, lambda z, x, y, k: (2, x, y, k) if z == 0 else None), half)
    half = jnp.where(z % 2 == 1, send(half, lambda z, x, y, k: (z + 1, x, y, k) if z % 2 == 0 else None), half)
    across, even, odd = gather_pieces(block, row_tiles, col_tiles, tile)
    half, across, to_far = lax.optimization_barrier((half, across, jnp.where(y == 0, across, even)))
    beside = send(half, lambda z, x, y, k: (z, 1 - x, y, k))
    above = send(half, lambda z, x, y, k: (z, x, 1 - y, k))
    corner = send(half, lambda z, x, y, k: (z, 1 - x, 1 - y, k))
    far = send(to_far, far_stage)
    over = send(across, lambda z, x, y, k: (z, x, 1, k) if y == 0 else None)
    mine = jnp.concatenate([half, beside, above, corner], axis=0)
    other = send(mine, lambda z, x, y, k: (z, x, y, 1 - k))
    state = corner_start(jnp.stack([core, x, y]).astype(jnp.int32), mine, other)

    state, far, over = lax.optimization_barrier((state, far, over))
    rows_mine = jnp.where(y == 0, across, over)
    first_held = jnp.where(z == 0, even, jnp.where(y == 0, jnp.where(z == 2, across, far), jnp.where(z == 2, far, over)))
    to_near = jnp.where(y == 0, jnp.where(z == 3, far, across), jnp.where(z == 0, odd, over))
    near = send(to_near, near_stage)
    first = [first_held, send(first_held, same_core(0)), send(first_held, cross_core(0))]
    rows_other = send(rows_mine, lambda z, x, y, k: (z, x, y, 1 - k))
    state, first_held, to_near = lax.optimization_barrier((state, first_held, to_near))
    inverse, gram = corner_end(state)

    inverse, near = lax.optimization_barrier((inverse, near))
    last_held = jnp.where(z == 0, odd, near)
    inverse, last_held = lax.optimization_barrier((inverse, last_held))
    last = [last_held, send(last_held, same_core(1)), send(last_held, cross_core(1))]
    pieces = [first, last]

    places = []
    for stage in range(2):
        first_odd = jnp.where(y == 0, (z == 1) | (z == 2), z == 3).astype(jnp.int32)
        parity = jnp.where(z == 0, stage, first_odd if stage == 0 else 1 - first_odd)
        rowwise = (z == 0) | ((y == 1) & (z == 2 - stage))
        own = core == x
        zero = jnp.where(rowwise, jnp.where(x == 0, 0, 1), jnp.where(own, jnp.where(core == 0, 0, 1), jnp.where(core == 0, 1, 2)))
        one = jnp.where(rowwise, jnp.where(x == 0, 1, 0), jnp.where(own, jnp.where(core == 0, 1, 0), jnp.where(core == 0, 2, 1)))
        places.append(jnp.stack([row, col, parity, zero, one, core]).astype(jnp.int32))
    result = trailing(places, block, rows_mine, rows_other, inverse, gram, pieces, row_tiles, col_tiles, tile)
    return result.reshape(kernel_tiles.shape)


def from_root(value, axis, root):
    mine = lax.axis_index(axis) == root
    return lax.psum(jnp.where(mine, value, jnp.zeros_like(value)), axis)


def shards_any(kernel_tiles):
    row_tiles, _, tile, col_tiles, _, _ = kernel_tiles.shape
    row = lax.axis_index("prow")
    col = lax.axis_index("pcol")
    per = tile // LANES
    block = kernel_tiles.reshape(row_tiles * tile * col_tiles * per, LANES)
    across, even, odd = gather_pieces(block, row_tiles, col_tiles, tile)
    rows = [from_root(across, "pcol", panel) for panel in range(2)]
    lead = kernel_tiles[0, 0, :, 0, 0, :].reshape(tile * per, LANES)
    middle = tile * per // 2
    columns = []
    for panel in range(2):
        tops = [from_root(from_root(lead, "pcol", panel), "prow", p) for p in range(2)]
        columns.append(jnp.concatenate([t[s : s + middle] for s in (0, middle) for t in tops], axis=0))
    inverse, gram = corner_end(corner_start(jnp.zeros((3,), jnp.int32), columns[0], columns[1]))
    pieces = []
    places = []
    zero = jnp.zeros((), jnp.int32)
    for stage, part in enumerate((even, odd)):
        panels = [from_root(part, "prow", p) for p in range(2)]
        pieces.append(panels + [panels[0]])
        places.append(jnp.stack([row, col, zero + stage, zero, zero + 1, zero]).astype(jnp.int32))
    result = trailing(places, block, rows[0], rows[1], inverse, gram, pieces, row_tiles, col_tiles, tile)
    return result.reshape(kernel_tiles.shape)


def solution(mesh):
    in_specs = (P(None, "prow", None, None, "pcol", None),)
    out_specs = P(None, "prow", None, None, "pcol", None)
    body = shards if (mesh.shape["prow"], mesh.shape["pcol"]) == (8, 4) else shards_any
    return jax.shard_map(body, mesh=mesh, in_specs=in_specs, out_specs=out_specs, check_vma=False)
```

```python
import functools

import jax
import jax.numpy as jnp
from jax import lax
from jax.experimental import pallas as pl
from jax.experimental.pallas import tpu as pltpu
from jax.sharding import PartitionSpec as P

HI = lax.Precision.HIGHEST
F32 = jnp.float32
BF16 = jnp.bfloat16
LANES = 128
VMEM_BYTES = 56 * 1024 * 1024


def splat(x, shape):
    return jnp.broadcast_to(x, shape)


def reciprocal(x):
    r = pl.reciprocal(x, approx=True)
    for _ in range(2):
        r = r * (2.0 - x * r)
    return r


def inverse_factor_128(block):
    size = 128
    step = 8
    count = size // step
    lane = lax.broadcasted_iota(jnp.int32, (step, size), 1)
    sub = lax.broadcasted_iota(jnp.int32, (step, size), 0)
    rows = [block[step * i : step * (i + 1), :] for i in range(count)]
    shape = (step, size)
    for j in range(count):
        base = step * j
        cols = [splat(rows[j][:, base + t : base + t + 1], shape) for t in range(step)]
        a = {}
        for t in range(step):
            for s in range(t, step):
                a[s, t] = splat(cols[t][s : s + 1, :], shape)
        in_block = (lane >= base) & (lane < base + step)
        unit = jnp.where(lane - base == sub, F32(1.0), F32(0.0))
        own = jnp.where(in_block, unit, rows[j])
        if j + 1 < count:
            below = [splat(rows[j + 1][:, base + t : base + t + 1], shape) for t in range(step)]
            near = jnp.where(in_block, F32(0.0), rows[j + 1])
        m = {}
        u = []
        w = []
        done = jnp.zeros(shape, F32)
        for t in range(0, step, 2):
            p, b, c = a[t, t], a[t + 1, t], a[t + 1, t + 1]
            det = p * c - b * b
            inv = reciprocal(det)
            for s in range(t + 2, step):
                m[s, t] = (c * a[s, t] - b * a[s, t + 1]) * inv
                m[s, t + 1] = (p * a[s, t + 1] - b * a[s, t]) * inv
            for v in range(t + 2, step):
                for s in range(v, step):
                    a[s, v] = a[s, v] - (m[s, t] * a[v, t] + m[s, t + 1] * a[v, t + 1])
            for k in (t, t + 1):
                row = splat(own[k : k + 1, :], shape)
                for s in range(t):
                    row = row - m[k, s] * u[s]
                u.append(row)
            w.append((c * u[t] - b * u[t + 1]) * inv)
            w.append((p * u[t + 1] - b * u[t]) * inv)
            root = lax.rsqrt(p)
            over = root * root
            done = jnp.where(sub == t, u[t] * root, done)
            done = jnp.where(sub == t + 1, (u[t + 1] - (b * over) * u[t]) * lax.rsqrt(det * over), done)
            if j + 1 < count:
                for k in (t, t + 1):
                    for s in range(t):
                        below[k] = below[k] - m[k, s] * below[s]
                near = near - (below[t] * w[t] + below[t + 1] * w[t + 1])
        if j + 1 < count:
            rows[j + 1] = near
        g = [None] * step
        for t in reversed(range(0, step, 2)):
            for k in (t + 1, t):
                row = w[k]
                for s in reversed(range(t + 2, step)):
                    row = row - m[s, k] * g[s]
                g[k] = row
        for i in range(j + 2, count):
            acc = jnp.where(in_block, F32(0.0), rows[i])
            for t in reversed(range(step)):
                acc = acc - splat(rows[i][:, base + t : base + t + 1], shape) * g[t]
            rows[i] = acc
        rows[j] = jnp.where(lane < base + step, done, F32(0.0))
    return jnp.concatenate(rows, axis=0)


def eliminate(state, first, last):
    rows = state.shape[0]
    for o in range(first, last):
        lo, hi = o * LANES, (o + 1) * LANES
        diag = inverse_factor_128(state[lo:hi, lo:hi])
        upper = jnp.dot(diag, state[lo:hi, :], precision=HI, preferred_element_type=F32)
        parts = ([upper[:, :lo]] if lo else []) + [diag] + ([upper[:, hi:]] if hi < rows else [])
        wide = jnp.concatenate(parts, axis=1)
        if hi < rows:
            state[hi:, lo:hi] = jnp.zeros((rows - hi, LANES), F32)
            state[hi:, :] -= lax.dot_general(
                upper[:, hi:], wide, (((0,), (0,)), ((), ())), precision=HI, preferred_element_type=F32
            )
            state[lo:hi, hi:] = jnp.zeros((LANES, rows - hi), F32)
        state[lo:hi, :hi] = wide[:, :hi]


def corner_start_kernel(place_ref, mine_ref, other_ref, state):
    core, side, across = place_ref[0], place_ref[1], place_ref[2]
    rows = state.shape[0]
    tile = rows // 2
    half = tile // 2
    per = tile // LANES
    for which, ref in ((core, mine_ref), (1 - core, other_ref)):
        for target in range(2):

            @pl.when(which == target)
            def _(ref=ref, target=target):
                for part in range(4):
                    at_side = side if part % 2 == 0 else 1 - side
                    at_half = across if part < 2 else 1 - across
                    at = pl.multiple_of(at_side * tile + at_half * half, half)
                    for h in range(per):
                        start = target * tile + h * LANES
                        state[pl.ds(at, half), start : start + LANES] = ref[
                            pl.ds(part * half * per + h, half, stride=per), :
                        ]

    eliminate(state, 0, tile // LANES)


def corner_end_kernel(state_ref, inverse_ref):
    rows = state_ref.shape[0]
    inverse_ref[...] = state_ref[...]
    eliminate(inverse_ref, rows // 2 // LANES, rows // LANES)


CORNER_COST = pl.CostEstimate(flops=1000, bytes_accessed=1000, transcendentals=0)


def corner_start(place, mine, other):
    width = mine.shape[0] // 2
    vmem = pl.BlockSpec(memory_space=pltpu.VMEM)
    return pl.pallas_call(
        corner_start_kernel,
        out_shape=jax.ShapeDtypeStruct((width, width), F32),
        in_specs=[pl.BlockSpec(memory_space=pltpu.SMEM), vmem, vmem],
        out_specs=vmem,
        compiler_params=pltpu.CompilerParams(vmem_limit_bytes=16 * 1024 * 1024),
        cost_estimate=CORNER_COST,
        name="corner_start",
    )(place, mine, other)


def corner_end(state):
    vmem = pl.BlockSpec(memory_space=pltpu.VMEM)
    return pl.pallas_call(
        corner_end_kernel,
        out_shape=jax.ShapeDtypeStruct(state.shape, F32),
        in_specs=[vmem],
        out_specs=vmem,
        compiler_params=pltpu.CompilerParams(vmem_limit_bytes=16 * 1024 * 1024),
        cost_estimate=CORNER_COST,
        name="corner_end",
    )(state)


def gather_kernel(row_tiles, col_tiles, tile, block_ref, across_ref, even_ref, odd_ref):
    step = pl.program_id(0)
    per = tile // LANES
    stride = col_tiles * per
    keep = row_tiles * per
    first = jnp.concatenate([block_ref[pl.ds(h, tile, stride=stride), :] for h in range(per)], axis=1).T
    for h in range(per):
        across_ref[pl.ds(step * per + h, tile, stride=keep), :] = first[:, h * LANES : (h + 1) * LANES]

    @pl.when(step == 0)
    def _():
        keep = col_tiles // 2 * per
        for parity, ref in enumerate((even_ref, odd_ref)):
            for i in range(col_tiles // 2):
                for h in range(per):
                    ref[pl.ds(i * per + h, tile, stride=keep), :] = block_ref[
                        pl.ds((2 * i + parity) * per + h, tile, stride=stride), :
                    ]


def gather_pieces(block, row_tiles, col_tiles, tile):
    per = tile // LANES
    shapes = [tile * row_tiles * per] + [tile * (col_tiles // 2) * per] * 2
    return pl.pallas_call(
        functools.partial(gather_kernel, row_tiles, col_tiles, tile),
        grid=(row_tiles,),
        out_shape=[jax.ShapeDtypeStruct((s, LANES), F32) for s in shapes],
        in_specs=[pl.BlockSpec((tile * col_tiles * per, LANES), lambda a: (a, 0))],
        out_specs=[pl.BlockSpec((s, LANES), lambda a: (0, 0)) for s in shapes],
        compiler_params=pltpu.CompilerParams(vmem_limit_bytes=VMEM_BYTES),
        cost_estimate=pl.CostEstimate(flops=1000, bytes_accessed=1000, transcendentals=0),
        name="gather_pieces",
    )(block)


def halves(x):
    high = x.astype(BF16)
    return high, (x - high.astype(F32)).astype(BF16)


def product(a, b, dims):
    (a_high, a_low), (b_high, b_low) = a, b
    dot = functools.partial(lax.dot_general, dimension_numbers=(dims, ((), ())), preferred_element_type=F32)
    return dot(a_high, b_high) + (dot(a_low, b_high) + dot(a_high, b_low))


def load_columns(place_ref, pieces, raw, col_high, col_low, sems, tile, count):
    per = tile // LANES
    for panel in range(2):
        for which, ref in enumerate(pieces):

            @pl.when(place_ref[3 + panel] == which)
            def _(panel=panel, ref=ref):
                pltpu.make_async_copy(ref, raw.at[panel], sems.at[panel]).start()

    for panel in range(2):
        pltpu.make_async_copy(pieces[0], raw.at[panel], sems.at[panel]).wait()
        for i in range(count):
            for h in range(per):
                high, low = halves(raw[panel, pl.ds(i * per + h, tile, stride=count * per), :])
                at = (i * per + h) * LANES
                col_high[panel * tile : (panel + 1) * tile, at : at + LANES] = high
                col_low[panel * tile : (panel + 1) * tile, at : at + LANES] = low


def subtract(place_ref, block_ref, out_ref, weights, col_high, col_low, tile, count):
    per = tile // LANES
    parity = place_ref[2]
    for i in range(count):
        at = i * tile
        update = product(weights, (col_high[:, at : at + tile], col_low[:, at : at + tile]), ((1,), (0,)))
        for h in range(per):
            where = pl.ds((2 * i + parity) * per + h, tile, stride=2 * count * per)
            out_ref[where, :] = block_ref[where, :] - update[:, h * LANES : (h + 1) * LANES]


def first_kernel(tile, row_tiles, count, place_ref, block_ref, rows_mine, rows_other, inverse_ref,
                 piece_a, piece_b, piece_c, out_ref, high_ref, low_ref, solved_ref, raw, col_high, col_low, sems,
                 inverse_high, inverse_low):
    step = pl.program_id(0)
    row, col, core = place_ref[0], place_ref[1], place_ref[5]
    per = tile // LANES

    @pl.when(step == 0)
    def _():
        inverse_high[...], inverse_low[...] = halves(inverse_ref[...])
        load_columns(place_ref, (piece_a, piece_b, piece_c), raw, col_high, col_low, sems, tile, count)

    out_ref[...] = block_ref[...]
    mine, other = [
        jnp.concatenate([r[pl.ds(step * per + h, tile, stride=row_tiles * per), :] for h in range(per)], axis=1)
        for r in (rows_mine, rows_other)
    ]
    lead = jnp.concatenate([jnp.where(core == 0, mine, other), jnp.where(core == 0, other, mine)], axis=0)
    inverse = (inverse_high[...], inverse_low[...])
    solved = product(halves(lead.T), inverse, ((1,), (1,)))
    weights = halves(product(halves(solved), inverse, ((1,), (0,))))
    high_ref[...], low_ref[...] = weights
    subtract(place_ref, block_ref, out_ref, weights, col_high, col_low, tile, count)

    @pl.when(col < 2)
    def _():
        mine = jnp.where(col == 0, solved[:, :tile], solved[:, tile:])
        r = lax.broadcasted_iota(jnp.int32, (tile, tile), 0)
        s = lax.broadcasted_iota(jnp.int32, (tile, tile), 1)
        top = (step == 0) & (row < 2)
        on_diag = top & (row == col)
        above = top & (row < col)
        keep = jnp.where(on_diag, s - r, jnp.where(above, 1, 0)) <= 0
        solved_ref[...] = jnp.where(keep, mine, F32(0.0))


def second_kernel(tile, row_tiles, count, place_ref, block_ref, high_ref, low_ref, solved_ref, piece_a, piece_b,
                  piece_c, out_ref, raw, col_high, col_low, sems):
    step = pl.program_id(0)
    row, col = place_ref[0], place_ref[1]
    per = tile // LANES
    top = (step == 0) & (row < 2)

    @pl.when(step == 0)
    def _():
        load_columns(place_ref, (piece_a, piece_b, piece_c), raw, col_high, col_low, sems, tile, count)

    @pl.when(top)
    def _():
        out_ref[...] = jnp.zeros_like(out_ref)

    @pl.when(jnp.logical_not(top))
    def _():
        out_ref[...] = block_ref[...]
        subtract(place_ref, block_ref, out_ref, (high_ref[...], low_ref[...]), col_high, col_low, tile, count)

    @pl.when(col < 2)
    def _():
        for h in range(per):
            out_ref[pl.ds(h, tile, stride=2 * count * per), :] = solved_ref[:, h * LANES : (h + 1) * LANES]


def trailing(places, block, rows_mine, rows_other, inverse, pieces, row_tiles, col_tiles, tile):
    per = tile // LANES
    depth = inverse.shape[0]
    count = col_tiles // 2
    smem = pl.BlockSpec(memory_space=pltpu.SMEM)
    whole = pl.BlockSpec((depth, depth), lambda a: (0, 0))
    rows_spec = pl.BlockSpec(rows_mine.shape, lambda a: (0, 0))
    block_spec = pl.BlockSpec((tile * col_tiles * per, LANES), lambda a: (a, 0))
    weight_spec = pl.BlockSpec((tile, depth), lambda a: (a, 0))
    solved_spec = pl.BlockSpec((tile, tile), lambda a: (a, 0))
    anywhere = [pl.BlockSpec(memory_space=pl.ANY)] * 3
    scratch = [
        pltpu.VMEM((2, tile * count * per, LANES), F32),
        pltpu.VMEM((depth, count * tile), BF16),
        pltpu.VMEM((depth, count * tile), BF16),
        pltpu.SemaphoreType.DMA((2,)),
    ]
    total = row_tiles * tile
    params = pltpu.CompilerParams(vmem_limit_bytes=40 * 1024 * 1024)
    cost = pl.CostEstimate(flops=1000, bytes_accessed=1000, transcendentals=0)
    block, high, low, solved = pl.pallas_call(
        functools.partial(first_kernel, tile, row_tiles, count),
        grid=(row_tiles,),
        out_shape=[
            jax.ShapeDtypeStruct(block.shape, F32),
            jax.ShapeDtypeStruct((total, depth), BF16),
            jax.ShapeDtypeStruct((total, depth), BF16),
            jax.ShapeDtypeStruct((total, tile), F32),
        ],
        in_specs=[smem, block_spec, rows_spec, rows_spec, whole] + anywhere,
        out_specs=[block_spec, weight_spec, weight_spec, solved_spec],
        scratch_shapes=scratch + [pltpu.VMEM((depth, depth), BF16)] * 2,
        compiler_params=params,
        cost_estimate=cost,
        name="trailing_first",
    )(places[0], block, rows_mine, rows_other, inverse, *pieces[0])
    return pl.pallas_call(
        functools.partial(second_kernel, tile, row_tiles, count),
        grid=(row_tiles,),
        out_shape=jax.ShapeDtypeStruct(block.shape, F32),
        in_specs=[smem, block_spec, weight_spec, weight_spec, solved_spec] + anywhere,
        out_specs=block_spec,
        scratch_shapes=scratch,
        compiler_params=params,
        cost_estimate=cost,
        input_output_aliases={1: 0},
        name="trailing_second",
    )(places[1], block, high, low, solved, *pieces[1])


AXES = ("prow", "pcol")


def send(value, route):
    pairs = []
    for device in range(32):
        to = route(device // 8, device // 4 % 2, device // 2 % 2, device % 2)
        if to is not None:
            pairs.append((device, ((to[0] * 2 + to[1]) * 2 + to[2]) * 2 + to[3]))
    return lax.ppermute(value, AXES, pairs)


def far_stage(z, x, y, k):
    to = {(0, 0): 3, (2, 0): 1, (0, 1): 2}.get((z, y))
    return None if to is None else (to, x, y, k)


def near_stage(z, x, y, k):
    to = {(0, 0): 1, (2, 0): 3, (3, 0): 2, (0, 1): 1, (1, 1): 3, (3, 1): 2}.get((z, y))
    return None if to is None else (to, x, y, k)


def by_rows(stage, z, y):
    return z == 0 or (y == 1 and z == (2 if stage == 0 else 1))


def same_core(stage):
    def route(z, x, y, k):
        if by_rows(stage, z, y) or k == x:
            return (z, 1 - x, y, k)
        return (z, x, y, x)

    return route


def cross_core(stage):
    def route(z, x, y, k):
        if by_rows(stage, z, y) or k == x:
            return None
        return (z, 1 - x, y, x)

    return route


def shards(kernel_tiles):
    row_tiles, _, tile, col_tiles, _, _ = kernel_tiles.shape
    row = lax.axis_index("prow")
    col = lax.axis_index("pcol")
    z, x, y, core = row // 2, row % 2, col // 2, col % 2
    per = tile // LANES
    block = kernel_tiles.reshape(row_tiles * tile * col_tiles * per, LANES)

    lead = kernel_tiles[0, 0, :, 0, 0, :].reshape(tile * per, LANES)
    middle = tile * per // 2
    half = send(lead[middle:], lambda z, x, y, k: (z, x, 1, k) if z == 0 and y == 0 else None)
    across, even, odd = gather_pieces(block, row_tiles, col_tiles, tile)
    to_far = jnp.where(y == 0, across, even)
    half, across, to_far = lax.optimization_barrier((half, across, to_far))
    over = send(across, lambda z, x, y, k: (z, x, 1, k) if y == 0 else None)
    half = jnp.where(y == 0, lead[:middle], half)
    half = jnp.where(z == 2, send(half, lambda z, x, y, k: (2, x, y, k) if z == 0 else None), half)
    half, to_far = lax.optimization_barrier((half, to_far))
    half = jnp.where(z % 2 == 1, send(half, lambda z, x, y, k: (z + 1, x, y, k) if z % 2 == 0 else None), half)
    far = send(to_far, far_stage)
    beside = send(half, lambda z, x, y, k: (z, 1 - x, y, k))
    above = send(half, lambda z, x, y, k: (z, x, 1 - y, k))
    corner = send(half, lambda z, x, y, k: (z, 1 - x, 1 - y, k))
    mine = jnp.concatenate([half, beside, above, corner], axis=0)
    other = send(mine, lambda z, x, y, k: (z, x, y, 1 - k))
    state = corner_start(jnp.stack([core, x, y]).astype(jnp.int32), mine, other)

    state, far, over = lax.optimization_barrier((state, far, over))
    rows_mine = jnp.where(y == 0, across, over)
    first_held = jnp.where(z == 0, even, jnp.where(y == 0, jnp.where(z == 2, across, far), jnp.where(z == 2, far, over)))
    to_near = jnp.where(y == 0, jnp.where(z == 3, far, across), jnp.where(z == 0, odd, over))
    near = send(to_near, near_stage)
    first = [first_held, send(first_held, same_core(0)), send(first_held, cross_core(0))]
    rows_other = send(rows_mine, lambda z, x, y, k: (z, x, y, 1 - k))
    state, first_held, to_near = lax.optimization_barrier((state, first_held, to_near))
    inverse = corner_end(state)

    inverse, near = lax.optimization_barrier((inverse, near))
    last_held = jnp.where(z == 0, odd, near)
    inverse, last_held = lax.optimization_barrier((inverse, last_held))
    last = [last_held, send(last_held, same_core(1)), send(last_held, cross_core(1))]
    pieces = [first, last]

    places = []
    for stage in range(2):
        first_odd = jnp.where(y == 0, (z == 1) | (z == 2), z == 3).astype(jnp.int32)
        parity = jnp.where(z == 0, stage, first_odd if stage == 0 else 1 - first_odd)
        rowwise = (z == 0) | ((y == 1) & (z == 2 - stage))
        own = core == x
        zero = jnp.where(rowwise, jnp.where(x == 0, 0, 1), jnp.where(own, jnp.where(core == 0, 0, 1), jnp.where(core == 0, 1, 2)))
        one = jnp.where(rowwise, jnp.where(x == 0, 1, 0), jnp.where(own, jnp.where(core == 0, 1, 0), jnp.where(core == 0, 2, 1)))
        places.append(jnp.stack([row, col, parity, zero, one, core]).astype(jnp.int32))
    result = trailing(places, block, rows_mine, rows_other, inverse, pieces, row_tiles, col_tiles, tile)
    return result.reshape(kernel_tiles.shape)


def from_root(value, axis, root):
    mine = lax.axis_index(axis) == root
    return lax.psum(jnp.where(mine, value, jnp.zeros_like(value)), axis)


def shards_any(kernel_tiles):
    row_tiles, _, tile, col_tiles, _, _ = kernel_tiles.shape
    row = lax.axis_index("prow")
    col = lax.axis_index("pcol")
    per = tile // LANES
    block = kernel_tiles.reshape(row_tiles * tile * col_tiles * per, LANES)
    across, even, odd = gather_pieces(block, row_tiles, col_tiles, tile)
    rows = [from_root(across, "pcol", panel) for panel in range(2)]
    lead = kernel_tiles[0, 0, :, 0, 0, :].reshape(tile * per, LANES)
    middle = tile * per // 2
    columns = []
    for panel in range(2):
        tops = [from_root(from_root(lead, "pcol", panel), "prow", p) for p in range(2)]
        columns.append(jnp.concatenate([t[s : s + middle] for s in (0, middle) for t in tops], axis=0))
    inverse = corner_end(corner_start(jnp.zeros((3,), jnp.int32), columns[0], columns[1]))
    pieces = []
    places = []
    zero = jnp.zeros((), jnp.int32)
    for stage, part in enumerate((even, odd)):
        panels = [from_root(part, "prow", p) for p in range(2)]
        pieces.append(panels + [panels[0]])
        places.append(jnp.stack([row, col, zero + stage, zero, zero + 1, zero]).astype(jnp.int32))
    result = trailing(places, block, rows[0], rows[1], inverse, pieces, row_tiles, col_tiles, tile)
    return result.reshape(kernel_tiles.shape)


def solution(mesh):
    in_specs = (P(None, "prow", None, None, "pcol", None),)
    out_specs = P(None, "prow", None, None, "pcol", None)
    body = shards if (mesh.shape["prow"], mesh.shape["pcol"]) == (8, 4) else shards_any
    return jax.shard_map(body, mesh=mesh, in_specs=in_specs, out_specs=out_specs, check_vma=False)
```

```python
import functools

import jax
import jax.numpy as jnp
from jax import lax
from jax.experimental import pallas as pl
from jax.experimental.pallas import tpu as pltpu
from jax.sharding import PartitionSpec as P

HI = lax.Precision.HIGHEST
F32 = jnp.float32
BF16 = jnp.bfloat16
LANES = 128
VMEM_BYTES = 56 * 1024 * 1024


def splat(x, shape):
    return jnp.broadcast_to(x, shape)


def reciprocal(x):
    r = pl.reciprocal(x, approx=True)
    for _ in range(2):
        r = r * (2.0 - x * r)
    return r


def inverse_factor_128(block):
    size = 128
    step = 8
    count = size // step
    lane = lax.broadcasted_iota(jnp.int32, (step, size), 1)
    sub = lax.broadcasted_iota(jnp.int32, (step, size), 0)
    rows = [block[step * i : step * (i + 1), :] for i in range(count)]
    shape = (step, size)
    for j in range(count):
        base = step * j
        cols = [splat(rows[j][:, base + t : base + t + 1], shape) for t in range(step)]
        a = {}
        for t in range(step):
            for s in range(t, step):
                a[s, t] = splat(cols[t][s : s + 1, :], shape)
        in_block = (lane >= base) & (lane < base + step)
        unit = jnp.where(lane - base == sub, F32(1.0), F32(0.0))
        own = jnp.where(in_block, unit, rows[j])
        if j + 1 < count:
            below = [splat(rows[j + 1][:, base + t : base + t + 1], shape) for t in range(step)]
            near = jnp.where(in_block, F32(0.0), rows[j + 1])
        m = {}
        u = []
        w = []
        done = jnp.zeros(shape, F32)
        for t in range(0, step, 2):
            p, b, c = a[t, t], a[t + 1, t], a[t + 1, t + 1]
            det = p * c - b * b
            inv = reciprocal(det)
            for s in range(t + 2, step):
                m[s, t] = (c * a[s, t] - b * a[s, t + 1]) * inv
                m[s, t + 1] = (p * a[s, t + 1] - b * a[s, t]) * inv
            for v in range(t + 2, step):
                for s in range(v, step):
                    a[s, v] = a[s, v] - (m[s, t] * a[v, t] + m[s, t + 1] * a[v, t + 1])
            for k in (t, t + 1):
                row = splat(own[k : k + 1, :], shape)
                for s in range(t):
                    row = row - m[k, s] * u[s]
                u.append(row)
            w.append((c * u[t] - b * u[t + 1]) * inv)
            w.append((p * u[t + 1] - b * u[t]) * inv)
            root = lax.rsqrt(p)
            over = root * root
            done = jnp.where(sub == t, u[t] * root, done)
            done = jnp.where(sub == t + 1, (u[t + 1] - (b * over) * u[t]) * lax.rsqrt(det * over), done)
            if j + 1 < count:
                for k in (t, t + 1):
                    for s in range(t):
                        below[k] = below[k] - m[k, s] * below[s]
                near = near - (below[t] * w[t] + below[t + 1] * w[t + 1])
        if j + 1 < count:
            rows[j + 1] = near
        g = [None] * step
        for t in reversed(range(0, step, 2)):
            for k in (t + 1, t):
                row = w[k]
                for s in reversed(range(t + 2, step)):
                    row = row - m[s, k] * g[s]
                g[k] = row
        for i in range(j + 2, count):
            acc = jnp.where(in_block, F32(0.0), rows[i])
            for t in reversed(range(step)):
                acc = acc - splat(rows[i][:, base + t : base + t + 1], shape) * g[t]
            rows[i] = acc
        rows[j] = jnp.where(lane < base + step, done, F32(0.0))
    return jnp.concatenate(rows, axis=0)


def eliminate(state, first, last):
    rows = state.shape[0]
    for o in range(first, last):
        lo, hi = o * LANES, (o + 1) * LANES
        diag = inverse_factor_128(state[lo:hi, lo:hi])
        upper = jnp.dot(diag, state[lo:hi, :], precision=HI, preferred_element_type=F32)
        parts = ([upper[:, :lo]] if lo else []) + [diag] + ([upper[:, hi:]] if hi < rows else [])
        wide = jnp.concatenate(parts, axis=1)
        if hi < rows:
            state[hi:, lo:hi] = jnp.zeros((rows - hi, LANES), F32)
            state[hi:, :] -= lax.dot_general(
                upper[:, hi:], wide, (((0,), (0,)), ((), ())), precision=HI, preferred_element_type=F32
            )
            state[lo:hi, hi:] = jnp.zeros((LANES, rows - hi), F32)
        state[lo:hi, :hi] = wide[:, :hi]


def corner_start_kernel(place_ref, mine_ref, other_ref, state):
    core, side, across = place_ref[0], place_ref[1], place_ref[2]
    rows = state.shape[0]
    tile = rows // 2
    half = tile // 2
    per = tile // LANES
    for which, ref in ((core, mine_ref), (1 - core, other_ref)):
        for part in range(4):
            at_side = side if part % 2 == 0 else 1 - side
            at_half = across if part < 2 else 1 - across
            at = pl.multiple_of(which * tile + at_half * half, half)
            for target in range(2):

                @pl.when(at_side == target)
                def _(ref=ref, part=part, at=at, target=target):
                    for h in range(per):
                        start = target * tile + h * LANES
                        state[pl.ds(at, half), start : start + LANES] = ref[
                            pl.ds(part * half * per + h, half, stride=per), :
                        ]

    eliminate(state, 0, tile // LANES)


def corner_end_kernel(state_ref, inverse_ref):
    rows = state_ref.shape[0]
    inverse_ref[...] = state_ref[...]
    eliminate(inverse_ref, rows // 2 // LANES, rows // LANES)


COST = pl.CostEstimate(flops=1000, bytes_accessed=1000, transcendentals=0)


def corner_start(place, mine, other):
    width = mine.shape[0] // 2
    vmem = pl.BlockSpec(memory_space=pltpu.VMEM)
    return pl.pallas_call(
        corner_start_kernel,
        out_shape=jax.ShapeDtypeStruct((width, width), F32),
        in_specs=[pl.BlockSpec(memory_space=pltpu.SMEM), vmem, vmem],
        out_specs=vmem,
        compiler_params=pltpu.CompilerParams(vmem_limit_bytes=16 * 1024 * 1024),
        cost_estimate=COST,
        name="corner_start",
    )(place, mine, other)


def corner_end(state):
    vmem = pl.BlockSpec(memory_space=pltpu.VMEM)
    return pl.pallas_call(
        corner_end_kernel,
        out_shape=jax.ShapeDtypeStruct(state.shape, F32),
        in_specs=[vmem],
        out_specs=vmem,
        compiler_params=pltpu.CompilerParams(vmem_limit_bytes=16 * 1024 * 1024),
        cost_estimate=COST,
        name="corner_end",
    )(state)


def transposed_tile(block_ref, tile, stride):
    per = tile // LANES
    return jnp.concatenate([block_ref[pl.ds(h, tile, stride=stride), :] for h in range(per)], axis=1).T


def store_tile(ref, start, value, tile):
    per = tile // LANES
    for h in range(per):
        ref[pl.ds(start + h, tile, stride=per), :] = value[:, h * LANES : (h + 1) * LANES]


def lead_kernel(tile, block_ref, out_ref):
    store_tile(out_ref, 0, transposed_tile(block_ref.reshape(tile * GROUP, LANES), tile, GROUP), tile)


def gather_kernel(tile, col_tiles, row_tiles, place_ref, lead_ref, block_ref, top_ref, rest_ref, far_ref, even_ref,
                  odd_ref):
    step = pl.program_id(0)
    per = tile // LANES
    size = tile * per
    value = transposed_tile(block_ref.reshape(tile * GROUP, LANES), tile, GROUP)
    store_tile(rest_ref, 0, value, tile)

    @pl.when(place_ref[0] == 0)
    def _():
        store_tile(far_ref, pl.multiple_of((step + 1) * size, size), value, tile)

    @pl.when(step == 0)
    def _():
        for parity, ref in enumerate((even_ref, odd_ref)):
            for i in range(col_tiles // 2):
                for h in range(per):
                    ref[pl.ds(i * size + h, tile, stride=per), :] = top_ref[
                        pl.ds((2 * i + parity) * per + h, tile, stride=col_tiles * per), :
                    ]

        @pl.when(place_ref[0] == 0)
        def _():
            far_ref[:size, :] = lead_ref[...]

        @pl.when(place_ref[0] != 0)
        def _():
            far_ref[...] = even_ref[...]


GROUP = 8


def grouped(block, row_tiles, col_tiles, tile):
    return block.reshape(row_tiles * tile, col_tiles * tile // LANES // GROUP, GROUP, LANES)


def gather_lead(block, row_tiles, col_tiles, tile):
    return pl.pallas_call(
        functools.partial(lead_kernel, tile),
        grid=(1,),
        out_shape=jax.ShapeDtypeStruct((tile * tile // LANES, LANES), F32),
        in_specs=[pl.BlockSpec((tile, None, GROUP, LANES), lambda a: (0, 0, 0, 0))],
        out_specs=pl.BlockSpec((tile * tile // LANES, LANES), lambda a: (0, 0)),
        compiler_params=pltpu.CompilerParams(vmem_limit_bytes=VMEM_BYTES),
        cost_estimate=COST,
        name="gather_lead",
    )(grouped(block, row_tiles, col_tiles, tile))


def gather_pieces(place, lead, block, row_tiles, col_tiles, tile):
    per = tile // LANES
    size = tile * per
    top = (tile * col_tiles * per, LANES)
    whole = [size * row_tiles] + [size * (col_tiles // 2)] * 2
    return pl.pallas_call(
        functools.partial(gather_kernel, tile, col_tiles, row_tiles),
        grid=(row_tiles - 1,),
        out_shape=[jax.ShapeDtypeStruct((s, LANES), F32) for s in [size * (row_tiles - 1)] + whole],
        in_specs=[
            pl.BlockSpec(memory_space=pltpu.SMEM),
            pl.BlockSpec((size, LANES), lambda a: (0, 0)),
            pl.BlockSpec((tile, None, GROUP, LANES), lambda a: (a + 1, 0, 0, 0)),
            pl.BlockSpec(top, lambda a: (0, 0)),
        ],
        out_specs=[pl.BlockSpec((size, LANES), lambda a: (a, 0))]
        + [pl.BlockSpec((s, LANES), lambda a: (0, 0)) for s in whole],
        compiler_params=pltpu.CompilerParams(vmem_limit_bytes=VMEM_BYTES),
        cost_estimate=COST,
        name="gather_pieces",
    )(place, lead, grouped(block, row_tiles, col_tiles, tile), block)


def halves(x):
    high = x.astype(BF16)
    return high, (x - high.astype(F32)).astype(BF16)


def product(a, b, dims):
    (a_high, a_low), (b_high, b_low) = a, b
    dot = functools.partial(lax.dot_general, dimension_numbers=(dims, ((), ())), preferred_element_type=F32)
    return dot(a_high, b_high) + (dot(a_low, b_high) + dot(a_high, b_low))


def weights_kernel(tile, place_ref, rows_mine, rows_other, inverse_ref, high_ref, low_ref, solved_ref, inverse_high,
                   inverse_low):
    step = pl.program_id(0)
    row, col, core = place_ref[0], place_ref[1], place_ref[2]
    per = tile // LANES

    @pl.when(step == 0)
    def _():
        inverse_high[...], inverse_low[...] = halves(inverse_ref[...])

    mine, other = [
        jnp.concatenate([r[pl.ds(h, tile, stride=per), :] for h in range(per)], axis=1)
        for r in (rows_mine, rows_other)
    ]
    lead = jnp.concatenate([jnp.where(core == 0, mine, other).T, jnp.where(core == 0, other, mine).T], axis=1)
    inverse = (inverse_high[...], inverse_low[...])
    solved = product(halves(lead), inverse, ((1,), (1,)))
    high_ref[...], low_ref[...] = halves(product(halves(solved), inverse, ((1,), (0,))))

    @pl.when(col < 2)
    def _():
        mine = jnp.where(col == 0, solved[:, :tile], solved[:, tile:])
        r = lax.broadcasted_iota(jnp.int32, (tile, tile), 0)
        s = lax.broadcasted_iota(jnp.int32, (tile, tile), 1)
        top = (step == 0) & (row < 2)
        on_diag = top & (row == col)
        above = top & (row < col)
        keep = jnp.where(on_diag, s - r, jnp.where(above, 1, 0)) <= 0
        solved_ref[...] = jnp.where(keep, mine, F32(0.0))


def row_weights(place, rows_mine, rows_other, inverse, row_tiles, tile):
    depth = inverse.shape[0]
    rows_spec = pl.BlockSpec((tile * tile // LANES, LANES), lambda a: (a, 0))
    total = row_tiles * tile
    return pl.pallas_call(
        functools.partial(weights_kernel, tile),
        grid=(row_tiles,),
        out_shape=[jax.ShapeDtypeStruct((total, depth), BF16)] * 2 + [jax.ShapeDtypeStruct((total, tile), F32)],
        in_specs=[
            pl.BlockSpec(memory_space=pltpu.SMEM),
            rows_spec,
            rows_spec,
            pl.BlockSpec((depth, depth), lambda a: (0, 0)),
        ],
        out_specs=[pl.BlockSpec((tile, depth), lambda a: (a, 0))] * 2 + [pl.BlockSpec((tile, tile), lambda a: (a, 0))],
        scratch_shapes=[pltpu.VMEM((depth, depth), BF16)] * 2,
        compiler_params=pltpu.CompilerParams(vmem_limit_bytes=32 * 1024 * 1024),
        cost_estimate=COST,
        name="row_weights",
    )(place, rows_mine, rows_other, inverse)


def load_columns(place_ref, pieces, offsets, raw, col_high, col_low, sems, tile, count):
    per = tile // LANES
    size = count * tile * per
    for stage in range(2):
        for panel in range(2):
            for which, ref in enumerate(pieces[stage]):

                @pl.when(place_ref[3 + 2 * stage + panel] == which)
                def _(stage=stage, panel=panel, ref=ref):
                    pltpu.make_async_copy(
                        ref.at[pl.ds(offsets[stage], size), :], raw.at[stage, panel], sems.at[stage, panel]
                    ).start()

    for stage in range(2):
        for panel in range(2):
            pltpu.make_async_copy(
                pieces[stage][0].at[pl.ds(offsets[stage], size), :], raw.at[stage, panel], sems.at[stage, panel]
            ).wait()
            for i in range(count):
                for h in range(per):
                    high, low = halves(raw[stage, panel, pl.ds(i * tile * per + h, tile, stride=per), :])
                    at = ((stage * count + i) * per + h) * LANES
                    col_high[panel * tile : (panel + 1) * tile, at : at + LANES] = high
                    col_low[panel * tile : (panel + 1) * tile, at : at + LANES] = low


def trailing_kernel(tile, group, count, offsets, place_ref, block_ref, high_ref, low_ref, *rest):
    solved_ref = rest[0] if group == 0 else None
    pieces = (rest[1:4], rest[4:7])
    block_out, raw, col_high, col_low, sems = rest[-5:]
    step = pl.program_id(0)
    row, col = place_ref[0], place_ref[1]
    per = tile // LANES
    top = (step == 0) & (row < 2)
    block = block_ref.reshape(tile * GROUP, LANES)
    out = block_out.reshape(tile * GROUP, LANES)

    @pl.when(step == 0)
    def _():
        load_columns(place_ref, pieces, offsets, raw, col_high, col_low, sems, tile, count)

    @pl.when(top)
    def _():
        block_out[...] = jnp.zeros_like(block_out)

    @pl.when(jnp.logical_not(top))
    def _():
        weights = (high_ref[...], low_ref[...])
        for stage in range(2):
            parity = place_ref[2] if stage == 0 else 1 - place_ref[2]
            for i in range(count):
                at = (stage * count + i) * tile
                update = product(weights, (col_high[:, at : at + tile], col_low[:, at : at + tile]), ((1,), (0,)))
                for h in range(per):
                    where = pl.ds((2 * i + parity) * per + h, tile, stride=GROUP)
                    out[where, :] = block[where, :] - update[:, h * LANES : (h + 1) * LANES]

    if group == 0:

        @pl.when(col < 2)
        def _():
            for h in range(per):
                out[pl.ds(h, tile, stride=GROUP), :] = solved_ref[:, h * LANES : (h + 1) * LANES]


def trailing(group, place, block, weights, extra, pieces, offsets, row_tiles, col_tiles, tile):
    per = tile // LANES
    high, low = weights
    depth = high.shape[1]
    count = GROUP // per // 2
    view = grouped(block, row_tiles, col_tiles, tile)
    block_spec = pl.BlockSpec((tile, None, GROUP, LANES), lambda a: (a, group, 0, 0))
    weight_spec = pl.BlockSpec((tile, depth), lambda a: (a, 0))
    anywhere = pl.BlockSpec(memory_space=pl.ANY)
    return pl.pallas_call(
        functools.partial(trailing_kernel, tile, group, count, offsets),
        grid=(row_tiles,),
        out_shape=jax.ShapeDtypeStruct(view.shape, F32),
        in_specs=[pl.BlockSpec(memory_space=pltpu.SMEM), block_spec, weight_spec, weight_spec]
        + [pl.BlockSpec((tile, tile), lambda a: (a, 0)) if group == 0 else anywhere]
        + [anywhere] * 6,
        out_specs=block_spec,
        scratch_shapes=[
            pltpu.VMEM((2, 2, count * tile * per, LANES), F32),
            pltpu.VMEM((depth, 2 * count * tile), BF16),
            pltpu.VMEM((depth, 2 * count * tile), BF16),
            pltpu.SemaphoreType.DMA((2, 2)),
        ],
        input_output_aliases={} if group == 0 else {4: 0},
        compiler_params=pltpu.CompilerParams(vmem_limit_bytes=40 * 1024 * 1024),
        cost_estimate=COST,
        name="trailing_%d" % group,
    )(place, view, high, low, extra, *pieces[0], *pieces[1])


AXES = ("prow", "pcol")


def send(value, route):
    pairs = []
    for device in range(32):
        to = route(device // 8, device // 4 % 2, device // 2 % 2, device % 2)
        if to is not None:
            pairs.append((device, ((to[0] * 2 + to[1]) * 2 + to[2]) * 2 + to[3]))
    return lax.ppermute(value, AXES, pairs)


def far_stage(z, x, y, k):
    to = {(0, 0): 3, (2, 0): 1, (0, 1): 2}.get((z, y))
    return None if to is None else (to, x, y, k)


def near_stage(z, x, y, k):
    to = {(0, 0): 1, (2, 0): 3, (3, 0): 2, (0, 1): 1, (1, 1): 3, (3, 1): 2}.get((z, y))
    return None if to is None else (to, x, y, k)


def by_rows(stage, z, y):
    return z == 0 or (y == 1 and z == (2 if stage == 0 else 1))


def same_core(stage):
    def route(z, x, y, k):
        if by_rows(stage, z, y) or k == x:
            return (z, 1 - x, y, k)
        return (z, x, y, x)

    return route


def cross_core(stage):
    def route(z, x, y, k):
        if by_rows(stage, z, y) or k == x:
            return None
        return (z, 1 - x, y, x)

    return route


def shards(kernel_tiles):
    row_tiles, _, tile, col_tiles, _, _ = kernel_tiles.shape
    row = lax.axis_index("prow")
    col = lax.axis_index("pcol")
    z, x, y, core = row // 2, row % 2, col // 2, col % 2
    per = tile // LANES
    block = kernel_tiles.reshape(row_tiles * tile * col_tiles * per, LANES)

    lead = gather_lead(block, row_tiles, col_tiles, tile)
    middle = tile * per // 2
    over_first = send(lead, lambda z, x, y, k: (z, x, 1, k) if y == 0 else None)
    rest, to_far, even, odd = gather_pieces(y.reshape(1), lead, block, row_tiles, col_tiles, tile)
    over_first, rest, to_far = lax.optimization_barrier((over_first, rest, to_far))
    half = jnp.where(y == 0, lead[:middle], over_first[middle:])
    half = jnp.where(z == 2, send(half, lambda z, x, y, k: (2, x, y, k) if z == 0 else None), half)
    half, to_far = lax.optimization_barrier((half, to_far))
    half = jnp.where(z % 2 == 1, send(half, lambda z, x, y, k: (z + 1, x, y, k) if z % 2 == 0 else None), half)
    far = send(to_far, far_stage)
    beside = send(half, lambda z, x, y, k: (z, 1 - x, y, k))
    above = send(half, lambda z, x, y, k: (z, x, 1 - y, k))
    corner = send(half, lambda z, x, y, k: (z, 1 - x, 1 - y, k))
    mine = jnp.concatenate([half, beside, above, corner], axis=0)
    mine, rest = lax.optimization_barrier((mine, rest))
    over_rest = send(rest, lambda z, x, y, k: (z, x, 1, k) if y == 0 else None)
    other = send(mine, lambda z, x, y, k: (z, x, y, 1 - k))
    state = corner_start(jnp.stack([core, x, y]).astype(jnp.int32), mine, other)

    state, far, over_rest = lax.optimization_barrier((state, far, over_rest))
    over = jnp.concatenate([over_first, over_rest], axis=0)
    rows_mine = jnp.where(y == 0, to_far, over)
    first = jnp.where(z == 0, even, jnp.where(y == 0, jnp.where(z == 2, to_far, far), jnp.where(z == 2, far, over)))
    to_near = jnp.where(y == 0, jnp.where(z == 3, far, to_far), jnp.where(z == 0, odd, over))
    split = to_near.shape[0] // 2
    to_near = [to_near[:split], to_near[split:]]
    state, first, to_near = lax.optimization_barrier((state, first, to_near))
    near = [send(to_near[0], near_stage), send(to_near[1], near_stage)]
    first = [first, send(first, same_core(0)), send(first, cross_core(0))]
    rows_other = send(rows_mine, lambda z, x, y, k: (z, x, y, 1 - k))
    inverse = corner_end(state)

    last = []
    for part in range(2):
        inverse, near[part] = lax.optimization_barrier((inverse, near[part]))
        held = jnp.where(z == 0, odd[part * split : (part + 1) * split], near[part])
        inverse, held = lax.optimization_barrier((inverse, held))
        last.append([held, send(held, same_core(1)), send(held, cross_core(1))])
        if part == 0:
            place = jnp.stack([row, col, core]).astype(jnp.int32)
            high, low, solved = row_weights(place, rows_mine, rows_other, inverse, row_tiles, tile)

    first_odd = jnp.where(y == 0, (z == 1) | (z == 2), z == 3).astype(jnp.int32)
    chosen = []
    for stage in range(2):
        rowwise = (z == 0) | ((y == 1) & (z == 2 - stage))
        own = core == x
        for panel in range(2):
            by_row = jnp.where(x == panel, 0, 1)
            by_col = jnp.where(own, jnp.where(core == panel, 0, 1), jnp.where(core == panel, 1, 2))
            chosen.append(jnp.where(rowwise, by_row, by_col))
    place = jnp.stack([row, col, jnp.where(z == 0, 0, first_odd)] + chosen).astype(jnp.int32)
    result = solved
    for part in range(2):
        result = trailing(
            part, place, block, (high, low), result, (first, last[part]), (part * split, 0), row_tiles, col_tiles, tile
        )
    return result.reshape(kernel_tiles.shape)


def from_root(value, axis, root):
    mine = lax.axis_index(axis) == root
    return lax.psum(jnp.where(mine, value, jnp.zeros_like(value)), axis)


def shards_any(kernel_tiles):
    row_tiles, _, tile, col_tiles, _, _ = kernel_tiles.shape
    row = lax.axis_index("prow")
    col = lax.axis_index("pcol")
    per = tile // LANES
    block = kernel_tiles.reshape(row_tiles * tile * col_tiles * per, LANES)
    zero = jnp.zeros((), jnp.int32)
    lead = gather_lead(block, row_tiles, col_tiles, tile)
    _, across, even, odd = gather_pieces(zero.reshape(1), lead, block, row_tiles, col_tiles, tile)
    rows = [from_root(across, "pcol", panel) for panel in range(2)]
    middle = tile * per // 2
    tile_rows = []
    for panel in range(2):
        tiles = [from_root(from_root(lead, "pcol", panel), "prow", p) for p in range(2)]
        tile_rows.append(jnp.concatenate([t[s : s + middle] for s in (0, middle) for t in tiles], axis=0))
    inverse = corner_end(corner_start(jnp.zeros((3,), jnp.int32), tile_rows[0], tile_rows[1]))
    pieces = []
    for part in (even, odd):
        panels = [from_root(part, "prow", p) for p in range(2)]
        pieces.append(panels + [panels[0]])
    place = jnp.stack([row, col, zero, zero, zero + 1, zero, zero + 1]).astype(jnp.int32)
    high, low, result = row_weights(place, rows[0], rows[1], inverse, row_tiles, tile)
    split = even.shape[0] // 2
    for part in range(2):
        result = trailing(
            part, place, block, (high, low), result, pieces, (part * split,) * 2, row_tiles, col_tiles, tile
        )
    return result.reshape(kernel_tiles.shape)


def solution(mesh):
    in_specs = (P(None, "prow", None, None, "pcol", None),)
    out_specs = P(None, "prow", None, None, "pcol", None)
    body = shards if (mesh.shape["prow"], mesh.shape["pcol"]) == (8, 4) else shards_any
    return jax.shard_map(body, mesh=mesh, in_specs=in_specs, out_specs=out_specs, check_vma=False)
```

```python
import functools

import jax
import jax.numpy as jnp
from jax import lax
from jax.experimental import pallas as pl
from jax.experimental.pallas import tpu as pltpu
from jax.sharding import PartitionSpec as P

HI = lax.Precision.HIGHEST
F32 = jnp.float32
BF16 = jnp.bfloat16
LANES = 128
VMEM_BYTES = 56 * 1024 * 1024


def splat(x, shape):
    return jnp.broadcast_to(x, shape)


def reciprocal(x):
    r = pl.reciprocal(x, approx=True)
    for _ in range(2):
        r = r * (2.0 - x * r)
    return r


def inverse_factor_128(block):
    size = 128
    step = 8
    count = size // step
    lane = lax.broadcasted_iota(jnp.int32, (step, size), 1)
    sub = lax.broadcasted_iota(jnp.int32, (step, size), 0)
    rows = [block[step * i : step * (i + 1), :] for i in range(count)]
    shape = (step, size)
    for j in range(count):
        base = step * j
        cols = [splat(rows[j][:, base + t : base + t + 1], shape) for t in range(step)]
        a = {}
        for t in range(step):
            for s in range(t, step):
                a[s, t] = splat(cols[t][s : s + 1, :], shape)
        in_block = (lane >= base) & (lane < base + step)
        unit = jnp.where(lane - base == sub, F32(1.0), F32(0.0))
        own = jnp.where(in_block, unit, rows[j])
        if j + 1 < count:
            below = [splat(rows[j + 1][:, base + t : base + t + 1], shape) for t in range(step)]
            near = jnp.where(in_block, F32(0.0), rows[j + 1])
        m = {}
        u = []
        w = []
        done = jnp.zeros(shape, F32)
        for t in range(0, step, 2):
            p, b, c = a[t, t], a[t + 1, t], a[t + 1, t + 1]
            det = p * c - b * b
            inv = reciprocal(det)
            for s in range(t + 2, step):
                m[s, t] = (c * a[s, t] - b * a[s, t + 1]) * inv
                m[s, t + 1] = (p * a[s, t + 1] - b * a[s, t]) * inv
            for v in range(t + 2, step):
                for s in range(v, step):
                    a[s, v] = a[s, v] - (m[s, t] * a[v, t] + m[s, t + 1] * a[v, t + 1])
            for k in (t, t + 1):
                row = splat(own[k : k + 1, :], shape)
                for s in range(t):
                    row = row - m[k, s] * u[s]
                u.append(row)
            w.append((c * u[t] - b * u[t + 1]) * inv)
            w.append((p * u[t + 1] - b * u[t]) * inv)
            root = lax.rsqrt(p)
            over = root * root
            done = jnp.where(sub == t, u[t] * root, done)
            done = jnp.where(sub == t + 1, (u[t + 1] - (b * over) * u[t]) * lax.rsqrt(det * over), done)
            if j + 1 < count:
                for k in (t, t + 1):
                    for s in range(t):
                        below[k] = below[k] - m[k, s] * below[s]
                near = near - (below[t] * w[t] + below[t + 1] * w[t + 1])
        if j + 1 < count:
            rows[j + 1] = near
        g = [None] * step
        for t in reversed(range(0, step, 2)):
            for k in (t + 1, t):
                row = w[k]
                for s in reversed(range(t + 2, step)):
                    row = row - m[s, k] * g[s]
                g[k] = row
        for i in range(j + 2, count):
            acc = jnp.where(in_block, F32(0.0), rows[i])
            for t in reversed(range(step)):
                acc = acc - splat(rows[i][:, base + t : base + t + 1], shape) * g[t]
            rows[i] = acc
        rows[j] = jnp.where(lane < base + step, done, F32(0.0))
    return jnp.concatenate(rows, axis=0)


def eliminate(state, first, last):
    rows = state.shape[0]
    for o in range(first, last):
        lo, hi = o * LANES, (o + 1) * LANES
        diag = inverse_factor_128(state[lo:hi, lo:hi])
        upper = jnp.dot(diag, state[lo:hi, :], precision=HI, preferred_element_type=F32)
        parts = ([upper[:, :lo]] if lo else []) + [diag] + ([upper[:, hi:]] if hi < rows else [])
        wide = jnp.concatenate(parts, axis=1)
        if hi < rows:
            state[hi:, lo:hi] = jnp.zeros((rows - hi, LANES), F32)
            state[hi:, :] -= lax.dot_general(
                upper[:, hi:], wide, (((0,), (0,)), ((), ())), precision=HI, preferred_element_type=F32
            )
            state[lo:hi, hi:] = jnp.zeros((LANES, rows - hi), F32)
        state[lo:hi, :hi] = wide[:, :hi]


def corner_start_kernel(place_ref, mine_ref, other_ref, state):
    core, side, across = place_ref[0], place_ref[1], place_ref[2]
    rows = state.shape[0]
    tile = rows // 2
    half = tile // 2
    per = tile // LANES
    for which, ref in ((core, mine_ref), (1 - core, other_ref)):
        for part in range(4):
            at_side = side if part % 2 == 0 else 1 - side
            at_half = across if part < 2 else 1 - across
            at = pl.multiple_of(which * tile + at_half * half, half)
            for target in range(2):

                @pl.when(at_side == target)
                def _(ref=ref, part=part, at=at, target=target):
                    for h in range(per):
                        start = target * tile + h * LANES
                        state[pl.ds(at, half), start : start + LANES] = ref[
                            pl.ds(part * half * per + h, half, stride=per), :
                        ]

    eliminate(state, 0, tile // LANES)


def corner_end_kernel(state_ref, inverse_ref):
    rows = state_ref.shape[0]
    inverse_ref[...] = state_ref[...]
    eliminate(inverse_ref, rows // 2 // LANES, rows // LANES)


COST = pl.CostEstimate(flops=1000, bytes_accessed=1000, transcendentals=0)


def corner_start(place, mine, other):
    width = mine.shape[0] // 2
    vmem = pl.BlockSpec(memory_space=pltpu.VMEM)
    return pl.pallas_call(
        corner_start_kernel,
        out_shape=jax.ShapeDtypeStruct((width, width), F32),
        in_specs=[pl.BlockSpec(memory_space=pltpu.SMEM), vmem, vmem],
        out_specs=vmem,
        compiler_params=pltpu.CompilerParams(vmem_limit_bytes=16 * 1024 * 1024),
        cost_estimate=COST,
        name="corner_start",
    )(place, mine, other)


def corner_end(state):
    vmem = pl.BlockSpec(memory_space=pltpu.VMEM)
    return pl.pallas_call(
        corner_end_kernel,
        out_shape=jax.ShapeDtypeStruct(state.shape, F32),
        in_specs=[vmem],
        out_specs=vmem,
        compiler_params=pltpu.CompilerParams(vmem_limit_bytes=16 * 1024 * 1024),
        cost_estimate=COST,
        name="corner_end",
    )(state)


def transposed_tile(block_ref, tile, stride):
    per = tile // LANES
    return jnp.concatenate([block_ref[pl.ds(h, tile, stride=stride), :] for h in range(per)], axis=1).T


def store_tile(ref, start, value, tile):
    per = tile // LANES
    for h in range(per):
        ref[pl.ds(start + h, tile, stride=per), :] = value[:, h * LANES : (h + 1) * LANES]


def lead_kernel(tile, block_ref, out_ref):
    store_tile(out_ref, 0, transposed_tile(block_ref.reshape(tile * GROUP, LANES), tile, GROUP), tile)


def gather_kernel(tile, col_tiles, row_tiles, place_ref, lead_ref, block_ref, top_ref, rest_ref, far_ref, even_ref,
                  odd_ref):
    step = pl.program_id(0)
    per = tile // LANES
    size = tile * per
    value = transposed_tile(block_ref.reshape(tile * GROUP, LANES), tile, GROUP)
    store_tile(rest_ref, 0, value, tile)

    @pl.when(place_ref[0] == 0)
    def _():
        store_tile(far_ref, pl.multiple_of((step + 1) * size, size), value, tile)

    @pl.when(step == 0)
    def _():
        for parity, ref in enumerate((even_ref, odd_ref)):
            for i in range(col_tiles // 2):
                for h in range(per):
                    ref[pl.ds(i * size + h, tile, stride=per), :] = top_ref[
                        pl.ds((2 * i + parity) * per + h, tile, stride=col_tiles * per), :
                    ]

        @pl.when(place_ref[0] == 0)
        def _():
            far_ref[:size, :] = lead_ref[...]

        @pl.when(place_ref[0] != 0)
        def _():
            far_ref[...] = even_ref[...]


GROUP = 8


def grouped(block, row_tiles, col_tiles, tile):
    return block.reshape(row_tiles * tile, col_tiles * tile // LANES // GROUP, GROUP, LANES)


def gather_lead(block, row_tiles, col_tiles, tile):
    return pl.pallas_call(
        functools.partial(lead_kernel, tile),
        grid=(1,),
        out_shape=jax.ShapeDtypeStruct((tile * tile // LANES, LANES), F32),
        in_specs=[pl.BlockSpec((tile, None, GROUP, LANES), lambda a: (0, 0, 0, 0))],
        out_specs=pl.BlockSpec((tile * tile // LANES, LANES), lambda a: (0, 0)),
        compiler_params=pltpu.CompilerParams(vmem_limit_bytes=VMEM_BYTES),
        cost_estimate=COST,
        name="gather_lead",
    )(grouped(block, row_tiles, col_tiles, tile))


def gather_pieces(place, lead, block, row_tiles, col_tiles, tile):
    per = tile // LANES
    size = tile * per
    top = (tile * col_tiles * per, LANES)
    whole = [size * row_tiles] + [size * (col_tiles // 2)] * 2
    return pl.pallas_call(
        functools.partial(gather_kernel, tile, col_tiles, row_tiles),
        grid=(row_tiles - 1,),
        out_shape=[jax.ShapeDtypeStruct((s, LANES), F32) for s in [size * (row_tiles - 1)] + whole],
        in_specs=[
            pl.BlockSpec(memory_space=pltpu.SMEM),
            pl.BlockSpec((size, LANES), lambda a: (0, 0)),
            pl.BlockSpec((tile, None, GROUP, LANES), lambda a: (a + 1, 0, 0, 0)),
            pl.BlockSpec(top, lambda a: (0, 0)),
        ],
        out_specs=[pl.BlockSpec((size, LANES), lambda a: (a, 0))]
        + [pl.BlockSpec((s, LANES), lambda a: (0, 0)) for s in whole],
        compiler_params=pltpu.CompilerParams(vmem_limit_bytes=VMEM_BYTES),
        cost_estimate=COST,
        name="gather_pieces",
    )(place, lead, grouped(block, row_tiles, col_tiles, tile), block)


def halves(x):
    high = x.astype(BF16)
    return high, (x - high.astype(F32)).astype(BF16)


def left_factor(x):
    high, low = halves(x)
    return jnp.concatenate([high, low, high], axis=1)


def right_factor(x, axis):
    high, low = halves(x)
    return jnp.concatenate([high, high, low], axis=axis)


def product(a, b, dims):
    return lax.dot_general(a, b, (dims, ((), ())), preferred_element_type=F32)


def weights_kernel(tile, place_ref, rows_mine, rows_other, inverse_ref, weights_ref, solved_ref, across, along):
    step = pl.program_id(0)
    row, col, core = place_ref[0], place_ref[1], place_ref[2]
    per = tile // LANES

    @pl.when(step == 0)
    def _():
        across[...] = right_factor(inverse_ref[...], 1)
        along[...] = right_factor(inverse_ref[...], 0)

    mine, other = [
        jnp.concatenate([r[pl.ds(h, tile, stride=per), :] for h in range(per)], axis=1)
        for r in (rows_mine, rows_other)
    ]
    lead = jnp.concatenate([jnp.where(core == 0, mine, other).T, jnp.where(core == 0, other, mine).T], axis=1)
    solved = product(left_factor(lead), across[...], ((1,), (1,)))
    weights_ref[...] = left_factor(product(left_factor(solved), along[...], ((1,), (0,))))

    @pl.when(col < 2)
    def _():
        mine = jnp.where(col == 0, solved[:, :tile], solved[:, tile:])
        r = lax.broadcasted_iota(jnp.int32, (tile, tile), 0)
        s = lax.broadcasted_iota(jnp.int32, (tile, tile), 1)
        top = (step == 0) & (row < 2)
        on_diag = top & (row == col)
        above = top & (row < col)
        keep = jnp.where(on_diag, s - r, jnp.where(above, 1, 0)) <= 0
        solved_ref[...] = jnp.where(keep, mine, F32(0.0))


def row_weights(place, rows_mine, rows_other, inverse, row_tiles, tile):
    depth = inverse.shape[0]
    rows_spec = pl.BlockSpec((tile * tile // LANES, LANES), lambda a: (a, 0))
    total = row_tiles * tile
    return pl.pallas_call(
        functools.partial(weights_kernel, tile),
        grid=(row_tiles,),
        out_shape=[jax.ShapeDtypeStruct((total, 3 * depth), BF16), jax.ShapeDtypeStruct((total, tile), F32)],
        in_specs=[
            pl.BlockSpec(memory_space=pltpu.SMEM),
            rows_spec,
            rows_spec,
            pl.BlockSpec((depth, depth), lambda a: (0, 0)),
        ],
        out_specs=[pl.BlockSpec((tile, 3 * depth), lambda a: (a, 0)), pl.BlockSpec((tile, tile), lambda a: (a, 0))],
        scratch_shapes=[pltpu.VMEM((depth, 3 * depth), BF16), pltpu.VMEM((3 * depth, depth), BF16)],
        compiler_params=pltpu.CompilerParams(vmem_limit_bytes=32 * 1024 * 1024),
        cost_estimate=COST,
        name="row_weights",
    )(place, rows_mine, rows_other, inverse)


def load_columns(place_ref, pieces, offsets, columns, tile, count):
    per = tile // LANES
    depth = 2 * tile
    for stage in range(2):
        for panel in range(2):
            for which, ref in enumerate(pieces[stage]):

                @pl.when(place_ref[3 + 2 * stage + panel] == which)
                def _(stage=stage, panel=panel, ref=ref):
                    for i in range(count):
                        for h in range(per):
                            start = offsets[stage] + i * tile * per + h
                            high, low = halves(ref[pl.ds(start, tile, stride=per), :])
                            at = ((stage * count + i) * per + h) * LANES
                            for copy, value in enumerate((high, high, low)):
                                row = copy * depth + panel * tile
                                columns[row : row + tile, at : at + LANES] = value


def trailing_kernel(tile, group, count, offsets, place_ref, block_ref, weights_ref, *rest):
    solved_ref = rest[0] if group == 0 else None
    pieces = (rest[1:4], rest[4:7])
    block_out, columns = rest[-2:]
    step = pl.program_id(0)
    row, col = place_ref[0], place_ref[1]
    per = tile // LANES
    top = (step == 0) & (row < 2)
    block = block_ref.reshape(tile * GROUP, LANES)
    out = block_out.reshape(tile * GROUP, LANES)

    @pl.when(step == 0)
    def _():
        load_columns(place_ref, pieces, offsets, columns, tile, count)

    @pl.when(top)
    def _():
        block_out[...] = jnp.zeros_like(block_out)

    @pl.when(jnp.logical_not(top))
    def _():
        for stage in range(2):
            parity = place_ref[2] if stage == 0 else 1 - place_ref[2]
            for i in range(count):
                at = (stage * count + i) * tile
                update = product(weights_ref[...], columns[:, at : at + tile], ((1,), (0,)))
                for h in range(per):
                    where = pl.ds((2 * i + parity) * per + h, tile, stride=GROUP)
                    out[where, :] = block[where, :] - update[:, h * LANES : (h + 1) * LANES]

    if group == 0:

        @pl.when(col < 2)
        def _():
            for h in range(per):
                out[pl.ds(h, tile, stride=GROUP), :] = solved_ref[:, h * LANES : (h + 1) * LANES]


def trailing(group, place, block, weights, extra, pieces, offsets, row_tiles, col_tiles, tile):
    per = tile // LANES
    depth = weights.shape[1]
    count = GROUP // per // 2
    view = grouped(block, row_tiles, col_tiles, tile)
    block_spec = pl.BlockSpec((tile, None, GROUP, LANES), lambda a: (a, group, 0, 0))
    weight_spec = pl.BlockSpec((tile, depth), lambda a: (a, 0))
    return pl.pallas_call(
        functools.partial(trailing_kernel, tile, group, count, offsets),
        grid=(row_tiles,),
        out_shape=jax.ShapeDtypeStruct(view.shape, F32),
        in_specs=[pl.BlockSpec(memory_space=pltpu.SMEM), block_spec, weight_spec]
        + [pl.BlockSpec((tile, tile), lambda a: (a, 0)) if group == 0 else pl.BlockSpec(memory_space=pl.ANY)]
        + [pl.BlockSpec(memory_space=pltpu.VMEM)] * 6,
        out_specs=block_spec,
        scratch_shapes=[pltpu.VMEM((depth, 2 * count * tile), BF16)],
        input_output_aliases={} if group == 0 else {3: 0},
        compiler_params=pltpu.CompilerParams(vmem_limit_bytes=32 * 1024 * 1024),
        cost_estimate=COST,
        name="trailing_%d" % group,
    )(place, view, weights, extra, *pieces[0], *pieces[1])


AXES = ("prow", "pcol")


def send(value, route):
    pairs = []
    for device in range(32):
        to = route(device // 8, device // 4 % 2, device // 2 % 2, device % 2)
        if to is not None:
            pairs.append((device, ((to[0] * 2 + to[1]) * 2 + to[2]) * 2 + to[3]))
    return lax.ppermute(value, AXES, pairs)


def far_stage(z, x, y, k):
    to = {(0, 0): 3, (2, 0): 1, (0, 1): 2}.get((z, y))
    return None if to is None else (to, x, y, k)


def near_stage(z, x, y, k):
    to = {(0, 0): 1, (2, 0): 3, (3, 0): 2, (0, 1): 1, (1, 1): 3, (3, 1): 2}.get((z, y))
    return None if to is None else (to, x, y, k)


def by_rows(stage, z, y):
    return z == 0 or (y == 1 and z == (2 if stage == 0 else 1))


def same_core(stage):
    def route(z, x, y, k):
        if by_rows(stage, z, y) or k == x:
            return (z, 1 - x, y, k)
        return (z, x, y, x)

    return route


def cross_core(stage):
    def route(z, x, y, k):
        if by_rows(stage, z, y) or k == x:
            return None
        return (z, 1 - x, y, x)

    return route


def shards(kernel_tiles):
    row_tiles, _, tile, col_tiles, _, _ = kernel_tiles.shape
    row = lax.axis_index("prow")
    col = lax.axis_index("pcol")
    z, x, y, core = row // 2, row % 2, col // 2, col % 2
    per = tile // LANES
    block = kernel_tiles.reshape(row_tiles * tile * col_tiles * per, LANES)

    lead = gather_lead(block, row_tiles, col_tiles, tile)
    middle = tile * per // 2
    over_first = send(lead, lambda z, x, y, k: (z, x, 1, k) if y == 0 else None)
    rest, to_far, even, odd = gather_pieces(y.reshape(1), lead, block, row_tiles, col_tiles, tile)
    over_first, rest, to_far = lax.optimization_barrier((over_first, rest, to_far))
    half = jnp.where(y == 0, lead[:middle], over_first[middle:])
    half = jnp.where(z == 2, send(half, lambda z, x, y, k: (2, x, y, k) if z == 0 else None), half)
    half = jnp.where(z % 2 == 1, send(half, lambda z, x, y, k: (z + 1, x, y, k) if z % 2 == 0 else None), half)
    half, to_far = lax.optimization_barrier((half, to_far))
    far = send(to_far, far_stage)
    beside = send(half, lambda z, x, y, k: (z, 1 - x, y, k))
    above = send(half, lambda z, x, y, k: (z, x, 1 - y, k))
    corner = send(half, lambda z, x, y, k: (z, 1 - x, 1 - y, k))
    corner, rest = lax.optimization_barrier((corner, rest))
    mine = jnp.concatenate([half, beside, above, corner], axis=0)
    over_rest = send(rest, lambda z, x, y, k: (z, x, 1, k) if y == 0 else None)
    other = send(mine, lambda z, x, y, k: (z, x, y, 1 - k))
    state = corner_start(jnp.stack([core, x, y]).astype(jnp.int32), mine, other)

    state, far, over_rest = lax.optimization_barrier((state, far, over_rest))
    over = jnp.concatenate([over_first, over_rest], axis=0)
    rows_mine = jnp.where(y == 0, to_far, over)
    first = jnp.where(z == 0, even, jnp.where(y == 0, jnp.where(z == 2, to_far, far), jnp.where(z == 2, far, over)))
    to_near = jnp.where(y == 0, jnp.where(z == 3, far, to_far), jnp.where(z == 0, odd, over))
    split = to_near.shape[0] // 2
    to_near = [to_near[:split], to_near[split:]]
    state, first, to_near = lax.optimization_barrier((state, first, to_near))
    near = [send(to_near[0], near_stage), send(to_near[1], near_stage)]
    first = [first, send(first, same_core(0)), send(first, cross_core(0))]
    rows_other = send(rows_mine, lambda z, x, y, k: (z, x, y, 1 - k))
    inverse = corner_end(state)

    last = []
    for part in range(2):
        held = jnp.where(z == 0, odd[part * split : (part + 1) * split], near[part])
        if part == 0:
            inverse, held = lax.optimization_barrier((inverse, held))
        last.append([held, send(held, same_core(1)), send(held, cross_core(1))])
        if part == 0:
            place = jnp.stack([row, col, core]).astype(jnp.int32)
            weights, solved = row_weights(place, rows_mine, rows_other, inverse, row_tiles, tile)
            weights, near[1] = lax.optimization_barrier((weights, near[1]))

    first_odd = jnp.where(y == 0, (z == 1) | (z == 2), z == 3).astype(jnp.int32)
    chosen = []
    for stage in range(2):
        rowwise = (z == 0) | ((y == 1) & (z == 2 - stage))
        own = core == x
        for panel in range(2):
            by_row = jnp.where(x == panel, 0, 1)
            by_col = jnp.where(own, jnp.where(core == panel, 0, 1), jnp.where(core == panel, 1, 2))
            chosen.append(jnp.where(rowwise, by_row, by_col))
    place = jnp.stack([row, col, jnp.where(z == 0, 0, first_odd)] + chosen).astype(jnp.int32)
    result = solved
    for part in range(2):
        result = trailing(
            part, place, block, weights, result, (first, last[part]), (part * split, 0), row_tiles, col_tiles, tile
        )
    return result.reshape(kernel_tiles.shape)


def from_root(value, axis, root):
    mine = lax.axis_index(axis) == root
    return lax.psum(jnp.where(mine, value, jnp.zeros_like(value)), axis)


def shards_any(kernel_tiles):
    row_tiles, _, tile, col_tiles, _, _ = kernel_tiles.shape
    row = lax.axis_index("prow")
    col = lax.axis_index("pcol")
    per = tile // LANES
    block = kernel_tiles.reshape(row_tiles * tile * col_tiles * per, LANES)
    zero = jnp.zeros((), jnp.int32)
    lead = gather_lead(block, row_tiles, col_tiles, tile)
    _, across, even, odd = gather_pieces(zero.reshape(1), lead, block, row_tiles, col_tiles, tile)
    rows = [from_root(across, "pcol", panel) for panel in range(2)]
    middle = tile * per // 2
    tile_rows = []
    for panel in range(2):
        tiles = [from_root(from_root(lead, "pcol", panel), "prow", p) for p in range(2)]
        tile_rows.append(jnp.concatenate([t[s : s + middle] for s in (0, middle) for t in tiles], axis=0))
    inverse = corner_end(corner_start(jnp.zeros((3,), jnp.int32), tile_rows[0], tile_rows[1]))
    pieces = []
    for part in (even, odd):
        panels = [from_root(part, "prow", p) for p in range(2)]
        pieces.append(panels + [panels[0]])
    place = jnp.stack([row, col, zero, zero, zero + 1, zero, zero + 1]).astype(jnp.int32)
    weights, result = row_weights(place, rows[0], rows[1], inverse, row_tiles, tile)
    split = even.shape[0] // 2
    for part in range(2):
        result = trailing(
            part, place, block, weights, result, pieces, (part * split,) * 2, row_tiles, col_tiles, tile
        )
    return result.reshape(kernel_tiles.shape)


def solution(mesh):
    in_specs = (P(None, "prow", None, None, "pcol", None),)
    out_specs = P(None, "prow", None, None, "pcol", None)
    body = shards if (mesh.shape["prow"], mesh.shape["pcol"]) == (8, 4) else shards_any
    return jax.shard_map(body, mesh=mesh, in_specs=in_specs, out_specs=out_specs, check_vma=False)
```

```python
import functools

import jax
import jax.numpy as jnp
from jax import lax
from jax.experimental import pallas as pl
from jax.experimental.pallas import tpu as pltpu
from jax.sharding import PartitionSpec as P

HI = lax.Precision.HIGHEST
F32 = jnp.float32
BF16 = jnp.bfloat16
LANES = 128
VMEM_BYTES = 56 * 1024 * 1024


def splat(x, shape):
    return jnp.broadcast_to(x, shape)


def reciprocal(x):
    r = pl.reciprocal(x, approx=True)
    for _ in range(2):
        r = r * (2.0 - x * r)
    return r


def inverse_factor_128(block):
    size = 128
    step = 8
    count = size // step
    lane = lax.broadcasted_iota(jnp.int32, (step, size), 1)
    sub = lax.broadcasted_iota(jnp.int32, (step, size), 0)
    rows = [block[step * i : step * (i + 1), :] for i in range(count)]
    shape = (step, size)
    for j in range(count):
        base = step * j
        cols = [splat(rows[j][:, base + t : base + t + 1], shape) for t in range(step)]
        a = {}
        for t in range(step):
            for s in range(t, step):
                a[s, t] = splat(cols[t][s : s + 1, :], shape)
        in_block = (lane >= base) & (lane < base + step)
        unit = jnp.where(lane - base == sub, F32(1.0), F32(0.0))
        own = jnp.where(in_block, unit, rows[j])
        if j + 1 < count:
            below = [splat(rows[j + 1][:, base + t : base + t + 1], shape) for t in range(step)]
            near = jnp.where(in_block, F32(0.0), rows[j + 1])
        m = {}
        u = []
        w = []
        done = jnp.zeros(shape, F32)
        for t in range(0, step, 2):
            p, b, c = a[t, t], a[t + 1, t], a[t + 1, t + 1]
            det = p * c - b * b
            inv = reciprocal(det)
            for s in range(t + 2, step):
                m[s, t] = (c * a[s, t] - b * a[s, t + 1]) * inv
                m[s, t + 1] = (p * a[s, t + 1] - b * a[s, t]) * inv
            for v in range(t + 2, step):
                for s in range(v, step):
                    a[s, v] = a[s, v] - (m[s, t] * a[v, t] + m[s, t + 1] * a[v, t + 1])
            for k in (t, t + 1):
                row = splat(own[k : k + 1, :], shape)
                for s in range(t):
                    row = row - m[k, s] * u[s]
                u.append(row)
            w.append((c * u[t] - b * u[t + 1]) * inv)
            w.append((p * u[t + 1] - b * u[t]) * inv)
            root = lax.rsqrt(p)
            over = root * root
            done = jnp.where(sub == t, u[t] * root, done)
            done = jnp.where(sub == t + 1, (u[t + 1] - (b * over) * u[t]) * lax.rsqrt(det * over), done)
            if j + 1 < count:
                for k in (t, t + 1):
                    for s in range(t):
                        below[k] = below[k] - m[k, s] * below[s]
                near = near - (below[t] * w[t] + below[t + 1] * w[t + 1])
        if j + 1 < count:
            rows[j + 1] = near
        g = [None] * step
        for t in reversed(range(0, step, 2)):
            for k in (t + 1, t):
                row = w[k]
                for s in reversed(range(t + 2, step)):
                    row = row - m[s, k] * g[s]
                g[k] = row
        for i in range(j + 2, count):
            acc = jnp.where(in_block, F32(0.0), rows[i])
            for t in reversed(range(step)):
                acc = acc - splat(rows[i][:, base + t : base + t + 1], shape) * g[t]
            rows[i] = acc
        rows[j] = jnp.where(lane < base + step, done, F32(0.0))
    return jnp.concatenate(rows, axis=0)


def eliminate(state, first, last):
    rows = state.shape[0]
    for o in range(first, last):
        lo, hi = o * LANES, (o + 1) * LANES
        diag = inverse_factor_128(state[lo:hi, lo:hi])
        upper = jnp.dot(diag, state[lo:hi, :], precision=HI, preferred_element_type=F32)
        parts = ([upper[:, :lo]] if lo else []) + [diag] + ([upper[:, hi:]] if hi < rows else [])
        wide = jnp.concatenate(parts, axis=1)
        if hi < rows:
            state[hi:, lo:hi] = jnp.zeros((rows - hi, LANES), F32)
            state[hi:, :] -= lax.dot_general(
                upper[:, hi:], wide, (((0,), (0,)), ((), ())), precision=HI, preferred_element_type=F32
            )
            state[lo:hi, hi:] = jnp.zeros((LANES, rows - hi), F32)
        state[lo:hi, :hi] = wide[:, :hi]


def corner_start_kernel(place_ref, mine_ref, other_ref, state):
    core, side, across = place_ref[0], place_ref[1], place_ref[2]
    rows = state.shape[0]
    tile = rows // 2
    half = tile // 2
    per = tile // LANES
    for which, ref in ((core, mine_ref), (1 - core, other_ref)):
        for part in range(4):
            at_side = side if part % 2 == 0 else 1 - side
            at_half = across if part < 2 else 1 - across
            at = pl.multiple_of(which * tile + at_half * half, half)
            for target in range(2):

                @pl.when(at_side == target)
                def _(ref=ref, part=part, at=at, target=target):
                    for h in range(per):
                        start = target * tile + h * LANES
                        state[pl.ds(at, half), start : start + LANES] = ref[
                            pl.ds(part * half * per + h, half, stride=per), :
                        ]

    eliminate(state, 0, tile // LANES)


def corner_end_kernel(state_ref, inverse_ref):
    rows = state_ref.shape[0]
    inverse_ref[...] = state_ref[...]
    eliminate(inverse_ref, rows // 2 // LANES, rows // LANES)


COST = pl.CostEstimate(flops=1000, bytes_accessed=1000, transcendentals=0)


def corner_start(place, mine, other):
    width = mine.shape[0] // 2
    vmem = pl.BlockSpec(memory_space=pltpu.VMEM)
    return pl.pallas_call(
        corner_start_kernel,
        out_shape=jax.ShapeDtypeStruct((width, width), F32),
        in_specs=[pl.BlockSpec(memory_space=pltpu.SMEM), vmem, vmem],
        out_specs=vmem,
        compiler_params=pltpu.CompilerParams(vmem_limit_bytes=16 * 1024 * 1024),
        cost_estimate=COST,
        name="corner_start",
    )(place, mine, other)


def corner_end(state):
    vmem = pl.BlockSpec(memory_space=pltpu.VMEM)
    return pl.pallas_call(
        corner_end_kernel,
        out_shape=jax.ShapeDtypeStruct(state.shape, F32),
        in_specs=[vmem],
        out_specs=vmem,
        compiler_params=pltpu.CompilerParams(vmem_limit_bytes=16 * 1024 * 1024),
        cost_estimate=COST,
        name="corner_end",
    )(state)


def transposed_tile(block_ref, tile, stride):
    per = tile // LANES
    return jnp.concatenate([block_ref[pl.ds(h, tile, stride=stride), :] for h in range(per)], axis=1).T


def store_tile(ref, start, value, tile):
    per = tile // LANES
    for h in range(per):
        ref[pl.ds(start + h, tile, stride=per), :] = value[:, h * LANES : (h + 1) * LANES]


def lead_kernel(tile, block_ref, out_ref):
    store_tile(out_ref, 0, transposed_tile(block_ref.reshape(tile * GROUP, LANES), tile, GROUP), tile)


def gather_kernel(tile, col_tiles, row_tiles, place_ref, lead_ref, block_ref, top_ref, rest_ref, far_ref, even_ref,
                  odd_ref):
    step = pl.program_id(0)
    per = tile // LANES
    size = tile * per
    value = transposed_tile(block_ref.reshape(tile * GROUP, LANES), tile, GROUP)
    store_tile(rest_ref, 0, value, tile)

    @pl.when(place_ref[0] == 0)
    def _():
        store_tile(far_ref, pl.multiple_of((step + 1) * size, size), value, tile)

    @pl.when(step == 0)
    def _():
        for parity, ref in enumerate((even_ref, odd_ref)):
            for i in range(col_tiles // 2):
                for h in range(per):
                    ref[pl.ds(i * size + h, tile, stride=per), :] = top_ref[
                        pl.ds((2 * i + parity) * per + h, tile, stride=col_tiles * per), :
                    ]

        @pl.when(place_ref[0] == 0)
        def _():
            far_ref[:size, :] = lead_ref[...]

        @pl.when(place_ref[0] != 0)
        def _():
            far_ref[...] = even_ref[...]


GROUP = 8


def grouped(block, row_tiles, col_tiles, tile):
    return block.reshape(row_tiles * tile, col_tiles * tile // LANES // GROUP, GROUP, LANES)


def gather_lead(block, row_tiles, col_tiles, tile):
    return pl.pallas_call(
        functools.partial(lead_kernel, tile),
        grid=(1,),
        out_shape=jax.ShapeDtypeStruct((tile * tile // LANES, LANES), F32),
        in_specs=[pl.BlockSpec((tile, None, GROUP, LANES), lambda a: (0, 0, 0, 0))],
        out_specs=pl.BlockSpec((tile * tile // LANES, LANES), lambda a: (0, 0)),
        compiler_params=pltpu.CompilerParams(vmem_limit_bytes=VMEM_BYTES),
        cost_estimate=COST,
        name="gather_lead",
    )(grouped(block, row_tiles, col_tiles, tile))


def gather_pieces(place, lead, block, row_tiles, col_tiles, tile):
    per = tile // LANES
    size = tile * per
    top = (tile * col_tiles * per, LANES)
    whole = [size * row_tiles] + [size * (col_tiles // 2)] * 2
    return pl.pallas_call(
        functools.partial(gather_kernel, tile, col_tiles, row_tiles),
        grid=(row_tiles - 1,),
        out_shape=[jax.ShapeDtypeStruct((s, LANES), F32) for s in [size * (row_tiles - 1)] + whole],
        in_specs=[
            pl.BlockSpec(memory_space=pltpu.SMEM),
            pl.BlockSpec((size, LANES), lambda a: (0, 0)),
            pl.BlockSpec((tile, None, GROUP, LANES), lambda a: (a + 1, 0, 0, 0)),
            pl.BlockSpec(top, lambda a: (0, 0)),
        ],
        out_specs=[pl.BlockSpec((size, LANES), lambda a: (a, 0))]
        + [pl.BlockSpec((s, LANES), lambda a: (0, 0)) for s in whole],
        compiler_params=pltpu.CompilerParams(vmem_limit_bytes=VMEM_BYTES),
        cost_estimate=COST,
        name="gather_pieces",
    )(place, lead, grouped(block, row_tiles, col_tiles, tile), block)


def halves(x):
    high = x.astype(BF16)
    return high, (x - high.astype(F32)).astype(BF16)


def left_factor(x):
    high, low = halves(x)
    return jnp.concatenate([high, low, high], axis=1)


def right_factor(x, axis):
    high, low = halves(x)
    return jnp.concatenate([high, high, low], axis=axis)


def product(a, b, dims):
    return lax.dot_general(a, b, (dims, ((), ())), preferred_element_type=F32)


def weights_kernel(tile, place_ref, rows_mine, rows_other, inverse_ref, weights_ref, solved_ref, across, along):
    step = pl.program_id(0)
    row, col, core = place_ref[0], place_ref[1], place_ref[2]
    per = tile // LANES

    @pl.when(step == 0)
    def _():
        across[...] = right_factor(inverse_ref[...], 1)
        along[...] = right_factor(inverse_ref[...], 0)

    mine, other = [
        jnp.concatenate([r[pl.ds(h, tile, stride=per), :] for h in range(per)], axis=1)
        for r in (rows_mine, rows_other)
    ]
    lead = jnp.concatenate([jnp.where(core == 0, mine, other).T, jnp.where(core == 0, other, mine).T], axis=1)
    solved = product(left_factor(lead), across[...], ((1,), (1,)))
    weights_ref[...] = left_factor(product(left_factor(solved), along[...], ((1,), (0,))))

    @pl.when(col < 2)
    def _():
        mine = jnp.where(col == 0, solved[:, :tile], solved[:, tile:])
        r = lax.broadcasted_iota(jnp.int32, (tile, tile), 0)
        s = lax.broadcasted_iota(jnp.int32, (tile, tile), 1)
        top = (step == 0) & (row < 2)
        on_diag = top & (row == col)
        above = top & (row < col)
        keep = jnp.where(on_diag, s - r, jnp.where(above, 1, 0)) <= 0
        solved_ref[...] = jnp.where(keep, mine, F32(0.0))


def row_weights(place, rows_mine, rows_other, inverse, row_tiles, tile):
    depth = inverse.shape[0]
    rows_spec = pl.BlockSpec((tile * tile // LANES, LANES), lambda a: (a, 0))
    total = row_tiles * tile
    return pl.pallas_call(
        functools.partial(weights_kernel, tile),
        grid=(row_tiles,),
        out_shape=[jax.ShapeDtypeStruct((total, 3 * depth), BF16), jax.ShapeDtypeStruct((total, tile), F32)],
        in_specs=[
            pl.BlockSpec(memory_space=pltpu.SMEM),
            rows_spec,
            rows_spec,
            pl.BlockSpec((depth, depth), lambda a: (0, 0)),
        ],
        out_specs=[pl.BlockSpec((tile, 3 * depth), lambda a: (a, 0)), pl.BlockSpec((tile, tile), lambda a: (a, 0))],
        scratch_shapes=[pltpu.VMEM((depth, 3 * depth), BF16), pltpu.VMEM((3 * depth, depth), BF16)],
        compiler_params=pltpu.CompilerParams(vmem_limit_bytes=18 * 1024 * 1024),
        cost_estimate=COST,
        name="row_weights",
    )(place, rows_mine, rows_other, inverse)


def load_columns(place_ref, pieces, offsets, columns, tile, count):
    per = tile // LANES
    depth = 2 * tile
    for stage in range(2):
        for panel in range(2):
            for which, ref in enumerate(pieces[stage]):

                @pl.when(place_ref[3 + 2 * stage + panel] == which)
                def _(stage=stage, panel=panel, ref=ref):
                    for i in range(count):
                        for h in range(per):
                            start = offsets[stage] + i * tile * per + h
                            high, low = halves(ref[pl.ds(start, tile, stride=per), :])
                            at = ((stage * count + i) * per + h) * LANES
                            for copy, value in enumerate((high, high, low)):
                                row = copy * depth + panel * tile
                                columns[row : row + tile, at : at + LANES] = value


def trailing_kernel(tile, group, count, offsets, place_ref, block_ref, weights_ref, *rest):
    solved_ref = rest[0] if group == 0 else None
    pieces = (rest[1:4], rest[4:7])
    block_out, columns = rest[-2:]
    step = pl.program_id(0)
    row, col = place_ref[0], place_ref[1]
    per = tile // LANES
    top = (step == 0) & (row < 2)
    block = block_ref.reshape(tile * GROUP, LANES)
    out = block_out.reshape(tile * GROUP, LANES)

    @pl.when(step == 0)
    def _():
        load_columns(place_ref, pieces, offsets, columns, tile, count)

    @pl.when(top)
    def _():
        block_out[...] = jnp.zeros_like(block_out)

    @pl.when(jnp.logical_not(top))
    def _():
        for stage in range(2):
            parity = place_ref[2] if stage == 0 else 1 - place_ref[2]
            for i in range(count):
                at = (stage * count + i) * tile
                update = product(weights_ref[...], columns[:, at : at + tile], ((1,), (0,)))
                for h in range(per):
                    where = pl.ds((2 * i + parity) * per + h, tile, stride=GROUP)
                    out[where, :] = block[where, :] - update[:, h * LANES : (h + 1) * LANES]

    if group == 0:

        @pl.when(col < 2)
        def _():
            for h in range(per):
                out[pl.ds(h, tile, stride=GROUP), :] = solved_ref[:, h * LANES : (h + 1) * LANES]


def trailing(group, place, block, weights, extra, pieces, offsets, row_tiles, col_tiles, tile):
    per = tile // LANES
    depth = weights.shape[1]
    count = GROUP // per // 2
    view = grouped(block, row_tiles, col_tiles, tile)
    block_spec = pl.BlockSpec((tile, None, GROUP, LANES), lambda a: (a, group, 0, 0))
    weight_spec = pl.BlockSpec((tile, depth), lambda a: (a, 0))
    return pl.pallas_call(
        functools.partial(trailing_kernel, tile, group, count, offsets),
        grid=(row_tiles,),
        out_shape=jax.ShapeDtypeStruct(view.shape, F32),
        in_specs=[pl.BlockSpec(memory_space=pltpu.SMEM), block_spec, weight_spec]
        + [pl.BlockSpec((tile, tile), lambda a: (a, 0)) if group == 0 else pl.BlockSpec(memory_space=pl.ANY)]
        + [pl.BlockSpec(memory_space=pltpu.VMEM)] * 6,
        out_specs=block_spec,
        scratch_shapes=[pltpu.VMEM((depth, 2 * count * tile), BF16)],
        input_output_aliases={} if group == 0 else {3: 0},
        compiler_params=pltpu.CompilerParams(vmem_limit_bytes=18 * 1024 * 1024),
        cost_estimate=COST,
        name="trailing_%d" % group,
    )(place, view, weights, extra, *pieces[0], *pieces[1])


AXES = ("prow", "pcol")


def send(value, route):
    pairs = []
    for device in range(32):
        to = route(device // 8, device // 4 % 2, device // 2 % 2, device % 2)
        if to is not None:
            pairs.append((device, ((to[0] * 2 + to[1]) * 2 + to[2]) * 2 + to[3]))
    return lax.ppermute(value, AXES, pairs)


def far_stage(z, x, y, k):
    to = {(0, 0): 3, (2, 0): 1, (0, 1): 2}.get((z, y))
    return None if to is None else (to, x, y, k)


def near_stage(z, x, y, k):
    to = {(0, 0): 1, (2, 0): 3, (3, 0): 2, (0, 1): 1, (1, 1): 3, (3, 1): 2}.get((z, y))
    return None if to is None else (to, x, y, k)


def by_rows(stage, z, y):
    return z == 0 or (y == 1 and z == (2 if stage == 0 else 1))


def same_core(stage):
    def route(z, x, y, k):
        if by_rows(stage, z, y) or k == x:
            return (z, 1 - x, y, k)
        return (z, x, y, x)

    return route


def cross_core(stage):
    def route(z, x, y, k):
        if by_rows(stage, z, y) or k == x:
            return None
        return (z, 1 - x, y, x)

    return route


def shards(kernel_tiles):
    row_tiles, _, tile, col_tiles, _, _ = kernel_tiles.shape
    row = lax.axis_index("prow")
    col = lax.axis_index("pcol")
    z, x, y, core = row // 2, row % 2, col // 2, col % 2
    per = tile // LANES
    block = kernel_tiles.reshape(row_tiles * tile * col_tiles * per, LANES)

    lead = gather_lead(block, row_tiles, col_tiles, tile)
    middle = tile * per // 2
    over_first = send(lead, lambda z, x, y, k: (z, x, 1, k) if y == 0 else None)
    rest, to_far, even, odd = gather_pieces(y.reshape(1), lead, block, row_tiles, col_tiles, tile)
    over_first, rest, to_far = lax.optimization_barrier((over_first, rest, to_far))
    half = jnp.where(y == 0, lead[:middle], over_first[middle:])
    down = [send(half, lambda z, x, y, k, to=to: (to, x, y, k) if z == 0 else None) for to in (1, 2, 3)]
    size = lead.shape[0]
    first_down, to_far, middle_rest = lax.optimization_barrier((down[0], to_far, rest[:size]))
    far = send(to_far, far_stage)
    over_middle = send(middle_rest, lambda z, x, y, k: (z, x, 1, k) if y == 0 else None)
    half = jnp.where(z == 0, half, jnp.where(z == 1, first_down, jnp.where(z == 2, down[1], down[2])))
    half, over_middle = lax.optimization_barrier((half, over_middle))
    beside = send(half, lambda z, x, y, k: (z, 1 - x, y, k))
    above = send(half, lambda z, x, y, k: (z, x, 1 - y, k))
    corner = send(half, lambda z, x, y, k: (z, 1 - x, 1 - y, k))
    corner, last_rest = lax.optimization_barrier((corner, rest[size:]))
    mine = jnp.concatenate([half, beside, above, corner], axis=0)
    over_last = send(last_rest, lambda z, x, y, k: (z, x, 1, k) if y == 0 else None)
    other = send(mine, lambda z, x, y, k: (z, x, y, 1 - k))
    state = corner_start(jnp.stack([core, x, y]).astype(jnp.int32), mine, other)

    state, far, over_middle, over_last = lax.optimization_barrier((state, far, over_middle, over_last))
    over = jnp.concatenate([over_first, over_middle, over_last], axis=0)
    rows_mine = jnp.where(y == 0, to_far, over)
    first = jnp.where(z == 0, even, jnp.where(y == 0, jnp.where(z == 2, to_far, far), jnp.where(z == 2, far, over)))
    to_near = jnp.where(y == 0, jnp.where(z == 3, far, to_far), jnp.where(z == 0, odd, over))
    split = to_near.shape[0] // 2
    to_near = [to_near[:split], to_near[split:]]
    state, first, to_near = lax.optimization_barrier((state, first, to_near))
    near = [send(to_near[0], near_stage), send(to_near[1], near_stage)]
    first = [first, send(first, same_core(0)), send(first, cross_core(0))]
    rows_other = send(rows_mine, lambda z, x, y, k: (z, x, y, 1 - k))
    inverse = corner_end(state)

    last = []
    for part in range(2):
        held = jnp.where(z == 0, odd[part * split : (part + 1) * split], near[part])
        if part == 0:
            inverse, held = lax.optimization_barrier((inverse, held))
        last.append([held, send(held, same_core(1)), send(held, cross_core(1))])
        if part == 0:
            place = jnp.stack([row, col, core]).astype(jnp.int32)
            weights, solved = row_weights(place, rows_mine, rows_other, inverse, row_tiles, tile)
            weights, near[1] = lax.optimization_barrier((weights, near[1]))

    first_odd = jnp.where(y == 0, (z == 1) | (z == 2), z == 3).astype(jnp.int32)
    chosen = []
    for stage in range(2):
        rowwise = (z == 0) | ((y == 1) & (z == 2 - stage))
        own = core == x
        for panel in range(2):
            by_row = jnp.where(x == panel, 0, 1)
            by_col = jnp.where(own, jnp.where(core == panel, 0, 1), jnp.where(core == panel, 1, 2))
            chosen.append(jnp.where(rowwise, by_row, by_col))
    place = jnp.stack([row, col, jnp.where(z == 0, 0, first_odd)] + chosen).astype(jnp.int32)
    result = solved
    for part in range(2):
        result = trailing(
            part, place, block, weights, result, (first, last[part]), (part * split, 0), row_tiles, col_tiles, tile
        )
    return result.reshape(kernel_tiles.shape)


def from_root(value, axis, root):
    mine = lax.axis_index(axis) == root
    return lax.psum(jnp.where(mine, value, jnp.zeros_like(value)), axis)


def shards_any(kernel_tiles):
    row_tiles, _, tile, col_tiles, _, _ = kernel_tiles.shape
    row = lax.axis_index("prow")
    col = lax.axis_index("pcol")
    per = tile // LANES
    block = kernel_tiles.reshape(row_tiles * tile * col_tiles * per, LANES)
    zero = jnp.zeros((), jnp.int32)
    lead = gather_lead(block, row_tiles, col_tiles, tile)
    _, across, even, odd = gather_pieces(zero.reshape(1), lead, block, row_tiles, col_tiles, tile)
    rows = [from_root(across, "pcol", panel) for panel in range(2)]
    middle = tile * per // 2
    tile_rows = []
    for panel in range(2):
        tiles = [from_root(from_root(lead, "pcol", panel), "prow", p) for p in range(2)]
        tile_rows.append(jnp.concatenate([t[s : s + middle] for s in (0, middle) for t in tiles], axis=0))
    inverse = corner_end(corner_start(jnp.zeros((3,), jnp.int32), tile_rows[0], tile_rows[1]))
    pieces = []
    for part in (even, odd):
        panels = [from_root(part, "prow", p) for p in range(2)]
        pieces.append(panels + [panels[0]])
    place = jnp.stack([row, col, zero, zero, zero + 1, zero, zero + 1]).astype(jnp.int32)
    weights, result = row_weights(place, rows[0], rows[1], inverse, row_tiles, tile)
    split = even.shape[0] // 2
    for part in range(2):
        result = trailing(
            part, place, block, weights, result, pieces, (part * split,) * 2, row_tiles, col_tiles, tile
        )
    return result.reshape(kernel_tiles.shape)


def solution(mesh):
    in_specs = (P(None, "prow", None, None, "pcol", None),)
    out_specs = P(None, "prow", None, None, "pcol", None)
    body = shards if (mesh.shape["prow"], mesh.shape["pcol"]) == (8, 4) else shards_any
    return jax.shard_map(body, mesh=mesh, in_specs=in_specs, out_specs=out_specs, check_vma=False)
```

```python
import functools

import jax
import jax.numpy as jnp
from jax import lax
from jax.experimental import pallas as pl
from jax.experimental.pallas import tpu as pltpu
from jax.sharding import PartitionSpec as P

HI = lax.Precision.HIGHEST
F32 = jnp.float32
BF16 = jnp.bfloat16
LANES = 128
VMEM_BYTES = 56 * 1024 * 1024


def splat(x, shape):
    return jnp.broadcast_to(x, shape)


def reciprocal(x):
    r = pl.reciprocal(x, approx=True)
    for _ in range(2):
        r = r * (2.0 - x * r)
    return r


def inverse_factor_128(block):
    size = 128
    step = 8
    count = size // step
    lane = lax.broadcasted_iota(jnp.int32, (step, size), 1)
    sub = lax.broadcasted_iota(jnp.int32, (step, size), 0)
    rows = [block[step * i : step * (i + 1), :] for i in range(count)]
    shape = (step, size)
    for j in range(count):
        base = step * j
        cols = [splat(rows[j][:, base + t : base + t + 1], shape) for t in range(step)]
        a = {}
        for t in range(step):
            for s in range(t, step):
                a[s, t] = splat(cols[t][s : s + 1, :], shape)
        in_block = (lane >= base) & (lane < base + step)
        unit = jnp.where(lane - base == sub, F32(1.0), F32(0.0))
        own = jnp.where(in_block, unit, rows[j])
        if j + 1 < count:
            below = [splat(rows[j + 1][:, base + t : base + t + 1], shape) for t in range(step)]
            near = jnp.where(in_block, F32(0.0), rows[j + 1])
        m = {}
        u = []
        w = []
        done = jnp.zeros(shape, F32)
        for t in range(0, step, 2):
            p, b, c = a[t, t], a[t + 1, t], a[t + 1, t + 1]
            det = p * c - b * b
            inv = reciprocal(det)
            for s in range(t + 2, step):
                m[s, t] = (c * a[s, t] - b * a[s, t + 1]) * inv
                m[s, t + 1] = (p * a[s, t + 1] - b * a[s, t]) * inv
            for v in range(t + 2, step):
                for s in range(v, step):
                    a[s, v] = a[s, v] - (m[s, t] * a[v, t] + m[s, t + 1] * a[v, t + 1])
            for k in (t, t + 1):
                row = splat(own[k : k + 1, :], shape)
                for s in range(t):
                    row = row - m[k, s] * u[s]
                u.append(row)
            w.append((c * u[t] - b * u[t + 1]) * inv)
            w.append((p * u[t + 1] - b * u[t]) * inv)
            root = lax.rsqrt(p)
            over = root * root
            done = jnp.where(sub == t, u[t] * root, done)
            done = jnp.where(sub == t + 1, (u[t + 1] - (b * over) * u[t]) * lax.rsqrt(det * over), done)
            if j + 1 < count:
                for k in (t, t + 1):
                    for s in range(t):
                        below[k] = below[k] - m[k, s] * below[s]
                near = near - (below[t] * w[t] + below[t + 1] * w[t + 1])
        if j + 1 < count:
            rows[j + 1] = near
        g = [None] * step
        for t in reversed(range(0, step, 2)):
            for k in (t + 1, t):
                row = w[k]
                for s in reversed(range(t + 2, step)):
                    row = row - m[s, k] * g[s]
                g[k] = row
        for i in range(j + 2, count):
            acc = jnp.where(in_block, F32(0.0), rows[i])
            for t in reversed(range(step)):
                acc = acc - splat(rows[i][:, base + t : base + t + 1], shape) * g[t]
            rows[i] = acc
        rows[j] = jnp.where(lane < base + step, done, F32(0.0))
    return jnp.concatenate(rows, axis=0)


def eliminate(state, first, last):
    rows = state.shape[0]
    for o in range(first, last):
        lo, hi = o * LANES, (o + 1) * LANES
        diag = inverse_factor_128(state[lo:hi, lo:hi])
        upper = jnp.dot(diag, state[lo:hi, :], precision=HI, preferred_element_type=F32)
        parts = ([upper[:, :lo]] if lo else []) + [diag] + ([upper[:, hi:]] if hi < rows else [])
        wide = jnp.concatenate(parts, axis=1)
        if hi < rows:
            state[hi:, lo:hi] = jnp.zeros((rows - hi, LANES), F32)
            state[hi:, :] -= lax.dot_general(
                upper[:, hi:], wide, (((0,), (0,)), ((), ())), precision=HI, preferred_element_type=F32
            )
            state[lo:hi, hi:] = jnp.zeros((LANES, rows - hi), F32)
        state[lo:hi, :hi] = wide[:, :hi]


def corner_start_kernel(place_ref, mine_ref, other_ref, state):
    core, side, across = place_ref[0], place_ref[1], place_ref[2]
    rows = state.shape[0]
    tile = rows // 2
    half = tile // 2
    per = tile // LANES
    for which, ref in ((core, mine_ref), (1 - core, other_ref)):
        for part in range(4):
            at_side = side if part % 2 == 0 else 1 - side
            at_half = across if part < 2 else 1 - across
            at = pl.multiple_of(which * tile + at_half * half, half)
            for target in range(2):

                @pl.when(at_side == target)
                def _(ref=ref, part=part, at=at, target=target):
                    for h in range(per):
                        start = target * tile + h * LANES
                        state[pl.ds(at, half), start : start + LANES] = ref[
                            pl.ds(part * half * per + h, half, stride=per), :
                        ]

    eliminate(state, 0, tile // LANES)


def corner_end_kernel(state_ref, inverse_ref):
    rows = state_ref.shape[0]
    inverse_ref[...] = state_ref[...]
    eliminate(inverse_ref, rows // 2 // LANES, rows // LANES)


COST = pl.CostEstimate(flops=1000, bytes_accessed=1000, transcendentals=0)


def corner_start(place, mine, other):
    width = mine.shape[0] // 2
    vmem = pl.BlockSpec(memory_space=pltpu.VMEM)
    return pl.pallas_call(
        corner_start_kernel,
        out_shape=jax.ShapeDtypeStruct((width, width), F32),
        in_specs=[pl.BlockSpec(memory_space=pltpu.SMEM), vmem, vmem],
        out_specs=vmem,
        compiler_params=pltpu.CompilerParams(vmem_limit_bytes=16 * 1024 * 1024),
        cost_estimate=COST,
        name="corner_start",
    )(place, mine, other)


def corner_end(state):
    vmem = pl.BlockSpec(memory_space=pltpu.VMEM)
    return pl.pallas_call(
        corner_end_kernel,
        out_shape=jax.ShapeDtypeStruct(state.shape, F32),
        in_specs=[vmem],
        out_specs=vmem,
        compiler_params=pltpu.CompilerParams(vmem_limit_bytes=16 * 1024 * 1024),
        cost_estimate=COST,
        name="corner_end",
    )(state)


def transposed_tile(block_ref, tile, stride):
    per = tile // LANES
    return jnp.concatenate([block_ref[pl.ds(h, tile, stride=stride), :] for h in range(per)], axis=1).T


def store_tile(ref, start, value, tile):
    per = tile // LANES
    for h in range(per):
        ref[pl.ds(start + h, tile, stride=per), :] = value[:, h * LANES : (h + 1) * LANES]


def lead_kernel(tile, block_ref, out_ref):
    store_tile(out_ref, 0, transposed_tile(block_ref.reshape(tile * GROUP, LANES), tile, GROUP), tile)


def gather_kernel(tile, col_tiles, row_tiles, place_ref, lead_ref, block_ref, top_ref, rest_ref, far_ref, even_ref,
                  odd_ref):
    step = pl.program_id(0)
    per = tile // LANES
    size = tile * per
    value = transposed_tile(block_ref.reshape(tile * GROUP, LANES), tile, GROUP)
    store_tile(rest_ref, 0, value, tile)

    @pl.when(place_ref[0] == 0)
    def _():
        store_tile(far_ref, pl.multiple_of((step + 1) * size, size), value, tile)

    @pl.when(step == 0)
    def _():
        for parity, ref in enumerate((even_ref, odd_ref)):
            for i in range(col_tiles // 2):
                for h in range(per):
                    ref[pl.ds(i * size + h, tile, stride=per), :] = top_ref[
                        pl.ds((2 * i + parity) * per + h, tile, stride=col_tiles * per), :
                    ]

        @pl.when(place_ref[0] == 0)
        def _():
            far_ref[:size, :] = lead_ref[...]

        @pl.when(place_ref[0] != 0)
        def _():
            far_ref[...] = even_ref[...]


GROUP = 8


def grouped(block, row_tiles, col_tiles, tile):
    return block.reshape(row_tiles * tile, col_tiles * tile // LANES // GROUP, GROUP, LANES)


def gather_lead(block, row_tiles, col_tiles, tile):
    return pl.pallas_call(
        functools.partial(lead_kernel, tile),
        grid=(1,),
        out_shape=jax.ShapeDtypeStruct((tile * tile // LANES, LANES), F32),
        in_specs=[pl.BlockSpec((tile, None, GROUP, LANES), lambda a: (0, 0, 0, 0))],
        out_specs=pl.BlockSpec((tile * tile // LANES, LANES), lambda a: (0, 0)),
        compiler_params=pltpu.CompilerParams(vmem_limit_bytes=VMEM_BYTES),
        cost_estimate=COST,
        name="gather_lead",
    )(grouped(block, row_tiles, col_tiles, tile))


def gather_pieces(place, lead, block, row_tiles, col_tiles, tile):
    per = tile // LANES
    size = tile * per
    top = (tile * col_tiles * per, LANES)
    whole = [size * row_tiles] + [size * (col_tiles // 2)] * 2
    return pl.pallas_call(
        functools.partial(gather_kernel, tile, col_tiles, row_tiles),
        grid=(row_tiles - 1,),
        out_shape=[jax.ShapeDtypeStruct((s, LANES), F32) for s in [size * (row_tiles - 1)] + whole],
        in_specs=[
            pl.BlockSpec(memory_space=pltpu.SMEM),
            pl.BlockSpec((size, LANES), lambda a: (0, 0)),
            pl.BlockSpec((tile, None, GROUP, LANES), lambda a: (a + 1, 0, 0, 0)),
            pl.BlockSpec(top, lambda a: (0, 0)),
        ],
        out_specs=[pl.BlockSpec((size, LANES), lambda a: (a, 0))]
        + [pl.BlockSpec((s, LANES), lambda a: (0, 0)) for s in whole],
        compiler_params=pltpu.CompilerParams(vmem_limit_bytes=VMEM_BYTES),
        cost_estimate=COST,
        name="gather_pieces",
    )(place, lead, grouped(block, row_tiles, col_tiles, tile), block)


def halves(x):
    high = x.astype(BF16)
    return high, (x - high.astype(F32)).astype(BF16)


def left_factor(x):
    high, low = halves(x)
    return jnp.concatenate([high, low, high], axis=1)


def right_factor(x, axis):
    high, low = halves(x)
    return jnp.concatenate([high, high, low], axis=axis)


def product(a, b, dims):
    return lax.dot_general(a, b, (dims, ((), ())), preferred_element_type=F32)


def weights_kernel(tile, place_ref, rows_mine, rows_other, inverse_ref, weights_ref, solved_ref, across, along):
    step = pl.program_id(0)
    row, col, core = place_ref[0], place_ref[1], place_ref[2]
    per = tile // LANES

    @pl.when(step == 0)
    def _():
        across[...] = right_factor(inverse_ref[...], 1)
        along[...] = right_factor(inverse_ref[...], 0)

    mine, other = [
        jnp.concatenate([r[pl.ds(h, tile, stride=per), :] for h in range(per)], axis=1)
        for r in (rows_mine, rows_other)
    ]
    lead = jnp.concatenate([jnp.where(core == 0, mine, other).T, jnp.where(core == 0, other, mine).T], axis=1)
    solved = product(left_factor(lead), across[...], ((1,), (1,)))
    weights_ref[...] = left_factor(product(left_factor(solved), along[...], ((1,), (0,))))

    @pl.when(col < 2)
    def _():
        mine = jnp.where(col == 0, solved[:, :tile], solved[:, tile:])
        r = lax.broadcasted_iota(jnp.int32, (tile, tile), 0)
        s = lax.broadcasted_iota(jnp.int32, (tile, tile), 1)
        top = (step == 0) & (row < 2)
        on_diag = top & (row == col)
        above = top & (row < col)
        keep = jnp.where(on_diag, s - r, jnp.where(above, 1, 0)) <= 0
        solved_ref[...] = jnp.where(keep, mine, F32(0.0))


def row_weights(place, rows_mine, rows_other, inverse, row_tiles, tile):
    depth = inverse.shape[0]
    rows_spec = pl.BlockSpec((tile * tile // LANES, LANES), lambda a: (a, 0))
    total = row_tiles * tile
    return pl.pallas_call(
        functools.partial(weights_kernel, tile),
        grid=(row_tiles,),
        out_shape=[jax.ShapeDtypeStruct((total, 3 * depth), BF16), jax.ShapeDtypeStruct((total, tile), F32)],
        in_specs=[
            pl.BlockSpec(memory_space=pltpu.SMEM),
            rows_spec,
            rows_spec,
            pl.BlockSpec((depth, depth), lambda a: (0, 0)),
        ],
        out_specs=[pl.BlockSpec((tile, 3 * depth), lambda a: (a, 0)), pl.BlockSpec((tile, tile), lambda a: (a, 0))],
        scratch_shapes=[pltpu.VMEM((depth, 3 * depth), BF16), pltpu.VMEM((3 * depth, depth), BF16)],
        compiler_params=pltpu.CompilerParams(vmem_limit_bytes=32 * 1024 * 1024),
        cost_estimate=COST,
        name="row_weights",
    )(place, rows_mine, rows_other, inverse)


def load_columns(choices, pieces, columns, tile, count):
    per = tile // LANES
    depth = 2 * tile
    for panel in range(2):
        for which, ref in enumerate(pieces):

            @pl.when(choices[panel] == which)
            def _(panel=panel, ref=ref):
                for i in range(count):
                    for h in range(per):
                        high, low = halves(ref[pl.ds(i * tile * per + h, tile, stride=per), :])
                        at = (i * per + h) * LANES
                        for copy, value in enumerate((high, high, low)):
                            row = copy * depth + panel * tile
                            columns[row : row + tile, at : at + LANES] = value


def products_kernel(tile, count, place_ref, weights_ref, piece_a, piece_b, piece_c, out_ref, columns):
    @pl.when(pl.program_id(0) == 0)
    def _():
        load_columns((place_ref[3], place_ref[4]), (piece_a, piece_b, piece_c), columns, tile, count)

    for i in range(count):
        at = i * tile
        out_ref[:, at : at + tile] = product(weights_ref[...], columns[:, at : at + tile], ((1,), (0,)))


def first_products(place, weights, pieces, row_tiles, tile):
    depth = weights.shape[1]
    vmem = pl.BlockSpec(memory_space=pltpu.VMEM)
    count = pieces[0].shape[0] * LANES // tile // tile
    return pl.pallas_call(
        functools.partial(products_kernel, tile, count),
        grid=(row_tiles,),
        out_shape=jax.ShapeDtypeStruct((row_tiles * tile, count * tile), F32),
        in_specs=[pl.BlockSpec(memory_space=pltpu.SMEM), pl.BlockSpec((tile, depth), lambda a: (a, 0))] + [vmem] * 3,
        out_specs=pl.BlockSpec((tile, count * tile), lambda a: (a, 0)),
        scratch_shapes=[pltpu.VMEM((depth, count * tile), BF16)],
        compiler_params=pltpu.CompilerParams(vmem_limit_bytes=24 * 1024 * 1024),
        cost_estimate=COST,
        name="first_products",
    )(place, weights, *pieces)


def trailing_kernel(tile, group, count, place_ref, block_ref, weights_ref, ready_ref, *rest):
    solved_ref = rest[0] if group == 0 else None
    pieces = rest[1:4]
    block_out, columns = rest[-2:]
    step = pl.program_id(0)
    row, col = place_ref[0], place_ref[1]
    per = tile // LANES
    top = (step == 0) & (row < 2)
    block = block_ref.reshape(tile * GROUP, LANES)
    out = block_out.reshape(tile * GROUP, LANES)

    @pl.when(step == 0)
    def _():
        load_columns((place_ref[5], place_ref[6]), pieces, columns, tile, count)

    @pl.when(top)
    def _():
        block_out[...] = jnp.zeros_like(block_out)

    @pl.when(jnp.logical_not(top))
    def _():
        for stage in range(2):
            parity = place_ref[2] if stage == 0 else 1 - place_ref[2]
            for i in range(count):
                at = i * tile
                if stage == 0:
                    update = ready_ref[:, at : at + tile]
                else:
                    update = product(weights_ref[...], columns[:, at : at + tile], ((1,), (0,)))
                for h in range(per):
                    where = pl.ds((2 * i + parity) * per + h, tile, stride=GROUP)
                    out[where, :] = block[where, :] - update[:, h * LANES : (h + 1) * LANES]

    if group == 0:

        @pl.when(col < 2)
        def _():
            for h in range(per):
                out[pl.ds(h, tile, stride=GROUP), :] = solved_ref[:, h * LANES : (h + 1) * LANES]


def trailing(group, place, block, weights, ready, extra, pieces, row_tiles, col_tiles, tile):
    per = tile // LANES
    depth = weights.shape[1]
    count = GROUP // per // 2
    view = grouped(block, row_tiles, col_tiles, tile)
    block_spec = pl.BlockSpec((tile, None, GROUP, LANES), lambda a: (a, group, 0, 0))
    return pl.pallas_call(
        functools.partial(trailing_kernel, tile, group, count),
        grid=(row_tiles,),
        out_shape=jax.ShapeDtypeStruct(view.shape, F32),
        in_specs=[
            pl.BlockSpec(memory_space=pltpu.SMEM),
            block_spec,
            pl.BlockSpec((tile, depth), lambda a: (a, 0)),
            pl.BlockSpec((tile, count * tile), lambda a: (a, group)),
        ]
        + [pl.BlockSpec((tile, tile), lambda a: (a, 0)) if group == 0 else pl.BlockSpec(memory_space=pl.ANY)]
        + [pl.BlockSpec(memory_space=pltpu.VMEM)] * 3,
        out_specs=block_spec,
        scratch_shapes=[pltpu.VMEM((depth, count * tile), BF16)],
        input_output_aliases={} if group == 0 else {4: 0},
        compiler_params=pltpu.CompilerParams(vmem_limit_bytes=44 * 1024 * 1024),
        cost_estimate=COST,
        name="trailing_%d" % group,
    )(place, view, weights, ready, extra, *pieces)


AXES = ("prow", "pcol")


def send(value, route):
    pairs = []
    for device in range(32):
        to = route(device // 8, device // 4 % 2, device // 2 % 2, device % 2)
        if to is not None:
            pairs.append((device, ((to[0] * 2 + to[1]) * 2 + to[2]) * 2 + to[3]))
    return lax.ppermute(value, AXES, pairs)


def far_stage(z, x, y, k):
    to = {(0, 0): 3, (2, 0): 1, (0, 1): 2}.get((z, y))
    return None if to is None else (to, x, y, k)


def near_stage(z, x, y, k):
    to = {(0, 0): 1, (2, 0): 3, (3, 0): 2, (0, 1): 1, (1, 1): 3, (3, 1): 2}.get((z, y))
    return None if to is None else (to, x, y, k)


def by_rows(stage, z, y):
    return z == 0 or (y == 1 and z == (2 if stage == 0 else 1))


def same_core(stage):
    def route(z, x, y, k):
        if by_rows(stage, z, y) or k == x:
            return (z, 1 - x, y, k)
        return (z, x, y, x)

    return route


def cross_core(stage):
    def route(z, x, y, k):
        if by_rows(stage, z, y) or k == x:
            return None
        return (z, 1 - x, y, x)

    return route


def shards(kernel_tiles):
    row_tiles, _, tile, col_tiles, _, _ = kernel_tiles.shape
    row = lax.axis_index("prow")
    col = lax.axis_index("pcol")
    z, x, y, core = row // 2, row % 2, col // 2, col % 2
    per = tile // LANES
    block = kernel_tiles.reshape(row_tiles * tile * col_tiles * per, LANES)

    first_odd = jnp.where(y == 0, (z == 1) | (z == 2), z == 3).astype(jnp.int32)
    chosen = []
    for stage in range(2):
        rowwise = (z == 0) | ((y == 1) & (z == 2 - stage))
        own = core == x
        for panel in range(2):
            by_row = jnp.where(x == panel, 0, 1)
            by_col = jnp.where(own, jnp.where(core == panel, 0, 1), jnp.where(core == panel, 1, 2))
            chosen.append(jnp.where(rowwise, by_row, by_col))
    place = jnp.stack([row, col, jnp.where(z == 0, 0, first_odd)] + chosen).astype(jnp.int32)

    lead = gather_lead(block, row_tiles, col_tiles, tile)
    middle = tile * per // 2
    over_first = send(lead, lambda z, x, y, k: (z, x, 1, k) if y == 0 else None)
    rest, to_far, even, odd = gather_pieces(y.reshape(1), lead, block, row_tiles, col_tiles, tile)
    over_first, rest, to_far = lax.optimization_barrier((over_first, rest, to_far))
    half = jnp.where(y == 0, lead[:middle], over_first[middle:])
    half = jnp.where(z == 2, send(half, lambda z, x, y, k: (2, x, y, k) if z == 0 else None), half)
    half = jnp.where(z % 2 == 1, send(half, lambda z, x, y, k: (z + 1, x, y, k) if z % 2 == 0 else None), half)
    half, to_far = lax.optimization_barrier((half, to_far))
    far = send(to_far, far_stage)
    beside = send(half, lambda z, x, y, k: (z, 1 - x, y, k))
    above = send(half, lambda z, x, y, k: (z, x, 1 - y, k))
    corner = send(half, lambda z, x, y, k: (z, 1 - x, 1 - y, k))
    corner, rest = lax.optimization_barrier((corner, rest))
    mine = jnp.concatenate([half, beside, above, corner], axis=0)
    over_rest = send(rest, lambda z, x, y, k: (z, x, 1, k) if y == 0 else None)
    other = send(mine, lambda z, x, y, k: (z, x, y, 1 - k))
    state = corner_start(jnp.stack([core, x, y]).astype(jnp.int32), mine, other)

    state, far, over_rest = lax.optimization_barrier((state, far, over_rest))
    over = jnp.concatenate([over_first, over_rest], axis=0)
    rows_mine = jnp.where(y == 0, to_far, over)
    first = jnp.where(z == 0, even, jnp.where(y == 0, jnp.where(z == 2, to_far, far), jnp.where(z == 2, far, over)))
    to_near = jnp.where(y == 0, jnp.where(z == 3, far, to_far), jnp.where(z == 0, odd, over))
    split = to_near.shape[0] // 2
    to_near = [to_near[:split], to_near[split:]]
    state, first, to_near = lax.optimization_barrier((state, first, to_near))
    near = [send(to_near[0], near_stage), send(to_near[1], near_stage)]
    first = [first, send(first, same_core(0)), send(first, cross_core(0))]
    rows_other = send(rows_mine, lambda z, x, y, k: (z, x, y, 1 - k))
    inverse = corner_end(state)

    last = []
    for part in range(2):
        held = jnp.where(z == 0, odd[part * split : (part + 1) * split], near[part])
        if part == 0:
            inverse, held = lax.optimization_barrier((inverse, held))
        last.append([held, send(held, same_core(1)), send(held, cross_core(1))])
        if part == 0:
            weights, solved = row_weights(
                jnp.stack([row, col, core]).astype(jnp.int32), rows_mine, rows_other, inverse, row_tiles, tile
            )
            weights, near[1] = lax.optimization_barrier((weights, near[1]))

    ready = first_products(place, weights, first, row_tiles, tile)
    result = solved
    for part in range(2):
        result = trailing(part, place, block, weights, ready, result, last[part], row_tiles, col_tiles, tile)
    return result.reshape(kernel_tiles.shape)


def from_root(value, axis, root):
    mine = lax.axis_index(axis) == root
    return lax.psum(jnp.where(mine, value, jnp.zeros_like(value)), axis)


def shards_any(kernel_tiles):
    row_tiles, _, tile, col_tiles, _, _ = kernel_tiles.shape
    row = lax.axis_index("prow")
    col = lax.axis_index("pcol")
    per = tile // LANES
    block = kernel_tiles.reshape(row_tiles * tile * col_tiles * per, LANES)
    zero = jnp.zeros((), jnp.int32)
    lead = gather_lead(block, row_tiles, col_tiles, tile)
    _, across, even, odd = gather_pieces(zero.reshape(1), lead, block, row_tiles, col_tiles, tile)
    rows = [from_root(across, "pcol", panel) for panel in range(2)]
    middle = tile * per // 2
    tile_rows = []
    for panel in range(2):
        tiles = [from_root(from_root(lead, "pcol", panel), "prow", p) for p in range(2)]
        tile_rows.append(jnp.concatenate([t[s : s + middle] for s in (0, middle) for t in tiles], axis=0))
    inverse = corner_end(corner_start(jnp.zeros((3,), jnp.int32), tile_rows[0], tile_rows[1]))
    pieces = []
    for part in (even, odd):
        panels = [from_root(part, "prow", p) for p in range(2)]
        pieces.append(panels + [panels[0]])
    place = jnp.stack([row, col, zero, zero, zero + 1, zero, zero + 1]).astype(jnp.int32)
    weights, result = row_weights(place, rows[0], rows[1], inverse, row_tiles, tile)
    split = even.shape[0] // 2
    ready = first_products(place, weights, pieces[0], row_tiles, tile)
    for part in range(2):
        last = [piece[part * split : (part + 1) * split] for piece in pieces[1]]
        result = trailing(part, place, block, weights, ready, result, last, row_tiles, col_tiles, tile)
    return result.reshape(kernel_tiles.shape)


def solution(mesh):
    in_specs = (P(None, "prow", None, None, "pcol", None),)
    out_specs = P(None, "prow", None, None, "pcol", None)
    body = shards if (mesh.shape["prow"], mesh.shape["pcol"]) == (8, 4) else shards_any
    return jax.shard_map(body, mesh=mesh, in_specs=in_specs, out_specs=out_specs, check_vma=False)
```

```python
import functools

import jax
import jax.numpy as jnp
from jax import lax
from jax.experimental import pallas as pl
from jax.experimental.pallas import tpu as pltpu
from jax.sharding import PartitionSpec as P

HI = lax.Precision.HIGHEST
F32 = jnp.float32
BF16 = jnp.bfloat16
LANES = 128
VMEM_BYTES = 56 * 1024 * 1024


def splat(x, shape):
    return jnp.broadcast_to(x, shape)


def reciprocal(x):
    r = pl.reciprocal(x, approx=True)
    for _ in range(2):
        r = r * (2.0 - x * r)
    return r


def inverse_factor_128(block):
    size = 128
    step = 8
    count = size // step
    lane = lax.broadcasted_iota(jnp.int32, (step, size), 1)
    sub = lax.broadcasted_iota(jnp.int32, (step, size), 0)
    rows = [block[step * i : step * (i + 1), :] for i in range(count)]
    shape = (step, size)
    for j in range(count):
        base = step * j
        cols = [splat(rows[j][:, base + t : base + t + 1], shape) for t in range(step)]
        a = {}
        for t in range(step):
            for s in range(t, step):
                a[s, t] = splat(cols[t][s : s + 1, :], shape)
        in_block = (lane >= base) & (lane < base + step)
        unit = jnp.where(lane - base == sub, F32(1.0), F32(0.0))
        own = jnp.where(in_block, unit, rows[j])
        if j + 1 < count:
            below = [splat(rows[j + 1][:, base + t : base + t + 1], shape) for t in range(step)]
            near = jnp.where(in_block, F32(0.0), rows[j + 1])
        m = {}
        u = []
        w = []
        done = jnp.zeros(shape, F32)
        for t in range(0, step, 2):
            p, b, c = a[t, t], a[t + 1, t], a[t + 1, t + 1]
            det = p * c - b * b
            inv = reciprocal(det)
            for s in range(t + 2, step):
                m[s, t] = (c * a[s, t] - b * a[s, t + 1]) * inv
                m[s, t + 1] = (p * a[s, t + 1] - b * a[s, t]) * inv
            for v in range(t + 2, step):
                for s in range(v, step):
                    a[s, v] = a[s, v] - (m[s, t] * a[v, t] + m[s, t + 1] * a[v, t + 1])
            for k in (t, t + 1):
                row = splat(own[k : k + 1, :], shape)
                for s in range(t):
                    row = row - m[k, s] * u[s]
                u.append(row)
            w.append((c * u[t] - b * u[t + 1]) * inv)
            w.append((p * u[t + 1] - b * u[t]) * inv)
            root = lax.rsqrt(p)
            over = root * root
            done = jnp.where(sub == t, u[t] * root, done)
            done = jnp.where(sub == t + 1, (u[t + 1] - (b * over) * u[t]) * lax.rsqrt(det * over), done)
            if j + 1 < count:
                for k in (t, t + 1):
                    for s in range(t):
                        below[k] = below[k] - m[k, s] * below[s]
                near = near - (below[t] * w[t] + below[t + 1] * w[t + 1])
        if j + 1 < count:
            rows[j + 1] = near
        g = [None] * step
        for t in reversed(range(0, step, 2)):
            for k in (t + 1, t):
                row = w[k]
                for s in reversed(range(t + 2, step)):
                    row = row - m[s, k] * g[s]
                g[k] = row
        for i in range(j + 2, count):
            acc = jnp.where(in_block, F32(0.0), rows[i])
            for t in reversed(range(step)):
                acc = acc - splat(rows[i][:, base + t : base + t + 1], shape) * g[t]
            rows[i] = acc
        rows[j] = jnp.where(lane < base + step, done, F32(0.0))
    return jnp.concatenate(rows, axis=0)


def eliminate(state, first, last):
    rows = state.shape[0]
    for o in range(first, last):
        lo, hi = o * LANES, (o + 1) * LANES
        diag = inverse_factor_128(state[lo:hi, lo:hi])
        upper = jnp.dot(diag, state[lo:hi, :], precision=HI, preferred_element_type=F32)
        parts = ([upper[:, :lo]] if lo else []) + [diag] + ([upper[:, hi:]] if hi < rows else [])
        wide = jnp.concatenate(parts, axis=1)
        if hi < rows:
            state[hi:, lo:hi] = jnp.zeros((rows - hi, LANES), F32)
            state[hi:, :] -= lax.dot_general(
                upper[:, hi:], wide, (((0,), (0,)), ((), ())), precision=HI, preferred_element_type=F32
            )
            state[lo:hi, hi:] = jnp.zeros((LANES, rows - hi), F32)
        state[lo:hi, :hi] = wide[:, :hi]


def corner_start_kernel(place_ref, mine_ref, other_ref, state):
    core, side, across = place_ref[0], place_ref[1], place_ref[2]
    rows = state.shape[0]
    tile = rows // 2
    half = tile // 2
    per = tile // LANES
    for which, ref in ((core, mine_ref), (1 - core, other_ref)):
        for part in range(4):
            at_side = side if part % 2 == 0 else 1 - side
            at_half = across if part < 2 else 1 - across
            at = pl.multiple_of(which * tile + at_half * half, half)
            for target in range(2):

                @pl.when(at_side == target)
                def _(ref=ref, part=part, at=at, target=target):
                    for h in range(per):
                        start = target * tile + h * LANES
                        state[pl.ds(at, half), start : start + LANES] = ref[
                            pl.ds(part * half * per + h, half, stride=per), :
                        ]

    eliminate(state, 0, tile // LANES)


def corner_end_kernel(state_ref, inverse_ref):
    rows = state_ref.shape[0]
    inverse_ref[...] = state_ref[...]
    eliminate(inverse_ref, rows // 2 // LANES, rows // LANES)


COST = pl.CostEstimate(flops=1000, bytes_accessed=1000, transcendentals=0)


def corner_start(place, mine, other):
    width = mine.shape[0] // 2
    vmem = pl.BlockSpec(memory_space=pltpu.VMEM)
    return pl.pallas_call(
        corner_start_kernel,
        out_shape=jax.ShapeDtypeStruct((width, width), F32),
        in_specs=[pl.BlockSpec(memory_space=pltpu.SMEM), vmem, vmem],
        out_specs=vmem,
        compiler_params=pltpu.CompilerParams(vmem_limit_bytes=16 * 1024 * 1024),
        cost_estimate=COST,
        name="corner_start",
    )(place, mine, other)


def corner_end(state):
    vmem = pl.BlockSpec(memory_space=pltpu.VMEM)
    return pl.pallas_call(
        corner_end_kernel,
        out_shape=jax.ShapeDtypeStruct(state.shape, F32),
        in_specs=[vmem],
        out_specs=vmem,
        compiler_params=pltpu.CompilerParams(vmem_limit_bytes=16 * 1024 * 1024),
        cost_estimate=COST,
        name="corner_end",
    )(state)


def transposed_tile(block_ref, tile, stride):
    per = tile // LANES
    return jnp.concatenate([block_ref[pl.ds(h, tile, stride=stride), :] for h in range(per)], axis=1).T


def store_tile(ref, start, value, tile):
    per = tile // LANES
    for h in range(per):
        ref[pl.ds(start + h, tile, stride=per), :] = value[:, h * LANES : (h + 1) * LANES]


def lead_kernel(tile, block_ref, out_ref):
    store_tile(out_ref, 0, transposed_tile(block_ref.reshape(tile * GROUP, LANES), tile, GROUP), tile)


def gather_kernel(tile, col_tiles, row_tiles, place_ref, lead_ref, block_ref, top_ref, rest_ref, far_ref, even_ref,
                  odd_ref):
    step = pl.program_id(0)
    per = tile // LANES
    size = tile * per
    value = transposed_tile(block_ref.reshape(tile * GROUP, LANES), tile, GROUP)
    store_tile(rest_ref, 0, value, tile)

    @pl.when(place_ref[0] == 0)
    def _():
        store_tile(far_ref, pl.multiple_of((step + 1) * size, size), value, tile)

    @pl.when(step == 0)
    def _():
        for parity, ref in enumerate((even_ref, odd_ref)):
            for i in range(col_tiles // 2):
                for h in range(per):
                    ref[pl.ds(i * size + h, tile, stride=per), :] = top_ref[
                        pl.ds((2 * i + parity) * per + h, tile, stride=col_tiles * per), :
                    ]

        @pl.when(place_ref[0] == 0)
        def _():
            far_ref[:size, :] = lead_ref[...]

        @pl.when(place_ref[0] != 0)
        def _():
            far_ref[...] = even_ref[...]


GROUP = 8


def grouped(block, row_tiles, col_tiles, tile):
    return block.reshape(row_tiles * tile, col_tiles * tile // LANES // GROUP, GROUP, LANES)


def gather_lead(block, row_tiles, col_tiles, tile):
    return pl.pallas_call(
        functools.partial(lead_kernel, tile),
        grid=(1,),
        out_shape=jax.ShapeDtypeStruct((tile * tile // LANES, LANES), F32),
        in_specs=[pl.BlockSpec((tile, None, GROUP, LANES), lambda a: (0, 0, 0, 0))],
        out_specs=pl.BlockSpec((tile * tile // LANES, LANES), lambda a: (0, 0)),
        compiler_params=pltpu.CompilerParams(vmem_limit_bytes=VMEM_BYTES),
        cost_estimate=COST,
        name="gather_lead",
    )(grouped(block, row_tiles, col_tiles, tile))


def gather_pieces(place, lead, block, row_tiles, col_tiles, tile):
    per = tile // LANES
    size = tile * per
    top = (tile * col_tiles * per, LANES)
    whole = [size * row_tiles] + [size * (col_tiles // 2)] * 2
    return pl.pallas_call(
        functools.partial(gather_kernel, tile, col_tiles, row_tiles),
        grid=(row_tiles - 1,),
        out_shape=[jax.ShapeDtypeStruct((s, LANES), F32) for s in [size * (row_tiles - 1)] + whole],
        in_specs=[
            pl.BlockSpec(memory_space=pltpu.SMEM),
            pl.BlockSpec((size, LANES), lambda a: (0, 0)),
            pl.BlockSpec((tile, None, GROUP, LANES), lambda a: (a + 1, 0, 0, 0)),
            pl.BlockSpec(top, lambda a: (0, 0)),
        ],
        out_specs=[pl.BlockSpec((size, LANES), lambda a: (a, 0))]
        + [pl.BlockSpec((s, LANES), lambda a: (0, 0)) for s in whole],
        compiler_params=pltpu.CompilerParams(vmem_limit_bytes=VMEM_BYTES),
        cost_estimate=COST,
        name="gather_pieces",
    )(place, lead, grouped(block, row_tiles, col_tiles, tile), block)


def halves(x):
    high = x.astype(BF16)
    return high, (x - high.astype(F32)).astype(BF16)


def left_factor(x):
    high, low = halves(x)
    return jnp.concatenate([high, low, high], axis=1)


def right_factor(x, axis):
    high, low = halves(x)
    return jnp.concatenate([high, high, low], axis=axis)


def product(a, b, dims):
    return lax.dot_general(a, b, (dims, ((), ())), preferred_element_type=F32)


def weights_kernel(tile, place_ref, rows_mine, rows_other, inverse_ref, weights_ref, solved_ref, across, along):
    step = pl.program_id(0)
    row, col, core = place_ref[0], place_ref[1], place_ref[2]
    per = tile // LANES

    @pl.when(step == 0)
    def _():
        across[...] = right_factor(inverse_ref[...], 1)
        along[...] = right_factor(inverse_ref[...], 0)

    mine, other = [
        jnp.concatenate([r[pl.ds(h, tile, stride=per), :] for h in range(per)], axis=1)
        for r in (rows_mine, rows_other)
    ]
    lead = jnp.concatenate([jnp.where(core == 0, mine, other).T, jnp.where(core == 0, other, mine).T], axis=1)
    solved = product(left_factor(lead), across[...], ((1,), (1,)))
    weights_ref[...] = left_factor(product(left_factor(solved), along[...], ((1,), (0,))))

    @pl.when(col < 2)
    def _():
        mine = jnp.where(col == 0, solved[:, :tile], solved[:, tile:])
        r = lax.broadcasted_iota(jnp.int32, (tile, tile), 0)
        s = lax.broadcasted_iota(jnp.int32, (tile, tile), 1)
        top = (step == 0) & (row < 2)
        on_diag = top & (row == col)
        above = top & (row < col)
        keep = jnp.where(on_diag, s - r, jnp.where(above, 1, 0)) <= 0
        solved_ref[...] = jnp.where(keep, mine, F32(0.0))


def row_weights(place, rows_mine, rows_other, inverse, row_tiles, tile):
    depth = inverse.shape[0]
    rows_spec = pl.BlockSpec((tile * tile // LANES, LANES), lambda a: (a, 0))
    total = row_tiles * tile
    return pl.pallas_call(
        functools.partial(weights_kernel, tile),
        grid=(row_tiles,),
        out_shape=[jax.ShapeDtypeStruct((total, 3 * depth), BF16), jax.ShapeDtypeStruct((total, tile), F32)],
        in_specs=[
            pl.BlockSpec(memory_space=pltpu.SMEM),
            rows_spec,
            rows_spec,
            pl.BlockSpec((depth, depth), lambda a: (0, 0)),
        ],
        out_specs=[pl.BlockSpec((tile, 3 * depth), lambda a: (a, 0)), pl.BlockSpec((tile, tile), lambda a: (a, 0))],
        scratch_shapes=[pltpu.VMEM((depth, 3 * depth), BF16), pltpu.VMEM((3 * depth, depth), BF16)],
        compiler_params=pltpu.CompilerParams(vmem_limit_bytes=32 * 1024 * 1024),
        cost_estimate=COST,
        name="row_weights",
    )(place, rows_mine, rows_other, inverse)


def load_columns(choices, pieces, columns, tile, count):
    per = tile // LANES
    depth = 2 * tile
    for panel in range(2):
        for which, ref in enumerate(pieces):

            @pl.when(choices[panel] == which)
            def _(panel=panel, ref=ref):
                for i in range(count):
                    for h in range(per):
                        high, low = halves(ref[pl.ds(i * tile * per + h, tile, stride=per), :])
                        at = (i * per + h) * LANES
                        for copy, value in enumerate((high, high, low)):
                            row = copy * depth + panel * tile
                            columns[row : row + tile, at : at + LANES] = value


def products_kernel(tile, count, place_ref, weights_ref, piece_a, piece_b, piece_c, out_ref, columns):
    @pl.when(pl.program_id(0) == 0)
    def _():
        load_columns((place_ref[3], place_ref[4]), (piece_a, piece_b, piece_c), columns, tile, count)

    for i in range(count):
        at = i * tile
        out_ref[:, at : at + tile] = product(weights_ref[...], columns[:, at : at + tile], ((1,), (0,)))


def first_products(place, weights, pieces, row_tiles, tile):
    depth = weights.shape[1]
    vmem = pl.BlockSpec(memory_space=pltpu.VMEM)
    count = pieces[0].shape[0] * LANES // tile // tile
    return pl.pallas_call(
        functools.partial(products_kernel, tile, count),
        grid=(row_tiles,),
        out_shape=jax.ShapeDtypeStruct((row_tiles * tile, count * tile), F32),
        in_specs=[pl.BlockSpec(memory_space=pltpu.SMEM), pl.BlockSpec((tile, depth), lambda a: (a, 0))] + [vmem] * 3,
        out_specs=pl.BlockSpec((tile, count * tile), lambda a: (a, 0)),
        scratch_shapes=[pltpu.VMEM((depth, count * tile), BF16)],
        compiler_params=pltpu.CompilerParams(vmem_limit_bytes=24 * 1024 * 1024),
        cost_estimate=COST,
        name="first_products",
    )(place, weights, *pieces)


def trailing_kernel(tile, group, count, place_ref, block_ref, weights_ref, ready_ref, *rest):
    solved_ref = rest[0] if group == 0 else None
    pieces = rest[1:4]
    block_out, columns = rest[-2:]
    step = pl.program_id(0)
    row, col = place_ref[0], place_ref[1]
    per = tile // LANES
    top = (step == 0) & (row < 2)
    block = block_ref.reshape(tile * GROUP, LANES)
    out = block_out.reshape(tile * GROUP, LANES)

    @pl.when(step == 0)
    def _():
        load_columns((place_ref[5], place_ref[6]), pieces, columns, tile, count)

    @pl.when(top)
    def _():
        block_out[...] = jnp.zeros_like(block_out)

    @pl.when(jnp.logical_not(top))
    def _():
        for stage in range(2):
            parity = place_ref[2] if stage == 0 else 1 - place_ref[2]
            for i in range(count):
                at = i * tile
                if stage == 0:
                    update = ready_ref[:, at : at + tile]
                else:
                    update = product(weights_ref[...], columns[:, at : at + tile], ((1,), (0,)))
                for h in range(per):
                    where = pl.ds((2 * i + parity) * per + h, tile, stride=GROUP)
                    out[where, :] = block[where, :] - update[:, h * LANES : (h + 1) * LANES]

    if group == 0:

        @pl.when(col < 2)
        def _():
            for h in range(per):
                out[pl.ds(h, tile, stride=GROUP), :] = solved_ref[:, h * LANES : (h + 1) * LANES]


def trailing(group, place, block, weights, ready, extra, pieces, row_tiles, col_tiles, tile):
    per = tile // LANES
    depth = weights.shape[1]
    count = GROUP // per // 2
    view = grouped(block, row_tiles, col_tiles, tile)
    block_spec = pl.BlockSpec((tile, None, GROUP, LANES), lambda a: (a, group, 0, 0))
    return pl.pallas_call(
        functools.partial(trailing_kernel, tile, group, count),
        grid=(row_tiles,),
        out_shape=jax.ShapeDtypeStruct(view.shape, F32),
        in_specs=[
            pl.BlockSpec(memory_space=pltpu.SMEM),
            block_spec,
            pl.BlockSpec((tile, depth), lambda a: (a, 0)),
            pl.BlockSpec((tile, count * tile), lambda a: (a, group)),
        ]
        + [pl.BlockSpec((tile, tile), lambda a: (a, 0)) if group == 0 else pl.BlockSpec(memory_space=pl.ANY)]
        + [pl.BlockSpec(memory_space=pltpu.VMEM)] * 3,
        out_specs=block_spec,
        scratch_shapes=[pltpu.VMEM((depth, count * tile), BF16)],
        input_output_aliases={} if group == 0 else {4: 0},
        compiler_params=pltpu.CompilerParams(vmem_limit_bytes=44 * 1024 * 1024),
        cost_estimate=COST,
        name="trailing_%d" % group,
    )(place, view, weights, ready, extra, *pieces)


AXES = ("prow", "pcol")


def send(value, route):
    pairs = []
    for device in range(32):
        to = route(device // 8, device // 4 % 2, device // 2 % 2, device % 2)
        if to is not None:
            pairs.append((device, ((to[0] * 2 + to[1]) * 2 + to[2]) * 2 + to[3]))
    return lax.ppermute(value, AXES, pairs)


def far_stage(z, x, y, k):
    to = {(0, 0): 3, (2, 0): 1, (0, 1): 2}.get((z, y))
    return None if to is None else (to, x, y, k)


def near_stage(z, x, y, k):
    to = {(0, 0): 1, (2, 0): 3, (3, 0): 2, (0, 1): 1, (1, 1): 3, (3, 1): 2}.get((z, y))
    return None if to is None else (to, x, y, k)


def by_rows(stage, z, y):
    return z == 0 or (y == 1 and z == (2 if stage == 0 else 1))


def same_core(stage):
    def route(z, x, y, k):
        if by_rows(stage, z, y) or k == x:
            return (z, 1 - x, y, k)
        return (z, x, y, x)

    return route


def cross_core(stage):
    def route(z, x, y, k):
        if by_rows(stage, z, y) or k == x:
            return None
        return (z, 1 - x, y, x)

    return route


def shards(kernel_tiles):
    row_tiles, _, tile, col_tiles, _, _ = kernel_tiles.shape
    row = lax.axis_index("prow")
    col = lax.axis_index("pcol")
    z, x, y, core = row // 2, row % 2, col // 2, col % 2
    per = tile // LANES
    block = kernel_tiles.reshape(row_tiles * tile * col_tiles * per, LANES)

    first_odd = jnp.where(y == 0, (z == 1) | (z == 2), z == 3).astype(jnp.int32)
    chosen = []
    for stage in range(2):
        rowwise = (z == 0) | ((y == 1) & (z == 2 - stage))
        own = core == x
        for panel in range(2):
            by_row = jnp.where(x == panel, 0, 1)
            by_col = jnp.where(own, jnp.where(core == panel, 0, 1), jnp.where(core == panel, 1, 2))
            chosen.append(jnp.where(rowwise, by_row, by_col))
    place = jnp.stack([row, col, jnp.where(z == 0, 0, first_odd)] + chosen).astype(jnp.int32)

    lead = gather_lead(block, row_tiles, col_tiles, tile)
    middle = tile * per // 2
    over_first = send(lead, lambda z, x, y, k: (z, x, 1, k) if y == 0 else None)
    rest, to_far, even, odd = gather_pieces(y.reshape(1), lead, block, row_tiles, col_tiles, tile)
    over_first, rest, to_far = lax.optimization_barrier((over_first, rest, to_far))
    half = jnp.where(y == 0, lead[:middle], over_first[middle:])
    down = [send(half, lambda z, x, y, k, to=to: (to, x, y, k) if z == 0 else None) for to in (1, 2, 3)]
    down, to_far, rest = lax.optimization_barrier((down, to_far, rest))
    far = send(to_far, far_stage)
    over_rest = send(rest, lambda z, x, y, k: (z, x, 1, k) if y == 0 else None)
    half = jnp.where(z == 0, half, jnp.where(z == 1, down[0], jnp.where(z == 2, down[1], down[2])))
    beside = send(half, lambda z, x, y, k: (z, 1 - x, y, k))
    above = send(half, lambda z, x, y, k: (z, x, 1 - y, k))
    corner = send(half, lambda z, x, y, k: (z, 1 - x, 1 - y, k))
    mine = jnp.concatenate([half, beside, above, corner], axis=0)
    other = send(mine, lambda z, x, y, k: (z, x, y, 1 - k))

    over = jnp.concatenate([over_first, over_rest], axis=0)
    rows_mine = jnp.where(y == 0, to_far, over)
    first = jnp.where(z == 0, even, jnp.where(y == 0, jnp.where(z == 2, to_far, far), jnp.where(z == 2, far, over)))
    to_near = jnp.where(y == 0, jnp.where(z == 3, far, to_far), jnp.where(z == 0, odd, over))
    split = to_near.shape[0] // 2
    to_near = [to_near[:split], to_near[split:]]
    mine, other, first, to_near = lax.optimization_barrier((mine, other, first, to_near))
    near = [send(to_near[0], near_stage), send(to_near[1], near_stage)]
    first = [first, send(first, same_core(0)), send(first, cross_core(0))]
    rows_other = send(rows_mine, lambda z, x, y, k: (z, x, y, 1 - k))
    inverse = corner_end(corner_start(jnp.stack([core, x, y]).astype(jnp.int32), mine, other))

    last = []
    for part in range(2):
        held = jnp.where(z == 0, odd[part * split : (part + 1) * split], near[part])
        if part == 0:
            inverse, held = lax.optimization_barrier((inverse, held))
        last.append([held, send(held, same_core(1)), send(held, cross_core(1))])
        if part == 0:
            inverse, first = lax.optimization_barrier((inverse, first))
            weights, solved = row_weights(
                jnp.stack([row, col, core]).astype(jnp.int32), rows_mine, rows_other, inverse, row_tiles, tile
            )
            weights, near[1] = lax.optimization_barrier((weights, near[1]))

    ready = first_products(place, weights, first, row_tiles, tile)
    result = solved
    for part in range(2):
        result = trailing(part, place, block, weights, ready, result, last[part], row_tiles, col_tiles, tile)
    return result.reshape(kernel_tiles.shape)


def from_root(value, axis, root):
    mine = lax.axis_index(axis) == root
    return lax.psum(jnp.where(mine, value, jnp.zeros_like(value)), axis)


def shards_any(kernel_tiles):
    row_tiles, _, tile, col_tiles, _, _ = kernel_tiles.shape
    row = lax.axis_index("prow")
    col = lax.axis_index("pcol")
    per = tile // LANES
    block = kernel_tiles.reshape(row_tiles * tile * col_tiles * per, LANES)
    zero = jnp.zeros((), jnp.int32)
    lead = gather_lead(block, row_tiles, col_tiles, tile)
    _, across, even, odd = gather_pieces(zero.reshape(1), lead, block, row_tiles, col_tiles, tile)
    rows = [from_root(across, "pcol", panel) for panel in range(2)]
    middle = tile * per // 2
    tile_rows = []
    for panel in range(2):
        tiles = [from_root(from_root(lead, "pcol", panel), "prow", p) for p in range(2)]
        tile_rows.append(jnp.concatenate([t[s : s + middle] for s in (0, middle) for t in tiles], axis=0))
    inverse = corner_end(corner_start(jnp.zeros((3,), jnp.int32), tile_rows[0], tile_rows[1]))
    pieces = []
    for part in (even, odd):
        panels = [from_root(part, "prow", p) for p in range(2)]
        pieces.append(panels + [panels[0]])
    place = jnp.stack([row, col, zero, zero, zero + 1, zero, zero + 1]).astype(jnp.int32)
    weights, result = row_weights(place, rows[0], rows[1], inverse, row_tiles, tile)
    split = even.shape[0] // 2
    ready = first_products(place, weights, pieces[0], row_tiles, tile)
    for part in range(2):
        last = [piece[part * split : (part + 1) * split] for piece in pieces[1]]
        result = trailing(part, place, block, weights, ready, result, last, row_tiles, col_tiles, tile)
    return result.reshape(kernel_tiles.shape)


def solution(mesh):
    in_specs = (P(None, "prow", None, None, "pcol", None),)
    out_specs = P(None, "prow", None, None, "pcol", None)
    body = shards if (mesh.shape["prow"], mesh.shape["pcol"]) == (8, 4) else shards_any
    return jax.shard_map(body, mesh=mesh, in_specs=in_specs, out_specs=out_specs, check_vma=False)
```

```python
import functools

import jax
import jax.numpy as jnp
from jax import lax
from jax.experimental import pallas as pl
from jax.experimental.pallas import tpu as pltpu
from jax.sharding import PartitionSpec as P

HI = lax.Precision.HIGHEST
F32 = jnp.float32
BF16 = jnp.bfloat16
LANES = 128
VMEM_BYTES = 56 * 1024 * 1024


def splat(x, shape):
    return jnp.broadcast_to(x, shape)


def reciprocal(x):
    r = pl.reciprocal(x, approx=True)
    for _ in range(2):
        r = r * (2.0 - x * r)
    return r


def inverse_factor_128(block):
    size = 128
    step = 8
    count = size // step
    lane = lax.broadcasted_iota(jnp.int32, (step, size), 1)
    sub = lax.broadcasted_iota(jnp.int32, (step, size), 0)
    rows = [block[step * i : step * (i + 1), :] for i in range(count)]
    shape = (step, size)
    for j in range(count):
        base = step * j
        cols = [splat(rows[j][:, base + t : base + t + 1], shape) for t in range(step)]
        a = {}
        for t in range(step):
            for s in range(t, step):
                a[s, t] = splat(cols[t][s : s + 1, :], shape)
        in_block = (lane >= base) & (lane < base + step)
        unit = jnp.where(lane - base == sub, F32(1.0), F32(0.0))
        own = jnp.where(in_block, unit, rows[j])
        if j + 1 < count:
            below = [splat(rows[j + 1][:, base + t : base + t + 1], shape) for t in range(step)]
            near = jnp.where(in_block, F32(0.0), rows[j + 1])
        m = {}
        u = []
        w = []
        done = jnp.zeros(shape, F32)
        for t in range(0, step, 2):
            p, b, c = a[t, t], a[t + 1, t], a[t + 1, t + 1]
            det = p * c - b * b
            inv = reciprocal(det)
            for s in range(t + 2, step):
                m[s, t] = (c * a[s, t] - b * a[s, t + 1]) * inv
                m[s, t + 1] = (p * a[s, t + 1] - b * a[s, t]) * inv
            for v in range(t + 2, step):
                for s in range(v, step):
                    a[s, v] = a[s, v] - (m[s, t] * a[v, t] + m[s, t + 1] * a[v, t + 1])
            for k in (t, t + 1):
                row = splat(own[k : k + 1, :], shape)
                for s in range(t):
                    row = row - m[k, s] * u[s]
                u.append(row)
            w.append((c * u[t] - b * u[t + 1]) * inv)
            w.append((p * u[t + 1] - b * u[t]) * inv)
            root = lax.rsqrt(p)
            over = root * root
            done = jnp.where(sub == t, u[t] * root, done)
            done = jnp.where(sub == t + 1, (u[t + 1] - (b * over) * u[t]) * lax.rsqrt(det * over), done)
            if j + 1 < count:
                for k in (t, t + 1):
                    for s in range(t):
                        below[k] = below[k] - m[k, s] * below[s]
                near = near - (below[t] * w[t] + below[t + 1] * w[t + 1])
        if j + 1 < count:
            rows[j + 1] = near
        g = [None] * step
        for t in reversed(range(0, step, 2)):
            for k in (t + 1, t):
                row = w[k]
                for s in reversed(range(t + 2, step)):
                    row = row - m[s, k] * g[s]
                g[k] = row
        for i in range(j + 2, count):
            acc = jnp.where(in_block, F32(0.0), rows[i])
            for t in reversed(range(step)):
                acc = acc - splat(rows[i][:, base + t : base + t + 1], shape) * g[t]
            rows[i] = acc
        rows[j] = jnp.where(lane < base + step, done, F32(0.0))
    return jnp.concatenate(rows, axis=0)


def eliminate(state, first, last):
    rows = state.shape[0]
    for o in range(first, last):
        lo, hi = o * LANES, (o + 1) * LANES
        diag = inverse_factor_128(state[lo:hi, lo:hi])
        upper = jnp.dot(diag, state[lo:hi, :], precision=HI, preferred_element_type=F32)
        parts = ([upper[:, :lo]] if lo else []) + [diag] + ([upper[:, hi:]] if hi < rows else [])
        wide = jnp.concatenate(parts, axis=1)
        if hi < rows:
            state[hi:, lo:hi] = jnp.zeros((rows - hi, LANES), F32)
            state[hi:, :] -= lax.dot_general(
                upper[:, hi:], wide, (((0,), (0,)), ((), ())), precision=HI, preferred_element_type=F32
            )
            state[lo:hi, hi:] = jnp.zeros((LANES, rows - hi), F32)
        state[lo:hi, :hi] = wide[:, :hi]


def corner_start_kernel(place_ref, mine_ref, other_ref, state):
    core, side, across = place_ref[0], place_ref[1], place_ref[2]
    rows = state.shape[0]
    tile = rows // 2
    half = tile // 2
    per = tile // LANES
    for which, ref in ((core, mine_ref), (1 - core, other_ref)):
        for part in range(4):
            at_side = side if part % 2 == 0 else 1 - side
            at_half = across if part < 2 else 1 - across
            at = pl.multiple_of(which * tile + at_half * half, half)
            for target in range(2):

                @pl.when(at_side == target)
                def _(ref=ref, part=part, at=at, target=target):
                    for h in range(per):
                        start = target * tile + h * LANES
                        state[pl.ds(at, half), start : start + LANES] = ref[
                            pl.ds(part * half * per + h, half, stride=per), :
                        ]

    eliminate(state, 0, tile // LANES)


def corner_end_kernel(state_ref, inverse_ref):
    rows = state_ref.shape[0]
    inverse_ref[...] = state_ref[...]
    eliminate(inverse_ref, rows // 2 // LANES, rows // LANES)


COST = pl.CostEstimate(flops=1000, bytes_accessed=1000, transcendentals=0)


def corner_start(place, mine, other):
    width = mine.shape[0] // 2
    vmem = pl.BlockSpec(memory_space=pltpu.VMEM)
    return pl.pallas_call(
        corner_start_kernel,
        out_shape=jax.ShapeDtypeStruct((width, width), F32),
        in_specs=[pl.BlockSpec(memory_space=pltpu.SMEM), vmem, vmem],
        out_specs=vmem,
        compiler_params=pltpu.CompilerParams(vmem_limit_bytes=16 * 1024 * 1024),
        cost_estimate=COST,
        name="corner_start",
    )(place, mine, other)


def corner_end(state):
    vmem = pl.BlockSpec(memory_space=pltpu.VMEM)
    return pl.pallas_call(
        corner_end_kernel,
        out_shape=jax.ShapeDtypeStruct(state.shape, F32),
        in_specs=[vmem],
        out_specs=vmem,
        compiler_params=pltpu.CompilerParams(vmem_limit_bytes=16 * 1024 * 1024),
        cost_estimate=COST,
        name="corner_end",
    )(state)


def transposed_tile(block_ref, tile, stride):
    per = tile // LANES
    return jnp.concatenate([block_ref[pl.ds(h, tile, stride=stride), :] for h in range(per)], axis=1).T


def store_tile(ref, start, value, tile):
    per = tile // LANES
    for h in range(per):
        ref[pl.ds(start + h, tile, stride=per), :] = value[:, h * LANES : (h + 1) * LANES]


def lead_kernel(tile, block_ref, out_ref):
    store_tile(out_ref, 0, transposed_tile(block_ref.reshape(tile * GROUP, LANES), tile, GROUP), tile)


def gather_kernel(tile, col_tiles, row_tiles, place_ref, lead_ref, block_ref, top_ref, rest_ref, far_ref, even_ref,
                  odd_ref):
    step = pl.program_id(0)
    per = tile // LANES
    size = tile * per
    value = transposed_tile(block_ref.reshape(tile * GROUP, LANES), tile, GROUP)
    store_tile(rest_ref, 0, value, tile)

    @pl.when(place_ref[0] == 0)
    def _():
        store_tile(far_ref, pl.multiple_of((step + 1) * size, size), value, tile)

    @pl.when(step == 0)
    def _():
        for parity, ref in enumerate((even_ref, odd_ref)):
            for i in range(col_tiles // 2):
                for h in range(per):
                    ref[pl.ds(i * size + h, tile, stride=per), :] = top_ref[
                        pl.ds((2 * i + parity) * per + h, tile, stride=col_tiles * per), :
                    ]

        @pl.when(place_ref[0] == 0)
        def _():
            far_ref[:size, :] = lead_ref[...]

        @pl.when(place_ref[0] != 0)
        def _():
            far_ref[...] = even_ref[...]


GROUP = 8


def grouped(block, row_tiles, col_tiles, tile):
    return block.reshape(row_tiles * tile, col_tiles * tile // LANES // GROUP, GROUP, LANES)


def gather_lead(block, row_tiles, col_tiles, tile):
    return pl.pallas_call(
        functools.partial(lead_kernel, tile),
        grid=(1,),
        out_shape=jax.ShapeDtypeStruct((tile * tile // LANES, LANES), F32),
        in_specs=[pl.BlockSpec((tile, None, GROUP, LANES), lambda a: (0, 0, 0, 0))],
        out_specs=pl.BlockSpec((tile * tile // LANES, LANES), lambda a: (0, 0)),
        compiler_params=pltpu.CompilerParams(vmem_limit_bytes=VMEM_BYTES),
        cost_estimate=COST,
        name="gather_lead",
    )(grouped(block, row_tiles, col_tiles, tile))


def gather_pieces(place, lead, block, row_tiles, col_tiles, tile):
    per = tile // LANES
    size = tile * per
    top = (tile * col_tiles * per, LANES)
    whole = [size * row_tiles] + [size * (col_tiles // 2)] * 2
    return pl.pallas_call(
        functools.partial(gather_kernel, tile, col_tiles, row_tiles),
        grid=(row_tiles - 1,),
        out_shape=[jax.ShapeDtypeStruct((s, LANES), F32) for s in [size * (row_tiles - 1)] + whole],
        in_specs=[
            pl.BlockSpec(memory_space=pltpu.SMEM),
            pl.BlockSpec((size, LANES), lambda a: (0, 0)),
            pl.BlockSpec((tile, None, GROUP, LANES), lambda a: (a + 1, 0, 0, 0)),
            pl.BlockSpec(top, lambda a: (0, 0)),
        ],
        out_specs=[pl.BlockSpec((size, LANES), lambda a: (a, 0))]
        + [pl.BlockSpec((s, LANES), lambda a: (0, 0)) for s in whole],
        compiler_params=pltpu.CompilerParams(vmem_limit_bytes=VMEM_BYTES),
        cost_estimate=COST,
        name="gather_pieces",
    )(place, lead, grouped(block, row_tiles, col_tiles, tile), block)


def halves(x):
    high = x.astype(BF16)
    return high, (x - high.astype(F32)).astype(BF16)


def left_factor(x):
    high, low = halves(x)
    return jnp.concatenate([high, low, high], axis=1)


def right_factor(x, axis):
    high, low = halves(x)
    return jnp.concatenate([high, high, low], axis=axis)


def product(a, b, dims):
    return lax.dot_general(a, b, (dims, ((), ())), preferred_element_type=F32)


def weights_kernel(tile, place_ref, rows_mine, rows_other, inverse_ref, weights_ref, solved_ref, across, along):
    step = pl.program_id(0)
    row, col, core = place_ref[0], place_ref[1], place_ref[2]
    per = tile // LANES

    @pl.when(step == 0)
    def _():
        across[...] = right_factor(inverse_ref[...], 1)
        along[...] = right_factor(inverse_ref[...], 0)

    mine, other = [
        jnp.concatenate([r[pl.ds(h, tile, stride=per), :] for h in range(per)], axis=1)
        for r in (rows_mine, rows_other)
    ]
    lead = jnp.concatenate([jnp.where(core == 0, mine, other).T, jnp.where(core == 0, other, mine).T], axis=1)
    solved = product(left_factor(lead), across[...], ((1,), (1,)))
    weights_ref[...] = left_factor(product(left_factor(solved), along[...], ((1,), (0,))))

    @pl.when(col < 2)
    def _():
        mine = jnp.where(col == 0, solved[:, :tile], solved[:, tile:])
        r = lax.broadcasted_iota(jnp.int32, (tile, tile), 0)
        s = lax.broadcasted_iota(jnp.int32, (tile, tile), 1)
        top = (step == 0) & (row < 2)
        on_diag = top & (row == col)
        above = top & (row < col)
        keep = jnp.where(on_diag, s - r, jnp.where(above, 1, 0)) <= 0
        solved_ref[...] = jnp.where(keep, mine, F32(0.0))


def row_weights(place, rows_mine, rows_other, inverse, row_tiles, tile):
    depth = inverse.shape[0]
    rows_spec = pl.BlockSpec((tile * tile // LANES, LANES), lambda a: (a, 0))
    total = row_tiles * tile
    return pl.pallas_call(
        functools.partial(weights_kernel, tile),
        grid=(row_tiles,),
        out_shape=[jax.ShapeDtypeStruct((total, 3 * depth), BF16), jax.ShapeDtypeStruct((total, tile), F32)],
        in_specs=[
            pl.BlockSpec(memory_space=pltpu.SMEM),
            rows_spec,
            rows_spec,
            pl.BlockSpec((depth, depth), lambda a: (0, 0)),
        ],
        out_specs=[pl.BlockSpec((tile, 3 * depth), lambda a: (a, 0)), pl.BlockSpec((tile, tile), lambda a: (a, 0))],
        scratch_shapes=[pltpu.VMEM((depth, 3 * depth), BF16), pltpu.VMEM((3 * depth, depth), BF16)],
        compiler_params=pltpu.CompilerParams(vmem_limit_bytes=32 * 1024 * 1024),
        cost_estimate=COST,
        name="row_weights",
    )(place, rows_mine, rows_other, inverse)


def load_columns(choices, pieces, columns, tile, count):
    per = tile // LANES
    depth = 2 * tile
    for panel in range(2):
        for which, ref in enumerate(pieces):

            @pl.when(choices[panel] == which)
            def _(panel=panel, ref=ref):
                for i in range(count):
                    for h in range(per):
                        high, low = halves(ref[pl.ds(i * tile * per + h, tile, stride=per), :])
                        at = (i * per + h) * LANES
                        for copy, value in enumerate((high, high, low)):
                            row = copy * depth + panel * tile
                            columns[row : row + tile, at : at + LANES] = value


def products_kernel(tile, count, place_ref, weights_ref, piece_a, piece_b, piece_c, out_ref, columns):
    @pl.when(pl.program_id(0) == 0)
    def _():
        load_columns((place_ref[3], place_ref[4]), (piece_a, piece_b, piece_c), columns, tile, count)

    for i in range(count):
        at = i * tile
        out_ref[:, at : at + tile] = product(weights_ref[...], columns[:, at : at + tile], ((1,), (0,)))


def first_products(place, weights, pieces, row_tiles, tile):
    depth = weights.shape[1]
    vmem = pl.BlockSpec(memory_space=pltpu.VMEM)
    count = pieces[0].shape[0] * LANES // tile // tile
    return pl.pallas_call(
        functools.partial(products_kernel, tile, count),
        grid=(row_tiles,),
        out_shape=jax.ShapeDtypeStruct((row_tiles * tile, count * tile), F32),
        in_specs=[pl.BlockSpec(memory_space=pltpu.SMEM), pl.BlockSpec((tile, depth), lambda a: (a, 0))] + [vmem] * 3,
        out_specs=pl.BlockSpec((tile, count * tile), lambda a: (a, 0)),
        scratch_shapes=[pltpu.VMEM((depth, count * tile), BF16)],
        compiler_params=pltpu.CompilerParams(vmem_limit_bytes=24 * 1024 * 1024),
        cost_estimate=COST,
        name="first_products",
    )(place, weights, *pieces)


def trailing_kernel(tile, group, count, place_ref, block_ref, weights_ref, ready_ref, *rest):
    solved_ref = rest[0] if group == 0 else None
    pieces = rest[1:4]
    block_out, columns = rest[-2:]
    step = pl.program_id(0)
    row, col = place_ref[0], place_ref[1]
    per = tile // LANES
    top = (step == 0) & (row < 2)
    block = block_ref.reshape(tile * GROUP, LANES)
    out = block_out.reshape(tile * GROUP, LANES)

    @pl.when(step == 0)
    def _():
        load_columns((place_ref[5], place_ref[6]), pieces, columns, tile, count)

    @pl.when(top)
    def _():
        block_out[...] = jnp.zeros_like(block_out)

    @pl.when(jnp.logical_not(top))
    def _():
        for stage in range(2):
            parity = place_ref[2] if stage == 0 else 1 - place_ref[2]
            for i in range(count):
                at = i * tile
                if stage == 0:
                    update = ready_ref[:, at : at + tile]
                else:
                    update = product(weights_ref[...], columns[:, at : at + tile], ((1,), (0,)))
                for h in range(per):
                    where = pl.ds((2 * i + parity) * per + h, tile, stride=GROUP)
                    out[where, :] = block[where, :] - update[:, h * LANES : (h + 1) * LANES]

    if group == 0:

        @pl.when(col < 2)
        def _():
            for h in range(per):
                out[pl.ds(h, tile, stride=GROUP), :] = solved_ref[:, h * LANES : (h + 1) * LANES]


def trailing(group, place, block, weights, ready, extra, pieces, row_tiles, col_tiles, tile):
    per = tile // LANES
    depth = weights.shape[1]
    count = GROUP // per // 2
    view = grouped(block, row_tiles, col_tiles, tile)
    block_spec = pl.BlockSpec((tile, None, GROUP, LANES), lambda a: (a, group, 0, 0))
    return pl.pallas_call(
        functools.partial(trailing_kernel, tile, group, count),
        grid=(row_tiles,),
        out_shape=jax.ShapeDtypeStruct(view.shape, F32),
        in_specs=[
            pl.BlockSpec(memory_space=pltpu.SMEM),
            block_spec,
            pl.BlockSpec((tile, depth), lambda a: (a, 0)),
            pl.BlockSpec((tile, count * tile), lambda a: (a, group)),
        ]
        + [pl.BlockSpec((tile, tile), lambda a: (a, 0)) if group == 0 else pl.BlockSpec(memory_space=pl.ANY)]
        + [pl.BlockSpec(memory_space=pltpu.VMEM)] * 3,
        out_specs=block_spec,
        scratch_shapes=[pltpu.VMEM((depth, count * tile), BF16)],
        input_output_aliases={} if group == 0 else {4: 0},
        compiler_params=pltpu.CompilerParams(vmem_limit_bytes=44 * 1024 * 1024),
        cost_estimate=COST,
        name="trailing_%d" % group,
    )(place, view, weights, ready, extra, *pieces)


AXES = ("prow", "pcol")


def send(value, route):
    pairs = []
    for device in range(32):
        to = route(device // 8, device // 4 % 2, device // 2 % 2, device % 2)
        if to is not None:
            pairs.append((device, ((to[0] * 2 + to[1]) * 2 + to[2]) * 2 + to[3]))
    return lax.ppermute(value, AXES, pairs)


def far_stage(z, x, y, k):
    to = {(0, 0): 3, (2, 0): 1, (0, 1): 2}.get((z, y))
    return None if to is None else (to, x, y, k)


def near_stage(z, x, y, k):
    to = {(0, 0): 1, (2, 0): 3, (3, 0): 2, (0, 1): 1, (1, 1): 3, (3, 1): 2}.get((z, y))
    return None if to is None else (to, x, y, k)


def by_rows(stage, z, y):
    return z == 0 or (y == 1 and z == (2 if stage == 0 else 1))


def same_core(stage):
    def route(z, x, y, k):
        if by_rows(stage, z, y) or k == x:
            return (z, 1 - x, y, k)
        return (z, x, y, x)

    return route


def cross_core(stage):
    def route(z, x, y, k):
        if by_rows(stage, z, y) or k == x:
            return None
        return (z, 1 - x, y, x)

    return route


def shards(kernel_tiles):
    row_tiles, _, tile, col_tiles, _, _ = kernel_tiles.shape
    row = lax.axis_index("prow")
    col = lax.axis_index("pcol")
    z, x, y, core = row // 2, row % 2, col // 2, col % 2
    per = tile // LANES
    block = kernel_tiles.reshape(row_tiles * tile * col_tiles * per, LANES)

    first_odd = jnp.where(y == 0, (z == 1) | (z == 2), z == 3).astype(jnp.int32)
    chosen = []
    for stage in range(2):
        rowwise = (z == 0) | ((y == 1) & (z == 2 - stage))
        own = core == x
        for panel in range(2):
            by_row = jnp.where(x == panel, 0, 1)
            by_col = jnp.where(own, jnp.where(core == panel, 0, 1), jnp.where(core == panel, 1, 2))
            chosen.append(jnp.where(rowwise, by_row, by_col))
    place = jnp.stack([row, col, jnp.where(z == 0, 0, first_odd)] + chosen).astype(jnp.int32)

    lead = gather_lead(block, row_tiles, col_tiles, tile)
    middle = tile * per // 2
    over_first = send(lead, lambda z, x, y, k: (z, x, 1, k) if y == 0 else None)
    rest, to_far, even, odd = gather_pieces(y.reshape(1), lead, block, row_tiles, col_tiles, tile)
    over_first, rest, to_far = lax.optimization_barrier((over_first, rest, to_far))
    half = jnp.where(y == 0, lead[:middle], over_first[middle:])
    half = jnp.where(z == 2, send(half, lambda z, x, y, k: (2, x, y, k) if z == 0 else None), half)
    half = jnp.where(z % 2 == 1, send(half, lambda z, x, y, k: (z + 1, x, y, k) if z % 2 == 0 else None), half)
    half, to_far = lax.optimization_barrier((half, to_far))
    far = send(to_far, far_stage)
    beside = send(half, lambda z, x, y, k: (z, 1 - x, y, k))
    above = send(half, lambda z, x, y, k: (z, x, 1 - y, k))
    corner = send(half, lambda z, x, y, k: (z, 1 - x, 1 - y, k))
    corner, rest = lax.optimization_barrier((corner, rest))
    mine = jnp.concatenate([half, beside, above, corner], axis=0)
    over_rest = send(rest, lambda z, x, y, k: (z, x, 1, k) if y == 0 else None)
    other = send(mine, lambda z, x, y, k: (z, x, y, 1 - k))
    state = corner_start(jnp.stack([core, x, y]).astype(jnp.int32), mine, other)

    state, far, over_rest = lax.optimization_barrier((state, far, over_rest))
    over = jnp.concatenate([over_first, over_rest], axis=0)
    rows_mine = jnp.where(y == 0, to_far, over)
    first = jnp.where(z == 0, even, jnp.where(y == 0, jnp.where(z == 2, to_far, far), jnp.where(z == 2, far, over)))
    to_near = jnp.where(y == 0, jnp.where(z == 3, far, to_far), jnp.where(z == 0, odd, over))
    split = to_near.shape[0] // 2
    to_near = [to_near[:split], to_near[split:]]
    state, first, to_near = lax.optimization_barrier((state, first, to_near))
    near = [send(to_near[0], near_stage), send(to_near[1], near_stage)]
    first = [first, send(first, same_core(0)), send(first, cross_core(0))]
    rows_other = send(rows_mine, lambda z, x, y, k: (z, x, y, 1 - k))
    inverse = corner_end(state)

    last = []
    for part in range(2):
        held = jnp.where(z == 0, odd[part * split : (part + 1) * split], near[part])
        if part == 0:
            inverse, held = lax.optimization_barrier((inverse, held))
        last.append([held, send(held, same_core(1)), send(held, cross_core(1))])
        if part == 0:
            inverse, first = lax.optimization_barrier((inverse, first))
            weights, solved = row_weights(
                jnp.stack([row, col, core]).astype(jnp.int32), rows_mine, rows_other, inverse, row_tiles, tile
            )
            weights, near[1] = lax.optimization_barrier((weights, near[1]))

    ready = first_products(place, weights, first, row_tiles, tile)
    result = solved
    for part in range(2):
        result = trailing(part, place, block, weights, ready, result, last[part], row_tiles, col_tiles, tile)
    return result.reshape(kernel_tiles.shape)


def from_root(value, axis, root):
    mine = lax.axis_index(axis) == root
    return lax.psum(jnp.where(mine, value, jnp.zeros_like(value)), axis)


def shards_any(kernel_tiles):
    row_tiles, _, tile, col_tiles, _, _ = kernel_tiles.shape
    row = lax.axis_index("prow")
    col = lax.axis_index("pcol")
    per = tile // LANES
    block = kernel_tiles.reshape(row_tiles * tile * col_tiles * per, LANES)
    zero = jnp.zeros((), jnp.int32)
    lead = gather_lead(block, row_tiles, col_tiles, tile)
    _, across, even, odd = gather_pieces(zero.reshape(1), lead, block, row_tiles, col_tiles, tile)
    rows = [from_root(across, "pcol", panel) for panel in range(2)]
    middle = tile * per // 2
    tile_rows = []
    for panel in range(2):
        tiles = [from_root(from_root(lead, "pcol", panel), "prow", p) for p in range(2)]
        tile_rows.append(jnp.concatenate([t[s : s + middle] for s in (0, middle) for t in tiles], axis=0))
    inverse = corner_end(corner_start(jnp.zeros((3,), jnp.int32), tile_rows[0], tile_rows[1]))
    pieces = []
    for part in (even, odd):
        panels = [from_root(part, "prow", p) for p in range(2)]
        pieces.append(panels + [panels[0]])
    place = jnp.stack([row, col, zero, zero, zero + 1, zero, zero + 1]).astype(jnp.int32)
    weights, result = row_weights(place, rows[0], rows[1], inverse, row_tiles, tile)
    split = even.shape[0] // 2
    ready = first_products(place, weights, pieces[0], row_tiles, tile)
    for part in range(2):
        last = [piece[part * split : (part + 1) * split] for piece in pieces[1]]
        result = trailing(part, place, block, weights, ready, result, last, row_tiles, col_tiles, tile)
    return result.reshape(kernel_tiles.shape)


def solution(mesh):
    in_specs = (P(None, "prow", None, None, "pcol", None),)
    out_specs = P(None, "prow", None, None, "pcol", None)
    body = shards if (mesh.shape["prow"], mesh.shape["pcol"]) == (8, 4) else shards_any
    return jax.shard_map(body, mesh=mesh, in_specs=in_specs, out_specs=out_specs, check_vma=False)
```

```python
import functools

import jax
import jax.numpy as jnp
from jax import lax
from jax.experimental import pallas as pl
from jax.experimental.pallas import tpu as pltpu
from jax.sharding import PartitionSpec as P

HI = lax.Precision.HIGHEST
F32 = jnp.float32
BF16 = jnp.bfloat16
LANES = 128
VMEM_BYTES = 56 * 1024 * 1024


def splat(x, shape):
    return jnp.broadcast_to(x, shape)


def reciprocal(x):
    r = pl.reciprocal(x, approx=True)
    for _ in range(2):
        r = r * (2.0 - x * r)
    return r


def inverse_factor_128(block):
    size = 128
    step = 8
    count = size // step
    lane = lax.broadcasted_iota(jnp.int32, (step, size), 1)
    sub = lax.broadcasted_iota(jnp.int32, (step, size), 0)
    rows = [block[step * i : step * (i + 1), :] for i in range(count)]
    shape = (step, size)
    for j in range(count):
        base = step * j
        cols = [splat(rows[j][:, base + t : base + t + 1], shape) for t in range(step)]
        a = {}
        for t in range(step):
            for s in range(t, step):
                a[s, t] = splat(cols[t][s : s + 1, :], shape)
        in_block = (lane >= base) & (lane < base + step)
        unit = jnp.where(lane - base == sub, F32(1.0), F32(0.0))
        own = jnp.where(in_block, unit, rows[j])
        if j + 1 < count:
            below = [splat(rows[j + 1][:, base + t : base + t + 1], shape) for t in range(step)]
            near = jnp.where(in_block, F32(0.0), rows[j + 1])
        m = {}
        u = []
        w = []
        done = jnp.zeros(shape, F32)
        for t in range(0, step, 2):
            p, b, c = a[t, t], a[t + 1, t], a[t + 1, t + 1]
            det = p * c - b * b
            inv = reciprocal(det)
            for s in range(t + 2, step):
                m[s, t] = (c * a[s, t] - b * a[s, t + 1]) * inv
                m[s, t + 1] = (p * a[s, t + 1] - b * a[s, t]) * inv
            for v in range(t + 2, step):
                for s in range(v, step):
                    a[s, v] = a[s, v] - (m[s, t] * a[v, t] + m[s, t + 1] * a[v, t + 1])
            for k in (t, t + 1):
                row = splat(own[k : k + 1, :], shape)
                for s in range(t):
                    row = row - m[k, s] * u[s]
                u.append(row)
            w.append((c * u[t] - b * u[t + 1]) * inv)
            w.append((p * u[t + 1] - b * u[t]) * inv)
            root = lax.rsqrt(p)
            over = root * root
            done = jnp.where(sub == t, u[t] * root, done)
            done = jnp.where(sub == t + 1, (u[t + 1] - (b * over) * u[t]) * lax.rsqrt(det * over), done)
            if j + 1 < count:
                for k in (t, t + 1):
                    for s in range(t):
                        below[k] = below[k] - m[k, s] * below[s]
                near = near - (below[t] * w[t] + below[t + 1] * w[t + 1])
        if j + 1 < count:
            rows[j + 1] = near
        g = [None] * step
        for t in reversed(range(0, step, 2)):
            for k in (t + 1, t):
                row = w[k]
                for s in reversed(range(t + 2, step)):
                    row = row - m[s, k] * g[s]
                g[k] = row
        for i in range(j + 2, count):
            acc = jnp.where(in_block, F32(0.0), rows[i])
            for t in reversed(range(step)):
                acc = acc - splat(rows[i][:, base + t : base + t + 1], shape) * g[t]
            rows[i] = acc
        rows[j] = jnp.where(lane < base + step, done, F32(0.0))
    return jnp.concatenate(rows, axis=0)


def eliminate(state, first, last):
    rows = state.shape[0]
    for o in range(first, last):
        lo, hi = o * LANES, (o + 1) * LANES
        diag = inverse_factor_128(state[lo:hi, lo:hi])
        upper = jnp.dot(diag, state[lo:hi, :], precision=HI, preferred_element_type=F32)
        parts = ([upper[:, :lo]] if lo else []) + [diag] + ([upper[:, hi:]] if hi < rows else [])
        wide = jnp.concatenate(parts, axis=1)
        if hi < rows:
            state[hi:, lo:hi] = jnp.zeros((rows - hi, LANES), F32)
            state[hi:, :] -= lax.dot_general(
                upper[:, hi:], wide, (((0,), (0,)), ((), ())), precision=HI, preferred_element_type=F32
            )
            state[lo:hi, hi:] = jnp.zeros((LANES, rows - hi), F32)
        state[lo:hi, :hi] = wide[:, :hi]


def corner_start_kernel(place_ref, mine_ref, other_ref, state):
    core, side, across = place_ref[0], place_ref[1], place_ref[2]
    rows = state.shape[0]
    tile = rows // 2
    half = tile // 2
    per = tile // LANES
    for which, ref in ((core, mine_ref), (1 - core, other_ref)):
        for part in range(4):
            at_side = side if part % 2 == 0 else 1 - side
            at_half = across if part < 2 else 1 - across
            at = pl.multiple_of(which * tile + at_half * half, half)
            for target in range(2):

                @pl.when(at_side == target)
                def _(ref=ref, part=part, at=at, target=target):
                    for h in range(per):
                        start = target * tile + h * LANES
                        state[pl.ds(at, half), start : start + LANES] = ref[
                            pl.ds(part * half * per + h, half, stride=per), :
                        ]

    eliminate(state, 0, tile // LANES)


def corner_end_kernel(state_ref, inverse_ref):
    rows = state_ref.shape[0]
    inverse_ref[...] = state_ref[...]
    eliminate(inverse_ref, rows // 2 // LANES, rows // LANES)


COST = pl.CostEstimate(flops=1000, bytes_accessed=1000, transcendentals=0)


def corner_start(place, mine, other):
    width = mine.shape[0] // 2
    vmem = pl.BlockSpec(memory_space=pltpu.VMEM)
    return pl.pallas_call(
        corner_start_kernel,
        out_shape=jax.ShapeDtypeStruct((width, width), F32),
        in_specs=[pl.BlockSpec(memory_space=pltpu.SMEM), vmem, vmem],
        out_specs=vmem,
        compiler_params=pltpu.CompilerParams(vmem_limit_bytes=16 * 1024 * 1024),
        cost_estimate=COST,
        name="corner_start",
    )(place, mine, other)


def corner_end(state):
    vmem = pl.BlockSpec(memory_space=pltpu.VMEM)
    return pl.pallas_call(
        corner_end_kernel,
        out_shape=jax.ShapeDtypeStruct(state.shape, F32),
        in_specs=[vmem],
        out_specs=vmem,
        compiler_params=pltpu.CompilerParams(vmem_limit_bytes=16 * 1024 * 1024),
        cost_estimate=COST,
        name="corner_end",
    )(state)


def transposed_tile(block_ref, tile, stride):
    per = tile // LANES
    return jnp.concatenate([block_ref[pl.ds(h, tile, stride=stride), :] for h in range(per)], axis=1).T


def store_tile(ref, start, value, tile):
    per = tile // LANES
    for h in range(per):
        ref[pl.ds(start + h, tile, stride=per), :] = value[:, h * LANES : (h + 1) * LANES]


def lead_kernel(tile, block_ref, out_ref):
    store_tile(out_ref, 0, transposed_tile(block_ref.reshape(tile * GROUP, LANES), tile, GROUP), tile)


def gather_kernel(tile, col_tiles, row_tiles, place_ref, lead_ref, block_ref, top_ref, rest_ref, far_ref, even_ref,
                  odd_ref):
    step = pl.program_id(0)
    per = tile // LANES
    size = tile * per
    value = transposed_tile(block_ref.reshape(tile * GROUP, LANES), tile, GROUP)
    store_tile(rest_ref, 0, value, tile)

    @pl.when(place_ref[0] == 0)
    def _():
        store_tile(far_ref, pl.multiple_of((step + 1) * size, size), value, tile)

    @pl.when(step == 0)
    def _():
        for parity, ref in enumerate((even_ref, odd_ref)):
            for i in range(col_tiles // 2):
                for h in range(per):
                    ref[pl.ds(i * size + h, tile, stride=per), :] = top_ref[
                        pl.ds((2 * i + parity) * per + h, tile, stride=col_tiles * per), :
                    ]

        @pl.when(place_ref[0] == 0)
        def _():
            far_ref[:size, :] = lead_ref[...]

        @pl.when(place_ref[0] != 0)
        def _():
            far_ref[...] = even_ref[...]


GROUP = 8


def grouped(block, row_tiles, col_tiles, tile):
    return block.reshape(row_tiles * tile, col_tiles * tile // LANES // GROUP, GROUP, LANES)


def gather_lead(block, row_tiles, col_tiles, tile):
    return pl.pallas_call(
        functools.partial(lead_kernel, tile),
        grid=(1,),
        out_shape=jax.ShapeDtypeStruct((tile * tile // LANES, LANES), F32),
        in_specs=[pl.BlockSpec((tile, None, GROUP, LANES), lambda a: (0, 0, 0, 0))],
        out_specs=pl.BlockSpec((tile * tile // LANES, LANES), lambda a: (0, 0)),
        compiler_params=pltpu.CompilerParams(vmem_limit_bytes=VMEM_BYTES),
        cost_estimate=COST,
        name="gather_lead",
    )(grouped(block, row_tiles, col_tiles, tile))


def gather_pieces(place, lead, block, row_tiles, col_tiles, tile):
    per = tile // LANES
    size = tile * per
    top = (tile * col_tiles * per, LANES)
    whole = [size * row_tiles] + [size * (col_tiles // 2)] * 2
    return pl.pallas_call(
        functools.partial(gather_kernel, tile, col_tiles, row_tiles),
        grid=(row_tiles - 1,),
        out_shape=[jax.ShapeDtypeStruct((s, LANES), F32) for s in [size * (row_tiles - 1)] + whole],
        in_specs=[
            pl.BlockSpec(memory_space=pltpu.SMEM),
            pl.BlockSpec((size, LANES), lambda a: (0, 0)),
            pl.BlockSpec((tile, None, GROUP, LANES), lambda a: (a + 1, 0, 0, 0)),
            pl.BlockSpec(top, lambda a: (0, 0)),
        ],
        out_specs=[pl.BlockSpec((size, LANES), lambda a: (a, 0))]
        + [pl.BlockSpec((s, LANES), lambda a: (0, 0)) for s in whole],
        compiler_params=pltpu.CompilerParams(vmem_limit_bytes=VMEM_BYTES),
        cost_estimate=COST,
        name="gather_pieces",
    )(place, lead, grouped(block, row_tiles, col_tiles, tile), block)


def halves(x):
    high = x.astype(BF16)
    return high, (x - high.astype(F32)).astype(BF16)


def left_factor(x):
    high, low = halves(x)
    return jnp.concatenate([high, low, high], axis=1)


def right_factor(x, axis):
    high, low = halves(x)
    return jnp.concatenate([high, high, low], axis=axis)


def product(a, b, dims):
    return lax.dot_general(a, b, (dims, ((), ())), preferred_element_type=F32)


def weights_kernel(tile, place_ref, rows_mine, rows_other, inverse_ref, weights_ref, solved_ref, across, along):
    step = pl.program_id(0)
    row, col, core = place_ref[0], place_ref[1], place_ref[2]
    per = tile // LANES

    @pl.when(step == 0)
    def _():
        across[...] = right_factor(inverse_ref[...], 1)
        along[...] = right_factor(inverse_ref[...], 0)

    mine, other = [
        jnp.concatenate([r[pl.ds(h, tile, stride=per), :] for h in range(per)], axis=1)
        for r in (rows_mine, rows_other)
    ]
    lead = jnp.concatenate([jnp.where(core == 0, mine, other).T, jnp.where(core == 0, other, mine).T], axis=1)
    solved = product(left_factor(lead), across[...], ((1,), (1,)))
    weights_ref[...] = left_factor(product(left_factor(solved), along[...], ((1,), (0,))))

    @pl.when(col < 2)
    def _():
        mine = jnp.where(col == 0, solved[:, :tile], solved[:, tile:])
        r = lax.broadcasted_iota(jnp.int32, (tile, tile), 0)
        s = lax.broadcasted_iota(jnp.int32, (tile, tile), 1)
        top = (step == 0) & (row < 2)
        on_diag = top & (row == col)
        above = top & (row < col)
        keep = jnp.where(on_diag, s - r, jnp.where(above, 1, 0)) <= 0
        solved_ref[...] = jnp.where(keep, mine, F32(0.0))


def row_weights(place, rows_mine, rows_other, inverse, row_tiles, tile):
    depth = inverse.shape[0]
    rows_spec = pl.BlockSpec((tile * tile // LANES, LANES), lambda a: (a, 0))
    total = row_tiles * tile
    return pl.pallas_call(
        functools.partial(weights_kernel, tile),
        grid=(row_tiles,),
        out_shape=[jax.ShapeDtypeStruct((total, 3 * depth), BF16), jax.ShapeDtypeStruct((total, tile), F32)],
        in_specs=[
            pl.BlockSpec(memory_space=pltpu.SMEM),
            rows_spec,
            rows_spec,
            pl.BlockSpec((depth, depth), lambda a: (0, 0)),
        ],
        out_specs=[pl.BlockSpec((tile, 3 * depth), lambda a: (a, 0)), pl.BlockSpec((tile, tile), lambda a: (a, 0))],
        scratch_shapes=[pltpu.VMEM((depth, 3 * depth), BF16), pltpu.VMEM((3 * depth, depth), BF16)],
        compiler_params=pltpu.CompilerParams(vmem_limit_bytes=32 * 1024 * 1024),
        cost_estimate=COST,
        name="row_weights",
    )(place, rows_mine, rows_other, inverse)


def load_columns(choices, pieces, columns, tile, count):
    per = tile // LANES
    depth = 2 * tile
    for panel in range(2):
        for which, ref in enumerate(pieces):

            @pl.when(choices[panel] == which)
            def _(panel=panel, ref=ref):
                for i in range(count):
                    for h in range(per):
                        high, low = halves(ref[pl.ds(i * tile * per + h, tile, stride=per), :])
                        at = (i * per + h) * LANES
                        for copy, value in enumerate((high, high, low)):
                            row = copy * depth + panel * tile
                            columns[row : row + tile, at : at + LANES] = value


def products_kernel(tile, count, place_ref, weights_ref, piece_a, piece_b, piece_c, out_ref, columns):
    @pl.when(pl.program_id(0) == 0)
    def _():
        load_columns((place_ref[3], place_ref[4]), (piece_a, piece_b, piece_c), columns, tile, count)

    for i in range(count):
        at = i * tile
        out_ref[:, at : at + tile] = product(weights_ref[...], columns[:, at : at + tile], ((1,), (0,)))


def first_products(place, weights, pieces, row_tiles, tile):
    depth = weights.shape[1]
    piece = pl.BlockSpec(pieces[0].shape, lambda a: (0, 0))
    count = pieces[0].shape[0] * LANES // tile // tile
    return pl.pallas_call(
        functools.partial(products_kernel, tile, count),
        grid=(row_tiles,),
        out_shape=jax.ShapeDtypeStruct((row_tiles * tile, count * tile), F32),
        in_specs=[pl.BlockSpec(memory_space=pltpu.SMEM), pl.BlockSpec((tile, depth), lambda a: (a, 0))] + [piece] * 3,
        out_specs=pl.BlockSpec((tile, count * tile), lambda a: (a, 0)),
        scratch_shapes=[pltpu.VMEM((depth, count * tile), BF16)],
        compiler_params=pltpu.CompilerParams(vmem_limit_bytes=24 * 1024 * 1024),
        cost_estimate=COST,
        name="first_products",
    )(place, weights, *pieces)


def trailing_kernel(tile, group, count, place_ref, block_ref, weights_ref, ready_ref, *rest):
    solved_ref = rest[0] if group == 0 else None
    pieces = rest[1:4]
    block_out, columns = rest[-2:]
    step = pl.program_id(0)
    row, col = place_ref[0], place_ref[1]
    per = tile // LANES
    top = (step == 0) & (row < 2)
    block = block_ref.reshape(tile * GROUP, LANES)
    out = block_out.reshape(tile * GROUP, LANES)

    @pl.when(step == 0)
    def _():
        load_columns((place_ref[5], place_ref[6]), pieces, columns, tile, count)

    @pl.when(top)
    def _():
        block_out[...] = jnp.zeros_like(block_out)

    @pl.when(jnp.logical_not(top))
    def _():
        for stage in range(2):
            parity = place_ref[2] if stage == 0 else 1 - place_ref[2]
            for i in range(count):
                at = i * tile
                if stage == 0:
                    update = ready_ref[:, at : at + tile]
                else:
                    update = product(weights_ref[...], columns[:, at : at + tile], ((1,), (0,)))
                for h in range(per):
                    where = pl.ds((2 * i + parity) * per + h, tile, stride=GROUP)
                    out[where, :] = block[where, :] - update[:, h * LANES : (h + 1) * LANES]

    if group == 0:

        @pl.when(col < 2)
        def _():
            for h in range(per):
                out[pl.ds(h, tile, stride=GROUP), :] = solved_ref[:, h * LANES : (h + 1) * LANES]


def trailing(group, place, block, weights, ready, extra, pieces, row_tiles, col_tiles, tile):
    per = tile // LANES
    depth = weights.shape[1]
    count = GROUP // per // 2
    view = grouped(block, row_tiles, col_tiles, tile)
    block_spec = pl.BlockSpec((tile, None, GROUP, LANES), lambda a: (a, group, 0, 0))
    return pl.pallas_call(
        functools.partial(trailing_kernel, tile, group, count),
        grid=(row_tiles,),
        out_shape=jax.ShapeDtypeStruct(view.shape, F32),
        in_specs=[
            pl.BlockSpec(memory_space=pltpu.SMEM),
            block_spec,
            pl.BlockSpec((tile, depth), lambda a: (a, 0)),
            pl.BlockSpec((tile, count * tile), lambda a: (a, group)),
        ]
        + [pl.BlockSpec((tile, tile), lambda a: (a, 0)) if group == 0 else pl.BlockSpec(memory_space=pl.ANY)]
        + [pl.BlockSpec(pieces[0].shape, lambda a: (0, 0))] * 3,
        out_specs=block_spec,
        scratch_shapes=[pltpu.VMEM((depth, count * tile), BF16)],
        input_output_aliases={} if group == 0 else {4: 0},
        compiler_params=pltpu.CompilerParams(vmem_limit_bytes=44 * 1024 * 1024),
        cost_estimate=COST,
        name="trailing_%d" % group,
    )(place, view, weights, ready, extra, *pieces)


AXES = ("prow", "pcol")


def send(value, route):
    pairs = []
    for device in range(32):
        to = route(device // 8, device // 4 % 2, device // 2 % 2, device % 2)
        if to is not None:
            pairs.append((device, ((to[0] * 2 + to[1]) * 2 + to[2]) * 2 + to[3]))
    return lax.ppermute(value, AXES, pairs)


def far_stage(z, x, y, k):
    to = {(0, 0): 3, (2, 0): 1, (0, 1): 2}.get((z, y))
    return None if to is None else (to, x, y, k)


def near_stage(z, x, y, k):
    to = {(0, 0): 1, (2, 0): 3, (3, 0): 2, (0, 1): 1, (1, 1): 3, (3, 1): 2}.get((z, y))
    return None if to is None else (to, x, y, k)


def by_rows(stage, z, y):
    return z == 0 or (y == 1 and z == (2 if stage == 0 else 1))


def same_core(stage):
    def route(z, x, y, k):
        if by_rows(stage, z, y) or k == x:
            return (z, 1 - x, y, k)
        return (z, x, y, x)

    return route


def cross_core(stage):
    def route(z, x, y, k):
        if by_rows(stage, z, y) or k == x:
            return None
        return (z, 1 - x, y, x)

    return route


def shards(kernel_tiles):
    row_tiles, _, tile, col_tiles, _, _ = kernel_tiles.shape
    row = lax.axis_index("prow")
    col = lax.axis_index("pcol")
    z, x, y, core = row // 2, row % 2, col // 2, col % 2
    per = tile // LANES
    block = kernel_tiles.reshape(row_tiles * tile * col_tiles * per, LANES)

    first_odd = jnp.where(y == 0, (z == 1) | (z == 2), z == 3).astype(jnp.int32)
    chosen = []
    for stage in range(2):
        rowwise = (z == 0) | ((y == 1) & (z == 2 - stage))
        own = core == x
        for panel in range(2):
            by_row = jnp.where(x == panel, 0, 1)
            by_col = jnp.where(own, jnp.where(core == panel, 0, 1), jnp.where(core == panel, 1, 2))
            chosen.append(jnp.where(rowwise, by_row, by_col))
    place = jnp.stack([row, col, jnp.where(z == 0, 0, first_odd)] + chosen).astype(jnp.int32)

    lead = gather_lead(block, row_tiles, col_tiles, tile)
    middle = tile * per // 2
    over_first = send(lead, lambda z, x, y, k: (z, x, 1, k) if y == 0 else None)
    rest, to_far, even, odd = gather_pieces(y.reshape(1), lead, block, row_tiles, col_tiles, tile)
    over_first, rest, to_far = lax.optimization_barrier((over_first, rest, to_far))
    half = jnp.where(y == 0, lead[:middle], over_first[middle:])
    half = jnp.where(z == 2, send(half, lambda z, x, y, k: (2, x, y, k) if z == 0 else None), half)
    half = jnp.where(z % 2 == 1, send(half, lambda z, x, y, k: (z + 1, x, y, k) if z % 2 == 0 else None), half)
    half, to_far = lax.optimization_barrier((half, to_far))
    far = send(to_far, far_stage)
    beside = send(half, lambda z, x, y, k: (z, 1 - x, y, k))
    above = send(half, lambda z, x, y, k: (z, x, 1 - y, k))
    corner = send(half, lambda z, x, y, k: (z, 1 - x, 1 - y, k))
    corner, rest = lax.optimization_barrier((corner, rest))
    mine = jnp.concatenate([half, beside, above, corner], axis=0)
    over_rest = send(rest, lambda z, x, y, k: (z, x, 1, k) if y == 0 else None)
    other = send(mine, lambda z, x, y, k: (z, x, y, 1 - k))
    state = corner_start(jnp.stack([core, x, y]).astype(jnp.int32), mine, other)

    state, far, over_rest = lax.optimization_barrier((state, far, over_rest))
    over = jnp.concatenate([over_first, over_rest], axis=0)
    rows_mine = jnp.where(y == 0, to_far, over)
    first = jnp.where(z == 0, even, jnp.where(y == 0, jnp.where(z == 2, to_far, far), jnp.where(z == 2, far, over)))
    to_near = jnp.where(y == 0, jnp.where(z == 3, far, to_far), jnp.where(z == 0, odd, over))
    split = to_near.shape[0] // 2
    to_near = [to_near[:split], to_near[split:]]
    state, first, to_near = lax.optimization_barrier((state, first, to_near))
    near = [send(to_near[0], near_stage), send(to_near[1], near_stage)]
    first = [first, send(first, same_core(0)), send(first, cross_core(0))]
    rows_other = send(rows_mine, lambda z, x, y, k: (z, x, y, 1 - k))
    inverse = corner_end(state)

    last = []
    for part in range(2):
        held = jnp.where(z == 0, odd[part * split : (part + 1) * split], near[part])
        if part == 0:
            inverse, held = lax.optimization_barrier((inverse, held))
        last.append([held, send(held, same_core(1)), send(held, cross_core(1))])
        if part == 0:
            weights, solved = row_weights(
                jnp.stack([row, col, core]).astype(jnp.int32), rows_mine, rows_other, inverse, row_tiles, tile
            )
            weights, near[1], first = lax.optimization_barrier((weights, near[1], first))

    ready = first_products(place, weights, first, row_tiles, tile)
    result = solved
    for part in range(2):
        result = trailing(part, place, block, weights, ready, result, last[part], row_tiles, col_tiles, tile)
    return result.reshape(kernel_tiles.shape)


def from_root(value, axis, root):
    mine = lax.axis_index(axis) == root
    return lax.psum(jnp.where(mine, value, jnp.zeros_like(value)), axis)


def shards_any(kernel_tiles):
    row_tiles, _, tile, col_tiles, _, _ = kernel_tiles.shape
    row = lax.axis_index("prow")
    col = lax.axis_index("pcol")
    per = tile // LANES
    block = kernel_tiles.reshape(row_tiles * tile * col_tiles * per, LANES)
    zero = jnp.zeros((), jnp.int32)
    lead = gather_lead(block, row_tiles, col_tiles, tile)
    _, across, even, odd = gather_pieces(zero.reshape(1), lead, block, row_tiles, col_tiles, tile)
    rows = [from_root(across, "pcol", panel) for panel in range(2)]
    middle = tile * per // 2
    tile_rows = []
    for panel in range(2):
        tiles = [from_root(from_root(lead, "pcol", panel), "prow", p) for p in range(2)]
        tile_rows.append(jnp.concatenate([t[s : s + middle] for s in (0, middle) for t in tiles], axis=0))
    inverse = corner_end(corner_start(jnp.zeros((3,), jnp.int32), tile_rows[0], tile_rows[1]))
    pieces = []
    for part in (even, odd):
        panels = [from_root(part, "prow", p) for p in range(2)]
        pieces.append(panels + [panels[0]])
    place = jnp.stack([row, col, zero, zero, zero + 1, zero, zero + 1]).astype(jnp.int32)
    weights, result = row_weights(place, rows[0], rows[1], inverse, row_tiles, tile)
    split = even.shape[0] // 2
    ready = first_products(place, weights, pieces[0], row_tiles, tile)
    for part in range(2):
        last = [piece[part * split : (part + 1) * split] for piece in pieces[1]]
        result = trailing(part, place, block, weights, ready, result, last, row_tiles, col_tiles, tile)
    return result.reshape(kernel_tiles.shape)


def solution(mesh):
    in_specs = (P(None, "prow", None, None, "pcol", None),)
    out_specs = P(None, "prow", None, None, "pcol", None)
    body = shards if (mesh.shape["prow"], mesh.shape["pcol"]) == (8, 4) else shards_any
    return jax.shard_map(body, mesh=mesh, in_specs=in_specs, out_specs=out_specs, check_vma=False)
```

```python
import functools

import jax
import jax.numpy as jnp
from jax import lax
from jax.experimental import pallas as pl
from jax.experimental.pallas import tpu as pltpu
from jax.sharding import PartitionSpec as P

HI = lax.Precision.HIGHEST
F32 = jnp.float32
BF16 = jnp.bfloat16
LANES = 128
VMEM_BYTES = 56 * 1024 * 1024


def splat(x, shape):
    return jnp.broadcast_to(x, shape)


def reciprocal(x):
    r = pl.reciprocal(x, approx=True)
    for _ in range(2):
        r = r * (2.0 - x * r)
    return r


def inverse_factor_128(block):
    size = 128
    step = 8
    count = size // step
    lane = lax.broadcasted_iota(jnp.int32, (step, size), 1)
    sub = lax.broadcasted_iota(jnp.int32, (step, size), 0)
    rows = [block[step * i : step * (i + 1), :] for i in range(count)]
    shape = (step, size)
    for j in range(count):
        base = step * j
        cols = [splat(rows[j][:, base + t : base + t + 1], shape) for t in range(step)]
        a = {}
        for t in range(step):
            for s in range(t, step):
                a[s, t] = splat(cols[t][s : s + 1, :], shape)
        in_block = (lane >= base) & (lane < base + step)
        unit = jnp.where(lane - base == sub, F32(1.0), F32(0.0))
        own = jnp.where(in_block, unit, rows[j])
        if j + 1 < count:
            below = [splat(rows[j + 1][:, base + t : base + t + 1], shape) for t in range(step)]
            near = jnp.where(in_block, F32(0.0), rows[j + 1])
        m = {}
        u = []
        w = []
        done = jnp.zeros(shape, F32)
        for t in range(0, step, 2):
            p, b, c = a[t, t], a[t + 1, t], a[t + 1, t + 1]
            det = p * c - b * b
            inv = reciprocal(det)
            for s in range(t + 2, step):
                m[s, t] = (c * a[s, t] - b * a[s, t + 1]) * inv
                m[s, t + 1] = (p * a[s, t + 1] - b * a[s, t]) * inv
            for v in range(t + 2, step):
                for s in range(v, step):
                    a[s, v] = a[s, v] - (m[s, t] * a[v, t] + m[s, t + 1] * a[v, t + 1])
            for k in (t, t + 1):
                row = splat(own[k : k + 1, :], shape)
                for s in range(t):
                    row = row - m[k, s] * u[s]
                u.append(row)
            w.append((c * u[t] - b * u[t + 1]) * inv)
            w.append((p * u[t + 1] - b * u[t]) * inv)
            root = lax.rsqrt(p)
            over = root * root
            done = jnp.where(sub == t, u[t] * root, done)
            done = jnp.where(sub == t + 1, (u[t + 1] - (b * over) * u[t]) * lax.rsqrt(det * over), done)
            if j + 1 < count:
                for k in (t, t + 1):
                    for s in range(t):
                        below[k] = below[k] - m[k, s] * below[s]
                near = near - (below[t] * w[t] + below[t + 1] * w[t + 1])
        if j + 1 < count:
            rows[j + 1] = near
        g = [None] * step
        for t in reversed(range(0, step, 2)):
            for k in (t + 1, t):
                row = w[k]
                for s in reversed(range(t + 2, step)):
                    row = row - m[s, k] * g[s]
                g[k] = row
        for i in range(j + 2, count):
            acc = jnp.where(in_block, F32(0.0), rows[i])
            for t in reversed(range(step)):
                acc = acc - splat(rows[i][:, base + t : base + t + 1], shape) * g[t]
            rows[i] = acc
        rows[j] = jnp.where(lane < base + step, done, F32(0.0))
    return jnp.concatenate(rows, axis=0)


def eliminate(state, first, last):
    rows = state.shape[0]
    for o in range(first, last):
        lo, hi = o * LANES, (o + 1) * LANES
        diag = inverse_factor_128(state[lo:hi, lo:hi])
        upper = jnp.dot(diag, state[lo:hi, :], precision=HI, preferred_element_type=F32)
        parts = ([upper[:, :lo]] if lo else []) + [diag] + ([upper[:, hi:]] if hi < rows else [])
        wide = jnp.concatenate(parts, axis=1)
        if hi < rows:
            state[hi:, lo:hi] = jnp.zeros((rows - hi, LANES), F32)
            state[hi:, :] -= lax.dot_general(
                upper[:, hi:], wide, (((0,), (0,)), ((), ())), precision=HI, preferred_element_type=F32
            )
            state[lo:hi, hi:] = jnp.zeros((LANES, rows - hi), F32)
        state[lo:hi, :hi] = wide[:, :hi]


def corner_start_kernel(place_ref, mine_ref, other_ref, state):
    core, side, across = place_ref[0], place_ref[1], place_ref[2]
    rows = state.shape[0]
    tile = rows // 2
    half = tile // 2
    per = tile // LANES
    for which, ref in ((core, mine_ref), (1 - core, other_ref)):
        for part in range(4):
            at_side = side if part % 2 == 0 else 1 - side
            at_half = across if part < 2 else 1 - across
            at = pl.multiple_of(which * tile + at_half * half, half)
            for target in range(2):

                @pl.when(at_side == target)
                def _(ref=ref, part=part, at=at, target=target):
                    for h in range(per):
                        start = target * tile + h * LANES
                        state[pl.ds(at, half), start : start + LANES] = ref[
                            pl.ds(part * half * per + h, half, stride=per), :
                        ]

    eliminate(state, 0, tile // LANES)


def corner_end_kernel(state_ref, inverse_ref):
    rows = state_ref.shape[0]
    inverse_ref[...] = state_ref[...]
    eliminate(inverse_ref, rows // 2 // LANES, rows // LANES)


COST = pl.CostEstimate(flops=1000, bytes_accessed=1000, transcendentals=0)


def corner_start(place, mine, other):
    width = mine.shape[0] // 2
    vmem = pl.BlockSpec(memory_space=pltpu.VMEM)
    return pl.pallas_call(
        corner_start_kernel,
        out_shape=jax.ShapeDtypeStruct((width, width), F32),
        in_specs=[pl.BlockSpec(memory_space=pltpu.SMEM), vmem, vmem],
        out_specs=vmem,
        compiler_params=pltpu.CompilerParams(vmem_limit_bytes=16 * 1024 * 1024),
        cost_estimate=COST,
        name="corner_start",
    )(place, mine, other)


def corner_end(state):
    vmem = pl.BlockSpec(memory_space=pltpu.VMEM)
    return pl.pallas_call(
        corner_end_kernel,
        out_shape=jax.ShapeDtypeStruct(state.shape, F32),
        in_specs=[vmem],
        out_specs=vmem,
        compiler_params=pltpu.CompilerParams(vmem_limit_bytes=16 * 1024 * 1024),
        cost_estimate=COST,
        name="corner_end",
    )(state)


def transposed_tile(block_ref, tile, stride):
    per = tile // LANES
    return jnp.concatenate([block_ref[pl.ds(h, tile, stride=stride), :] for h in range(per)], axis=1).T


def store_tile(ref, start, value, tile):
    per = tile // LANES
    for h in range(per):
        ref[pl.ds(start + h, tile, stride=per), :] = value[:, h * LANES : (h + 1) * LANES]


def lead_kernel(tile, block_ref, out_ref):
    store_tile(out_ref, 0, transposed_tile(block_ref.reshape(tile * GROUP, LANES), tile, GROUP), tile)


def gather_kernel(tile, col_tiles, row_tiles, place_ref, lead_ref, block_ref, top_ref, rest_ref, far_ref, even_ref,
                  odd_ref):
    step = pl.program_id(0)
    per = tile // LANES
    size = tile * per
    value = transposed_tile(block_ref.reshape(tile * GROUP, LANES), tile, GROUP)
    store_tile(rest_ref, 0, value, tile)

    @pl.when(place_ref[0] == 0)
    def _():
        store_tile(far_ref, pl.multiple_of((step + 1) * size, size), value, tile)

    @pl.when(step == 0)
    def _():
        for parity, ref in enumerate((even_ref, odd_ref)):
            for i in range(col_tiles // 2):
                for h in range(per):
                    ref[pl.ds(i * size + h, tile, stride=per), :] = top_ref[
                        pl.ds((2 * i + parity) * per + h, tile, stride=col_tiles * per), :
                    ]

        @pl.when(place_ref[0] == 0)
        def _():
            far_ref[:size, :] = lead_ref[...]

        @pl.when(place_ref[0] != 0)
        def _():
            far_ref[...] = even_ref[...]


GROUP = 8


def grouped(block, row_tiles, col_tiles, tile):
    return block.reshape(row_tiles * tile, col_tiles * tile // LANES // GROUP, GROUP, LANES)


def gather_lead(block, row_tiles, col_tiles, tile):
    return pl.pallas_call(
        functools.partial(lead_kernel, tile),
        grid=(1,),
        out_shape=jax.ShapeDtypeStruct((tile * tile // LANES, LANES), F32),
        in_specs=[pl.BlockSpec((tile, None, GROUP, LANES), lambda a: (0, 0, 0, 0))],
        out_specs=pl.BlockSpec((tile * tile // LANES, LANES), lambda a: (0, 0)),
        compiler_params=pltpu.CompilerParams(vmem_limit_bytes=VMEM_BYTES),
        cost_estimate=COST,
        name="gather_lead",
    )(grouped(block, row_tiles, col_tiles, tile))


def gather_pieces(place, lead, block, row_tiles, col_tiles, tile):
    per = tile // LANES
    size = tile * per
    top = (tile * col_tiles * per, LANES)
    whole = [size * row_tiles] + [size * (col_tiles // 2)] * 2
    return pl.pallas_call(
        functools.partial(gather_kernel, tile, col_tiles, row_tiles),
        grid=(row_tiles - 1,),
        out_shape=[jax.ShapeDtypeStruct((s, LANES), F32) for s in [size * (row_tiles - 1)] + whole],
        in_specs=[
            pl.BlockSpec(memory_space=pltpu.SMEM),
            pl.BlockSpec((size, LANES), lambda a: (0, 0)),
            pl.BlockSpec((tile, None, GROUP, LANES), lambda a: (a + 1, 0, 0, 0)),
            pl.BlockSpec(top, lambda a: (0, 0)),
        ],
        out_specs=[pl.BlockSpec((size, LANES), lambda a: (a, 0))]
        + [pl.BlockSpec((s, LANES), lambda a: (0, 0)) for s in whole],
        compiler_params=pltpu.CompilerParams(vmem_limit_bytes=VMEM_BYTES),
        cost_estimate=COST,
        name="gather_pieces",
    )(place, lead, grouped(block, row_tiles, col_tiles, tile), block)


def halves(x):
    high = x.astype(BF16)
    return high, (x - high.astype(F32)).astype(BF16)


def left_factor(x):
    high, low = halves(x)
    return jnp.concatenate([high, low, high], axis=1)


def right_factor(x, axis):
    high, low = halves(x)
    return jnp.concatenate([high, high, low], axis=axis)


def product(a, b, dims):
    return lax.dot_general(a, b, (dims, ((), ())), preferred_element_type=F32)


def weights_kernel(tile, place_ref, rows_mine, rows_other, inverse_ref, weights_ref, solved_ref, across, along):
    step = pl.program_id(0)
    row, col, core = place_ref[0], place_ref[1], place_ref[2]
    per = tile // LANES

    @pl.when(step == 0)
    def _():
        across[...] = right_factor(inverse_ref[...], 1)
        along[...] = right_factor(inverse_ref[...], 0)

    mine, other = [
        jnp.concatenate([r[pl.ds(h, tile, stride=per), :] for h in range(per)], axis=1)
        for r in (rows_mine, rows_other)
    ]
    lead = jnp.concatenate([jnp.where(core == 0, mine, other).T, jnp.where(core == 0, other, mine).T], axis=1)
    solved = product(left_factor(lead), across[...], ((1,), (1,)))
    weights_ref[...] = left_factor(product(left_factor(solved), along[...], ((1,), (0,))))

    @pl.when(col < 2)
    def _():
        mine = jnp.where(col == 0, solved[:, :tile], solved[:, tile:])
        r = lax.broadcasted_iota(jnp.int32, (tile, tile), 0)
        s = lax.broadcasted_iota(jnp.int32, (tile, tile), 1)
        top = (step == 0) & (row < 2)
        on_diag = top & (row == col)
        above = top & (row < col)
        keep = jnp.where(on_diag, s - r, jnp.where(above, 1, 0)) <= 0
        solved_ref[...] = jnp.where(keep, mine, F32(0.0))


def row_weights(place, rows_mine, rows_other, inverse, row_tiles, tile):
    depth = inverse.shape[0]
    rows_spec = pl.BlockSpec((tile * tile // LANES, LANES), lambda a: (a, 0))
    total = row_tiles * tile
    return pl.pallas_call(
        functools.partial(weights_kernel, tile),
        grid=(row_tiles,),
        out_shape=[jax.ShapeDtypeStruct((total, 3 * depth), BF16), jax.ShapeDtypeStruct((total, tile), F32)],
        in_specs=[
            pl.BlockSpec(memory_space=pltpu.SMEM),
            rows_spec,
            rows_spec,
            pl.BlockSpec((depth, depth), lambda a: (0, 0)),
        ],
        out_specs=[pl.BlockSpec((tile, 3 * depth), lambda a: (a, 0)), pl.BlockSpec((tile, tile), lambda a: (a, 0))],
        scratch_shapes=[pltpu.VMEM((depth, 3 * depth), BF16), pltpu.VMEM((3 * depth, depth), BF16)],
        compiler_params=pltpu.CompilerParams(vmem_limit_bytes=18 * 1024 * 1024),
        cost_estimate=COST,
        name="row_weights",
    )(place, rows_mine, rows_other, inverse)


def load_columns(choices, pieces, columns, tile, count):
    per = tile // LANES
    depth = 2 * tile
    for panel in range(2):
        for which, ref in enumerate(pieces):

            @pl.when(choices[panel] == which)
            def _(panel=panel, ref=ref):
                for i in range(count):
                    for h in range(per):
                        high, low = halves(ref[pl.ds(i * tile * per + h, tile, stride=per), :])
                        at = (i * per + h) * LANES
                        for copy, value in enumerate((high, high, low)):
                            row = copy * depth + panel * tile
                            columns[row : row + tile, at : at + LANES] = value


def products_kernel(tile, count, place_ref, weights_ref, piece_a, piece_b, piece_c, out_ref, columns):
    @pl.when(pl.program_id(0) == 0)
    def _():
        load_columns((place_ref[3], place_ref[4]), (piece_a, piece_b, piece_c), columns, tile, count)

    for i in range(count):
        at = i * tile
        out_ref[:, at : at + tile] = product(weights_ref[...], columns[:, at : at + tile], ((1,), (0,)))


def first_products(place, weights, pieces, row_tiles, tile):
    depth = weights.shape[1]
    piece = pl.BlockSpec(pieces[0].shape, lambda a: (0, 0))
    count = pieces[0].shape[0] * LANES // tile // tile
    return pl.pallas_call(
        functools.partial(products_kernel, tile, count),
        grid=(row_tiles,),
        out_shape=jax.ShapeDtypeStruct((row_tiles * tile, count * tile), F32),
        in_specs=[pl.BlockSpec(memory_space=pltpu.SMEM), pl.BlockSpec((tile, depth), lambda a: (a, 0))] + [piece] * 3,
        out_specs=pl.BlockSpec((tile, count * tile), lambda a: (a, 0)),
        scratch_shapes=[pltpu.VMEM((depth, count * tile), BF16)],
        compiler_params=pltpu.CompilerParams(vmem_limit_bytes=20 * 1024 * 1024),
        cost_estimate=COST,
        name="first_products",
    )(place, weights, *pieces)


def trailing_kernel(tile, group, count, place_ref, block_ref, weights_ref, ready_ref, *rest):
    solved_ref = rest[0] if group == 0 else None
    pieces = rest[1:4]
    block_out, columns = rest[-2:]
    step = pl.program_id(0)
    row, col = place_ref[0], place_ref[1]
    per = tile // LANES
    top = (step == 0) & (row < 2)
    block = block_ref.reshape(tile * GROUP, LANES)
    out = block_out.reshape(tile * GROUP, LANES)

    @pl.when(step == 0)
    def _():
        load_columns((place_ref[5], place_ref[6]), pieces, columns, tile, count)

    @pl.when(top)
    def _():
        block_out[...] = jnp.zeros_like(block_out)

    @pl.when(jnp.logical_not(top))
    def _():
        for stage in range(2):
            parity = place_ref[2] if stage == 0 else 1 - place_ref[2]
            for i in range(count):
                at = i * tile
                if stage == 0:
                    update = ready_ref[:, at : at + tile]
                else:
                    update = product(weights_ref[...], columns[:, at : at + tile], ((1,), (0,)))
                for h in range(per):
                    where = pl.ds((2 * i + parity) * per + h, tile, stride=GROUP)
                    out[where, :] = block[where, :] - update[:, h * LANES : (h + 1) * LANES]

    if group == 0:

        @pl.when(col < 2)
        def _():
            for h in range(per):
                out[pl.ds(h, tile, stride=GROUP), :] = solved_ref[:, h * LANES : (h + 1) * LANES]


def trailing(group, place, block, weights, ready, extra, pieces, row_tiles, col_tiles, tile):
    per = tile // LANES
    depth = weights.shape[1]
    count = GROUP // per // 2
    view = grouped(block, row_tiles, col_tiles, tile)
    block_spec = pl.BlockSpec((tile, None, GROUP, LANES), lambda a: (a, group, 0, 0))
    return pl.pallas_call(
        functools.partial(trailing_kernel, tile, group, count),
        grid=(row_tiles,),
        out_shape=jax.ShapeDtypeStruct(view.shape, F32),
        in_specs=[
            pl.BlockSpec(memory_space=pltpu.SMEM),
            block_spec,
            pl.BlockSpec((tile, depth), lambda a: (a, 0)),
            pl.BlockSpec((tile, count * tile), lambda a: (a, group)),
        ]
        + [pl.BlockSpec((tile, tile), lambda a: (a, 0)) if group == 0 else pl.BlockSpec(memory_space=pl.ANY)]
        + [pl.BlockSpec(pieces[0].shape, lambda a: (0, 0))] * 3,
        out_specs=block_spec,
        scratch_shapes=[pltpu.VMEM((depth, count * tile), BF16)],
        input_output_aliases={} if group == 0 else {4: 0},
        compiler_params=pltpu.CompilerParams(vmem_limit_bytes=44 * 1024 * 1024),
        cost_estimate=COST,
        name="trailing_%d" % group,
    )(place, view, weights, ready, extra, *pieces)


AXES = ("prow", "pcol")


def send(value, route):
    pairs = []
    for device in range(32):
        to = route(device // 8, device // 4 % 2, device // 2 % 2, device % 2)
        if to is not None:
            pairs.append((device, ((to[0] * 2 + to[1]) * 2 + to[2]) * 2 + to[3]))
    return lax.ppermute(value, AXES, pairs)


def far_stage(z, x, y, k):
    to = {(0, 0): 3, (2, 0): 1, (0, 1): 2}.get((z, y))
    return None if to is None else (to, x, y, k)


def near_stage(z, x, y, k):
    to = {(0, 0): 1, (2, 0): 3, (3, 0): 2, (0, 1): 1, (1, 1): 3, (3, 1): 2}.get((z, y))
    return None if to is None else (to, x, y, k)


def by_rows(stage, z, y):
    return z == 0 or (y == 1 and z == (2 if stage == 0 else 1))


def same_core(stage):
    def route(z, x, y, k):
        if by_rows(stage, z, y) or k == x:
            return (z, 1 - x, y, k)
        return (z, x, y, x)

    return route


def cross_core(stage):
    def route(z, x, y, k):
        if by_rows(stage, z, y) or k == x:
            return None
        return (z, 1 - x, y, x)

    return route


def shards(kernel_tiles):
    row_tiles, _, tile, col_tiles, _, _ = kernel_tiles.shape
    row = lax.axis_index("prow")
    col = lax.axis_index("pcol")
    z, x, y, core = row // 2, row % 2, col // 2, col % 2
    per = tile // LANES
    block = kernel_tiles.reshape(row_tiles * tile * col_tiles * per, LANES)

    first_odd = jnp.where(y == 0, (z == 1) | (z == 2), z == 3).astype(jnp.int32)
    chosen = []
    for stage in range(2):
        rowwise = (z == 0) | ((y == 1) & (z == 2 - stage))
        own = core == x
        for panel in range(2):
            by_row = jnp.where(x == panel, 0, 1)
            by_col = jnp.where(own, jnp.where(core == panel, 0, 1), jnp.where(core == panel, 1, 2))
            chosen.append(jnp.where(rowwise, by_row, by_col))
    place = jnp.stack([row, col, jnp.where(z == 0, 0, first_odd)] + chosen).astype(jnp.int32)

    lead = gather_lead(block, row_tiles, col_tiles, tile)
    middle = tile * per // 2
    over_first = send(lead, lambda z, x, y, k: (z, x, 1, k) if y == 0 else None)
    rest, to_far, even, odd = gather_pieces(y.reshape(1), lead, block, row_tiles, col_tiles, tile)
    over_first, rest, to_far = lax.optimization_barrier((over_first, rest, to_far))
    half = jnp.where(y == 0, lead[:middle], over_first[middle:])
    half = jnp.where(z == 2, send(half, lambda z, x, y, k: (2, x, y, k) if z == 0 else None), half)
    half = jnp.where(z % 2 == 1, send(half, lambda z, x, y, k: (z + 1, x, y, k) if z % 2 == 0 else None), half)
    half, to_far = lax.optimization_barrier((half, to_far))
    far = send(to_far, far_stage)
    beside = send(half, lambda z, x, y, k: (z, 1 - x, y, k))
    above = send(half, lambda z, x, y, k: (z, x, 1 - y, k))
    corner = send(half, lambda z, x, y, k: (z, 1 - x, 1 - y, k))
    corner, rest = lax.optimization_barrier((corner, rest))
    mine = jnp.concatenate([half, beside, above, corner], axis=0)
    over_rest = send(rest, lambda z, x, y, k: (z, x, 1, k) if y == 0 else None)
    other = send(mine, lambda z, x, y, k: (z, x, y, 1 - k))
    state = corner_start(jnp.stack([core, x, y]).astype(jnp.int32), mine, other)

    state, far, over_rest = lax.optimization_barrier((state, far, over_rest))
    over = jnp.concatenate([over_first, over_rest], axis=0)
    rows_mine = jnp.where(y == 0, to_far, over)
    first = jnp.where(z == 0, even, jnp.where(y == 0, jnp.where(z == 2, to_far, far), jnp.where(z == 2, far, over)))
    to_near = jnp.where(y == 0, jnp.where(z == 3, far, to_far), jnp.where(z == 0, odd, over))
    split = to_near.shape[0] // 2
    to_near = [to_near[:split], to_near[split:]]
    state, first, to_near = lax.optimization_barrier((state, first, to_near))
    near = [send(to_near[0], near_stage), send(to_near[1], near_stage)]
    first = [first, send(first, same_core(0)), send(first, cross_core(0))]
    rows_other = send(rows_mine, lambda z, x, y, k: (z, x, y, 1 - k))
    inverse = corner_end(state)

    last = []
    for part in range(2):
        held = jnp.where(z == 0, odd[part * split : (part + 1) * split], near[part])
        if part == 0:
            inverse, held = lax.optimization_barrier((inverse, held))
        last.append([held, send(held, same_core(1)), send(held, cross_core(1))])
        if part == 0:
            weights, solved = row_weights(
                jnp.stack([row, col, core]).astype(jnp.int32), rows_mine, rows_other, inverse, row_tiles, tile
            )
            weights, near[1], first = lax.optimization_barrier((weights, near[1], first))

    ready = first_products(place, weights, first, row_tiles, tile)
    result = solved
    for part in range(2):
        result = trailing(part, place, block, weights, ready, result, last[part], row_tiles, col_tiles, tile)
    return result.reshape(kernel_tiles.shape)


def from_root(value, axis, root):
    mine = lax.axis_index(axis) == root
    return lax.psum(jnp.where(mine, value, jnp.zeros_like(value)), axis)


def shards_any(kernel_tiles):
    row_tiles, _, tile, col_tiles, _, _ = kernel_tiles.shape
    row = lax.axis_index("prow")
    col = lax.axis_index("pcol")
    per = tile // LANES
    block = kernel_tiles.reshape(row_tiles * tile * col_tiles * per, LANES)
    zero = jnp.zeros((), jnp.int32)
    lead = gather_lead(block, row_tiles, col_tiles, tile)
    _, across, even, odd = gather_pieces(zero.reshape(1), lead, block, row_tiles, col_tiles, tile)
    rows = [from_root(across, "pcol", panel) for panel in range(2)]
    middle = tile * per // 2
    tile_rows = []
    for panel in range(2):
        tiles = [from_root(from_root(lead, "pcol", panel), "prow", p) for p in range(2)]
        tile_rows.append(jnp.concatenate([t[s : s + middle] for s in (0, middle) for t in tiles], axis=0))
    inverse = corner_end(corner_start(jnp.zeros((3,), jnp.int32), tile_rows[0], tile_rows[1]))
    pieces = []
    for part in (even, odd):
        panels = [from_root(part, "prow", p) for p in range(2)]
        pieces.append(panels + [panels[0]])
    place = jnp.stack([row, col, zero, zero, zero + 1, zero, zero + 1]).astype(jnp.int32)
    weights, result = row_weights(place, rows[0], rows[1], inverse, row_tiles, tile)
    split = even.shape[0] // 2
    ready = first_products(place, weights, pieces[0], row_tiles, tile)
    for part in range(2):
        last = [piece[part * split : (part + 1) * split] for piece in pieces[1]]
        result = trailing(part, place, block, weights, ready, result, last, row_tiles, col_tiles, tile)
    return result.reshape(kernel_tiles.shape)


def solution(mesh):
    in_specs = (P(None, "prow", None, None, "pcol", None),)
    out_specs = P(None, "prow", None, None, "pcol", None)
    body = shards if (mesh.shape["prow"], mesh.shape["pcol"]) == (8, 4) else shards_any
    return jax.shard_map(body, mesh=mesh, in_specs=in_specs, out_specs=out_specs, check_vma=False)
```
